32 devices in a mesh: batch: 8 (over z, y), hidden: 4 (over x, core).
Axes of the slice: x: 2, y: 2, z: 4, core: 2. Of those that a mesh axis runs over, the one named last changes fastest.
Arguments:
- layer_input: float32 [2, 768, 8192], P(None, 'hidden', 'batch'), may hold values from -6 to 6
- gain_first: float32 [768], P('hidden'), may hold values from 0.5 to 1.5
- shift_first: float32 [768], P('hidden'), may hold values from -2 to 2
- weight_in: float32 [768, 3072], P(None, 'hidden'), may hold values from -0.21875 to 0.21875
- bias_in: float32 [3072], P('hidden'), may hold values from -2 to 2
- weight_out: float32 [3072, 768], P('hidden'), may hold values from -0.109375 to 0.109375
- bias_out: float32 [768], P('hidden'), may hold values from -2 to 2
- gain_second: float32 [768], P('hidden'), may hold values from 0.5 to 1.5
- shift_second: float32 [768], P('hidden'), may hold values from -2 to 2
- cotangent: float32 [2, 768, 8192], P(None, 'hidden', 'batch'), may hold values from -6 to 6
- live_counts: int32 [8], P('batch'), may hold values from 1 to 2, as said below
Outputs:
- layer_output: float32 [2, 768, 8192], P(None, 'hidden', 'batch')
- input_grad: float32 [2, 768, 8192], P(None, 'hidden', 'batch')
- gain_first_grad: float32 [768], P('hidden')
- shift_first_grad: float32 [768], P('hidden')
- weight_in_grad: float32 [768, 3072], P(None, 'hidden')
- bias_in_grad: float32 [3072], P('hidden')
- weight_out_grad: float32 [3072, 768], P('hidden')
- bias_out_grad: float32 [768], P('hidden')
- gain_second_grad: float32 [768], P('hidden')
- shift_second_grad: float32 [768], P('hidden')
The draws below stay inside these ranges and needn't reach their ends.
Inputs may be any that keep to these rules, and one draw needn't show every extreme that they name: `live_counts`: entries are equal within each aligned block of 4 batch indices (one batch group); each group holds 1 to 2 live sequences in its first slots; some group has all 2 slots live.
All inputs are finite; a program needn't handle non-finite values.
Results may differ from the reference program's by a relative error of at most 0.008.
Values may be sent and summed in bfloat16 or wider, within the bound.
A program may use at most 128 MiB of HBM per device.

```python
import math
import jax
import jax.numpy as jnp
from jax import lax

D = 768
FF = 3072
SEQ = 4096
SPLIT = 4
SLOTS = 2
GROUPS = 2
SEQS = 4
TOKENS = 8192
N_BATCH = 8


def draw_live_counts(key, part):
    key = jax.random.fold_in(key, 11)
    groups = N_BATCH // SPLIT
    counts = jax.random.randint(key, (groups,), 1, SLOTS + 1)
    chosen = jax.random.randint(jax.random.fold_in(key, 2), (), 0, groups)
    counts = counts.at[chosen].set(SLOTS)
    return jnp.repeat(counts, SPLIT).astype(jnp.int32)


def block_scale(rng, dims, cuts, smallest, high):
    factor_of = 1.0
    for position, parts in cuts:
        heights = jax.random.uniform(jax.random.fold_in(jax.random.fold_in(rng, 6), position), (parts,), jnp.float32, smallest / len(cuts), high / len(cuts))
        factor_of = factor_of * jnp.repeat(jnp.exp(heights), dims[position] // parts).reshape((-1,) + (1,) * (len(dims) - 1 - position))
    return factor_of


def centred(stream_key, extent, scale, limit, shards=(), held_as=jnp.bfloat16):
    result = scale * jax.random.normal(stream_key, extent, jnp.float32)
    if shards:
        result = result * block_scale(stream_key, extent, shards, -0.22, 0.18)
    return jnp.clip(result, -limit, limit).astype(held_as)


def setup_inputs(seed: int = 0) -> dict:
    key_of = jax.random.split(jax.random.key(seed), 12)
    return {
        "layer_input": centred(key_of[0], (SLOTS, D, TOKENS), 1.0, 6.0, ((1, 4), (2, 8)), jnp.float32),
        "gain_first": jnp.clip(1.0 + 0.1 * jax.random.normal(key_of[1], (D,), jnp.float32), 0.5, 1.5),
        "shift_first": centred(key_of[2], (D,), 0.3, 2.0, ((0, 4),), jnp.float32),
        "weight_in": centred(key_of[3], (D, FF), D ** -0.5, 0.21875, ((1, 4),), jnp.float32),
        "bias_in": centred(key_of[4], (FF,), 0.3, 2.0, ((0, 4),), jnp.float32),
        "weight_out": centred(key_of[5], (FF, D), FF ** -0.5, 0.109375, ((0, 4),), jnp.float32),
        "bias_out": centred(key_of[6], (D,), 0.3, 2.0, ((0, 4),), jnp.float32),
        "gain_second": jnp.clip(1.0 + 0.1 * jax.random.normal(key_of[7], (D,), jnp.float32), 0.5, 1.5),
        "shift_second": centred(key_of[8], (D,), 0.3, 2.0, ((0, 4),), jnp.float32),
        "cotangent": centred(key_of[9], (SLOTS, D, TOKENS), 1.0, 6.0, ((1, 4), (2, 8)), jnp.float32),
        "live_counts": draw_live_counts(jax.random.fold_in(key_of[11], 71), 0),
    }


EPS = 1e-06

@jax.custom_vjp
def low(v):
    return lax.optimization_barrier(v.astype(jnp.bfloat16)).astype(jnp.float32)

@jax.custom_vjp
def low_back(v):
    return v

def low_keep(v):
    return (low(v), None)

def low_pass(kept, grad):
    return (grad,)

def back_keep(v):
    return (v, None)

def back_low(kept, grad):
    return (low(grad),)
low.defvjp(low_keep, low_pass)
low_back.defvjp(back_keep, back_low)

def dft_tables(count, first, rows):
    index = first + jnp.arange(rows, dtype=jnp.int32)
    column = jnp.arange(count, dtype=jnp.int32)
    phase = index[:, None] * column[None, :] % count
    angle = phase.astype(jnp.float32) * (2.0 * math.pi / count)
    factor = 1.0 / math.sqrt(count)
    return (jnp.cos(angle) * factor, jnp.sin(angle) * factor)

def product(left, right):
    return jnp.dot(left, right, precision=lax.Precision.HIGHEST, preferred_element_type=jnp.float32)

def normalize(resid, gain, shift):
    average = lax.optimization_barrier(jnp.mean(resid, -1, keepdims=True))
    variance = lax.optimization_barrier(jnp.mean(resid * resid, -1, keepdims=True)) - average * average
    return (resid - average) * lax.rsqrt(variance + EPS) * gain + shift

def forward(values, params, tables):
    gain_first, shift_first, weight_in, bias_in, weight_out, bias_out, gain_second, shift_second = params
    cos_seq, sin_seq, cos_hid, sin_hid = tables
    rounded = low(values)
    spec_cos = low(low_back(product(cos_seq, rounded)))
    spec_sin = low(low_back(product(sin_seq, rounded)))
    mixed = low_back(product(spec_cos, cos_hid) - product(spec_sin, sin_hid))
    first = normalize(values + mixed, gain_first, shift_first)
    before = low_back(product(low(first), low(weight_in))) + bias_in
    hidden = low(jax.nn.gelu(before, approximate=True))
    branch = low_back(product(hidden, low(weight_out))) + bias_out
    return normalize(first + branch, gain_second, shift_second)

def to_sequences(array):
    return array.reshape(SLOTS, D, GROUPS, SEQ).transpose(0, 2, 3, 1).reshape(SEQS, SEQ, D)

def from_sequences(array):
    return array.reshape(SLOTS, GROUPS, SEQ, D).transpose(0, 3, 1, 2).reshape(SLOTS, D, GROUPS * SEQ)

def reference(layer_input, gain_first, shift_first, weight_in, bias_in, weight_out, bias_out, gain_second, shift_second, cotangent, live_counts):
    cos_seq, sin_seq = dft_tables(SEQ, 0, SEQ)
    cos_hid, sin_hid = dft_tables(D, 0, D)
    tables = (low(cos_seq), low(sin_seq), low(cos_hid), low(sin_hid))
    params = (gain_first, shift_first, weight_in, bias_in, weight_out, bias_out, gain_second, shift_second)
    item = jnp.arange(SEQS, dtype=jnp.int32)
    slot_number = item // GROUPS
    group = item % GROUPS
    live = (slot_number < live_counts[group * SPLIT]).astype(jnp.float32)

    def step(totals, entry):
        values, grad_out, weight = entry
        output, pull = jax.vjp(lambda inner, inner_params: forward(inner, inner_params, tables), values, params)
        grad_in, param_grads = pull(grad_out * weight)
        totals = jax.tree.map(lambda left, right: left + right, totals, param_grads)
        return (totals, (output * weight, grad_in * weight))
    zeros = jax.tree.map(jnp.zeros_like, params)
    totals, (outputs, input_grads) = lax.scan(step, zeros, (to_sequences(layer_input), to_sequences(cotangent), live))
    return (from_sequences(outputs), from_sequences(input_grads), totals[0], totals[1], totals[2], totals[3], totals[4], totals[5], totals[6], totals[7])
```

```python
import functools
import math

import jax
import jax.numpy as jnp
import ml_dtypes
import numpy as np
from jax import lax
from jax.experimental import pallas as pl
from jax.experimental.pallas import tpu as pltpu
from jax.sharding import PartitionSpec as P

SPLIT = 4
HOLD = 4
EPS = 1e-06
FINE = 64
LOW = jnp.bfloat16
F32 = jnp.float32
MESH = pl.DeviceIdType.MESH
VMEM_LIMIT = 58 * 2**20


def dot(left, right):
    return jnp.dot(left, right, preferred_element_type=F32)


def dot_rows(left, right):
    return lax.dot_general(left, right, (((1,), (1,)), ((), ())), preferred_element_type=F32)


@functools.cache
def sequence_tables(length, split):
    column = np.arange(length)
    coarse = 2 * np.pi * ((FINE * np.arange(length // FINE)[:, None] * column) % length) / length
    fine = 2 * np.pi * ((np.arange(FINE)[:, None] * column) % length) / length
    factor = 1 / math.sqrt(length)
    whole = np.stack([np.cos(coarse), np.sin(coarse), factor * np.cos(fine), factor * np.sin(fine)])
    return np.ascontiguousarray(
        whole.reshape(4, FINE, split, length // split).transpose(2, 0, 1, 3).astype(np.float32)
    )


@functools.cache
def feature_tables(width, parts):
    index = np.arange(width)
    angle = 2 * np.pi * ((index[:, None] * index) % width) / width
    factor = 1 / math.sqrt(width)
    cos = (np.cos(angle) * factor).astype(np.float32).astype(ml_dtypes.bfloat16)
    sin = (np.sin(angle) * factor).astype(np.float32).astype(ml_dtypes.bfloat16)
    part = width // parts
    pad = part + 16
    forward = np.zeros((parts, parts, part, 2 * part), ml_dtypes.bfloat16)
    backward = np.zeros((parts, pad, width), ml_dtypes.bfloat16)
    order = np.zeros((parts, part, pad), ml_dtypes.bfloat16)
    for h in range(parts):
        own = slice(h * part, (h + 1) * part)
        forward[h, :, :, :part] = cos[:, own].reshape(parts, part, part)
        forward[h, :, :, part:] = -sin[:, own].reshape(parts, part, part)
        first = (h // 2) * part
        backward[h, : part + 1] = (cos, sin)[h % 2][first : first + part + 1]
        for i in range(part):
            order[h, i, i if h in (0, 3) else part - i] = 1
    return forward, backward, order


class Place:
    def __init__(self):
        h = lax.axis_index("hidden")
        b = lax.axis_index("batch")
        self.h, self.b = h, b
        self.c = lax.rem(h, 2)
        self.x = lax.div(h, 2)
        self.hc = h + 1 - 2 * self.c
        self.hx = lax.rem(h + 2, 4)
        self.hd = lax.rem(self.hc + 2, 4)
        self.p = lax.rem(b, 4)
        y = lax.rem(b, 2)
        z = lax.div(self.p, 2)
        self.py = self.p + 1 - 2 * y
        self.pz = lax.rem(self.p + 2, 4)
        self.core = {"hidden": self.hc}
        self.side = {"hidden": self.hx}
        self.cross = {"hidden": self.hd}
        self.ydev = {"batch": b + 1 - 2 * y}
        self.zdev = {"batch": b + 2 - 4 * z}


class Links:
    def __init__(self, send, recv):
        self.send, self.recv, self.used, self.open = send, recv, 0, []

    def copy(self, src, dst, device):
        i = self.used
        self.used += 1
        made = pltpu.make_async_remote_copy(
            src_ref=src,
            dst_ref=dst,
            send_sem=self.send.at[i],
            recv_sem=self.recv.at[i],
            device_id=device,
            device_id_type=MESH,
        )
        made.start()
        self.open.append(made)
        return made

    def close(self):
        for made in self.open:
            made.wait_send()


def greet(devices):
    barrier = pltpu.get_barrier_semaphore()
    for device in devices:
        pl.semaphore_signal(barrier, inc=1, device_id=device, device_id_type=MESH)
    pl.semaphore_wait(barrier, len(devices))


class GatherHidden:
    def __init__(self, me, links, full):
        self.me, self.links, self.full = me, links, full

    def start_core(self):
        own = self.full.at[self.me.h]
        self.by_core = self.links.copy(own, own, self.me.core)

    def start_side(self):
        own = self.full.at[self.me.h]
        self.by_side = self.links.copy(own, own, self.me.side)

    def forward(self):
        self.by_side.wait_recv()
        far = self.full.at[self.me.hx]
        self.by_far = self.links.copy(far, far, self.me.core)


class GatherBatch:
    def __init__(self, me, links, full, cut):
        self.me, self.links, self.full, self.cut = me, links, full, cut

    def start(self):
        own = self.full.at[self.me.p]
        self.by_y = self.links.copy(own, own, self.me.ydev)
        self.by_z = self.links.copy(own, own, self.me.zdev)

    def forward(self):
        rows = self.full.shape[1]
        self.by_y.wait_recv()
        part = self.full.at[self.me.py, pl.ds(0, self.cut)]
        self.on_z = self.links.copy(part, part, self.me.zdev)
        self.by_z.wait_recv()
        part = self.full.at[self.me.pz, pl.ds(self.cut, rows - self.cut)]
        self.on_y = self.links.copy(part, part, self.me.ydev)

    def finish(self):
        self.on_z.wait_recv()
        self.on_y.wait_recv()


class Scatter:
    def __init__(self, me, links, sc, rc, sx, rx, acc, parts):
        self.me, self.links, self.parts = me, links, parts
        self.sc, self.rc, self.sx, self.rx, self.acc = sc, rc, sx, rx, acc

    def blocks(self):
        x, c = self.me.x, self.me.c
        far, near = 2 * (1 - x), 2 * x
        return far + 1 - c, far + c, near + 1 - c, near + c

    def run(self, block):
        for k, t in enumerate(self.blocks()):
            far, first = k < 2, k % 2 == 0
            n = 0 if far else 1

            def sink(i, value):
                if first:
                    self.sc[n, i] = value.astype(LOW)
                    return
                if i == 0:
                    self.by_core.wait_recv()
                value = value + self.rc[n, i].astype(F32)
                if far:
                    self.sx[i] = value.astype(LOW)
                else:
                    self.acc[i] = value

            block(t, sink)
            if first:
                self.by_core = self.links.copy(self.sc.at[n], self.rc.at[n], self.me.core)
            elif far:
                self.by_side = self.links.copy(self.sx, self.rx, self.me.side)

    def wait(self):
        self.by_side.wait_recv()

    def value(self, i):
        return self.acc[i] + self.rx[i].astype(F32)


def columns(t, size):
    return pl.ds(pl.multiple_of(t * size, size), size)


def mix_kernel(
    x_ref, cot_ref, live_ref, small_ref, ht_ref, r1_ref, ctok_ref,
    xg, tc, ts, cs, ct, ab, sc, rc, sx, rx, acc, send, recv,
):
    me = Place()
    slots, rows, piece = x_ref.shape
    tokens = piece // HOLD
    greet([me.core, me.side, me.cross, me.ydev, me.zdev])
    links = Links(send, recv)
    gathers = []
    for s in range(slots):
        xg[s, me.p] = x_ref[s].astype(LOW)
        gathers.append(GatherBatch(me, links, xg.at[s], rows // 2))
        if s == 0:
            gathers[0].start()
    moved = []
    for s in range(slots):
        for t in range(HOLD):
            cs[s, t] = (cot_ref[s, :, t * tokens : (t + 1) * tokens] * live_ref[s]).astype(LOW)
        ct[s, me.h] = cs[s, me.h]
        for to, device in ((me.hc, me.core), (me.hx, me.side), (me.hd, me.cross)):
            moved.append(links.copy(cs.at[s, to], ct.at[s, me.h], device))

    def make_rows(i, carry):
        big_cos, big_sin = small_ref[0, pl.ds(i, 1), :], small_ref[1, pl.ds(i, 1), :]
        at = pl.ds(pl.multiple_of(i * FINE, FINE), FINE)
        for n in range(piece // 256):
            cut = slice(n * 256, (n + 1) * 256)
            fine_cos, fine_sin = small_ref[2, :, cut], small_ref[3, :, cut]
            tc[at, cut] = (big_cos[:, cut] * fine_cos - big_sin[:, cut] * fine_sin).astype(LOW)
            ts[at, cut] = (big_sin[:, cut] * fine_cos + big_cos[:, cut] * fine_sin).astype(LOW)
        return carry

    lax.fori_loop(0, FINE, make_rows, 0)
    sums = [Scatter(me, links, sc.at[s], rc.at[s], sx.at[s], rx.at[s], acc.at[s], HOLD) for s in range(slots)]
    gathers[0].forward()
    for s in range(slots):
        gathers[s].finish()
        if s + 1 < slots:
            gathers[s + 1].start()

        def block(t, sink, s=s):
            at = columns(t, tokens)
            for part, table in ((0, tc), (1, ts)):
                total = dot(xg[s, 0], table[0:piece, at])
                for q in range(1, SPLIT):
                    total += dot(xg[s, q], table[q * piece : (q + 1) * piece, at])
                ab[part * rows : (part + 1) * rows, :] = total.astype(LOW)
            for i in range(HOLD):
                own = jnp.where(me.h == i, 1.0, 0.0).astype(F32)
                sink(i, dot(ht_ref[i], ab[...]) + own * x_ref[s, :, at])

        sums[s].run(block)
        if s + 1 < slots:
            gathers[s + 1].forward()
    for s in range(slots):
        sums[s].wait()
        for i in range(HOLD):
            r1_ref[s, i] = sums[s].value(i)
    for made in moved:
        made.wait_recv()
    ctok_ref[...] = ct[...]
    links.close()


ROOT = math.sqrt(2 / math.pi)
CUBE = 0.044715


def gelu_both(v):
    square = v * v
    t = jnp.tanh(v * (ROOT + ROOT * CUBE * square))
    half = 0.5 + 0.5 * t
    slope = half + (0.5 * v) * (1 - t * t) * (ROOT + 3 * ROOT * CUBE * square)
    return v * half, slope


def feed_kernel(
    r1_ref, ctok_ref, w1t_ref, w2t_ref, w1_ref, w2_ref, bin_ref, g1_ref, s1_ref, bo_ref, g2_ref, s2_ref,
    lo_ref, gm_ref, wg1_ref, wg2_ref, sg_ref,
    yf, hf, df, zf, y1, u1, gr2, inv1, lanes, sc, rc, sx, rx, acc, send, recv,
):
    me = Place()
    slots, parts, rows, tokens = r1_ref.shape
    width = parts * rows
    units = w1_ref.shape[1]
    steps = units // 256
    greet([me.core, me.side])
    links = Links(send, recv)

    def lane_sum(k, i, s, value):
        folded = value[:, :128] + value[:, 128:]
        lanes[k, i] = folded if s == 0 else lanes[k, i] + folded

    def up(value):
        return jnp.sum(value, 0, keepdims=True)

    def norm_first(s):
        total, squares = 0.0, 0.0
        for i in range(parts):
            v = r1_ref[s, i]
            total, squares = total + up(v), squares + up(v * v)
        mean = total / width
        inverse = lax.rsqrt(squares / width - mean * mean + EPS)
        inv1[s] = inverse
        for i in range(parts):
            u = (r1_ref[s, i] - mean) * inverse
            u1[s, i] = u
            y = u * g1_ref[i] + s1_ref[i]
            y1[s, i] = y
            yf[s, me.h, i * rows : (i + 1) * rows, :] = y.astype(LOW)

    def forward_in(s, t):
        for r in range(steps):
            at = slice(r * 256, (r + 1) * 256)
            h, slope = gelu_both(dot(w1t_ref[at, :], yf[s, t]) + bin_ref[at, :])
            hf[s, t, at, :] = h.astype(LOW)
            df[s, t, at, :] = slope.astype(LOW)

    def forward_out(s, t, sink):
        for i in range(parts):
            sink(i, dot(w2t_ref[i * rows : (i + 1) * rows, :], hf[s, t]))

    def norm_second(s, summed):
        total, squares = 0.0, 0.0
        for i in range(parts):
            v = y1[s, i] + summed.value(i) + bo_ref[i]
            summed.acc[i] = v
            total, squares = total + up(v), squares + up(v * v)
        mean = total / width
        inverse = lax.rsqrt(squares / width - mean * mean + EPS)
        total, cross = 0.0, 0.0
        for i in range(parts):
            u = (summed.acc[i] - mean) * inverse
            summed.acc[i] = u
            lo_ref[s, i] = (u * g2_ref[i] + s2_ref[i]).astype(LOW)
            g = ctok_ref[s, i].astype(F32)
            lane_sum(0, i, s, g * u)
            lane_sum(1, i, s, g)
            q = g * g2_ref[i]
            total, cross = total + up(q), cross + up(q * u)
        total, cross = total / width, cross / width
        for i in range(parts):
            q = ctok_ref[s, i].astype(F32) * g2_ref[i]
            grad = inverse * (q - total - summed.acc[i] * cross)
            gr2[s, i] = grad
            lane_sum(2, i, s, grad)
            zf[s, me.h, i * rows : (i + 1) * rows, :] = grad.astype(LOW)

    def backward_in(s, t, fresh):
        for r in range(steps):
            at = slice(r * 256, (r + 1) * 256)
            gp = dot(w2_ref[at, :], zf[s, t]) * df[s, t, at, :].astype(F32)
            folded = gp[:, :128] + gp[:, 128:]
            for n in range(256 // 64):
                cut = slice(n * 64, (n + 1) * 64)
                place = r * 256 + n * 64
                i, o = place // rows, place % rows
                lanes[5, i, o : o + 64] = folded[cut] if fresh else lanes[5, i, o : o + 64] + folded[cut]
            df[s, t, at, :] = gp.astype(LOW)

    def backward_out(s, t, sink):
        for i in range(parts):
            sink(i, dot(w1_ref[i * rows : (i + 1) * rows, :], df[s, t]))

    def weight_grads(s):
        def one(r, carry):
            at = columns(r, 256)
            for n in range(units // 256):
                cut = slice(n * 256, (n + 1) * 256)
                first, second = 0.0, 0.0
                for t in range(HOLD):
                    first = first + dot_rows(yf[s, t, at, :], df[s, t, cut, :])
                    second = second + dot_rows(hf[s, t, at, :], zf[s, t, cut, :])
                wg1_ref[at, cut] = first if s == 0 else wg1_ref[at, cut] + first
                wg2_ref[at, cut] = second if s == 0 else wg2_ref[at, cut] + second
            return carry

        lax.fori_loop(0, steps, one, 0)

    def norm_first_back(s, summed):
        total, cross = 0.0, 0.0
        for i in range(parts):
            grad = gr2[s, i] + summed.value(i)
            summed.acc[i] = grad
            u = u1[s, i]
            lane_sum(3, i, s, grad * u)
            lane_sum(4, i, s, grad)
            q = grad * g1_ref[i]
            total, cross = total + up(q), cross + up(q * u)
        total, cross = total / width, cross / width
        for i in range(parts):
            q = summed.acc[i] * g1_ref[i]
            gm_ref[s, i] = (inv1[s] * (q - total - u1[s, i] * cross)).astype(LOW)

    def scatter(s, way):
        n = 2 * way + s
        return Scatter(me, links, sc.at[n], rc.at[n], sx.at[n], rx.at[n], acc.at[n], parts)

    gathers = [GatherHidden(me, links, yf.at[s]) for s in range(slots)]
    sums = [scatter(s, 0) for s in range(slots)]
    for s in range(slots):
        norm_first(s)
        gathers[s].start_core()
        if s == 0:
            gathers[0].start_side()
    for s in range(slots):
        forward_in(s, me.h)
        gathers[s].by_core.wait_recv()
        forward_in(s, me.hc)
        gathers[s].forward()
        if s + 1 < slots:
            gathers[s + 1].start_side()
        forward_in(s, me.hx)
        gathers[s].by_far.wait_recv()
        forward_in(s, me.hd)
        sums[s].run(functools.partial(forward_out, s))
    gathers = [GatherHidden(me, links, zf.at[s]) for s in range(slots)]
    for s in range(slots):
        sums[s].wait()
        norm_second(s, sums[s])
        gathers[s].start_core()
        gathers[s].start_side()
    sums = [scatter(s, 1) for s in range(slots)]
    for s in range(slots):
        backward_in(s, me.h, s == 0)
        gathers[s].by_core.wait_recv()
        backward_in(s, me.hc, False)
        gathers[s].forward()
        backward_in(s, me.hx, False)
        gathers[s].by_far.wait_recv()
        backward_in(s, me.hd, False)
        sums[s].run(functools.partial(backward_out, s))
        weight_grads(s)
    for s in range(slots):
        sums[s].wait()
        norm_first_back(s, sums[s])
    lane = lax.broadcasted_iota(jnp.int32, (rows, 128), 1)
    for i in range(parts):
        packed = jnp.zeros((rows, 128), F32)
        for k in range(6):
            packed = jnp.where(lane == k, jnp.sum(lanes[k, i], 1, keepdims=True), packed)
        sg_ref[i] = packed
    links.close()


def back_kernel(
    gm_ref, lo_ref, live_ref, small_ref, gt_ref, order_ref, out_ref, grad_ref,
    gf, ug, og, tab, wv, ws, wr, rs, rr, send, recv,
):
    me = Place()
    slots, parts, rows, tokens = gm_ref.shape
    piece = parts * tokens
    width = parts * rows
    pad = gt_ref.shape[0]
    greet([me.core, me.side, me.cross, me.ydev, me.zdev])
    links = Links(send, recv)
    gathers = []
    for s in range(slots):
        gf[s, me.h] = gm_ref[s]
        gathers.append(GatherHidden(me, links, gf.at[s]))
        gathers[s].start_core()
        if s == 0:
            gathers[s].start_side()
    is_cos = me.c == 0

    def make_rows(i, carry):
        big_cos, big_sin = small_ref[0, pl.ds(i, 1), :], small_ref[1, pl.ds(i, 1), :]
        by_cos = jnp.where(is_cos, big_cos, big_sin)
        by_sin = jnp.where(is_cos, -big_sin, big_cos)
        at = pl.ds(pl.multiple_of(i * FINE, FINE), FINE)
        for n in range(piece // 256):
            cut = slice(n * 256, (n + 1) * 256)
            tab[at, cut] = (by_cos[:, cut] * small_ref[2, :, cut] + by_sin[:, cut] * small_ref[3, :, cut]).astype(LOW)
        return carry

    lax.fori_loop(0, FINE, make_rows, 0)
    spreads = [GatherBatch(me, links, ug.at[s], (pad // 32) * 16) for s in range(slots)]

    def features(s, t):
        whole = gf[s, t].reshape(width, tokens)
        ug[s, me.p, :, columns(t, tokens)] = dot(gt_ref[...], whole).astype(LOW)

    for s in range(slots):
        features(s, me.h)
        gathers[s].by_core.wait_recv()
        features(s, me.hc)
        gathers[s].forward()
        if s + 1 < slots:
            gathers[s + 1].start_side()
        features(s, me.hx)
        gathers[s].by_far.wait_recv()
        features(s, me.hd)
        if s > 0:
            spreads[s - 1].forward()
        spreads[s].start()
    moved = []
    for s in range(slots):
        og[s, me.h] = lo_ref[s, me.h]
        for to, device in ((me.hc, me.core), (me.hx, me.side), (me.hd, me.cross)):
            moved.append(links.copy(lo_ref.at[s, to], og.at[s, me.h], device))
    sign = jnp.where((me.h == 0) | (me.h == 3), -1.0, 1.0).astype(F32)
    mine = jnp.where(is_cos, 1.0, sign)
    theirs = jnp.where(is_cos, sign, 1.0)
    for s in range(slots):
        if s == slots - 1:
            spreads[s].forward()
        spreads[s].finish()
        for t in range(parts):
            at = slice(t * tokens, (t + 1) * tokens)
            total = dot(ug[s, 0], tab[0:piece, at])
            for q in range(1, SPLIT):
                total += dot(ug[s, q], tab[q * piece : (q + 1) * piece, at])
            wv[:, at] = total
            ws[s, :, at] = total.astype(LOW)
        swap = links.copy(ws.at[s], wr.at[s], me.core)
        swap.wait_recv()
        for t in range(parts):
            at = slice(t * tokens, (t + 1) * tokens)
            pair = (mine * wv[:, at] + theirs * wr[s, :, at].astype(F32)).astype(LOW)
            rs[s, :, at] = dot(order_ref[...], pair).astype(LOW)

        @pl.when(is_cos)
        def _(s=s):
            rr[s] = rs[s]

        @pl.when(jnp.logical_not(is_cos))
        def _(s=s):
            made = links.copy(rs.at[s], rr.at[s], me.side)
            links.open.pop()
            made.wait()

        for t in range(parts):
            at = slice(t * tokens, (t + 1) * tokens)
            grad_ref[s, :, at] = rr[s, :, at].astype(F32) + gf[s, t, me.h].astype(F32)
    for made in moved:
        made.wait_recv()
    for s in range(slots):
        for t in range(parts):
            out_ref[s, :, t * tokens : (t + 1) * tokens] = og[s, t].astype(F32) * live_ref[s]
    links.close()


def call(kernel, name, number, outs, scratch, smem, flops, *operands):
    specs = [
        pl.BlockSpec(memory_space=pltpu.SMEM if i in smem else pltpu.VMEM) for i in range(len(operands))
    ]
    return pl.pallas_call(
        kernel,
        name=name,
        out_shape=[jax.ShapeDtypeStruct(shape, kind) for shape, kind in outs],
        in_specs=specs,
        out_specs=[pl.BlockSpec(memory_space=pltpu.VMEM)] * len(outs),
        scratch_shapes=[pltpu.VMEM(shape, kind) for shape, kind in scratch]
        + [pltpu.SemaphoreType.DMA((64,)), pltpu.SemaphoreType.DMA((64,))],
        cost_estimate=pl.CostEstimate(flops=flops, bytes_accessed=16 * 2**20, transcendentals=0),
        compiler_params=pltpu.CompilerParams(
            collective_id=number, has_side_effects=True, vmem_limit_bytes=VMEM_LIMIT
        ),
    )(*operands)


def local(
    layer_input,
    gain_first,
    shift_first,
    weight_in,
    bias_in,
    weight_out,
    bias_out,
    gain_second,
    shift_second,
    cotangent,
    live_counts,
):
    slots, rows, piece = layer_input.shape
    width = rows * HOLD
    tokens = piece // HOLD
    units = weight_in.shape[1]
    length = piece * SPLIT
    pad = rows + 16
    hidden = lax.axis_index("hidden")
    position = lax.axis_index("batch") % SPLIT
    live = (jnp.arange(slots) < live_counts[0]).astype(F32)

    def pick(table, index):
        return lax.dynamic_index_in_dim(jnp.asarray(table), index, 0, keepdims=False)

    small = pick(sequence_tables(length, SPLIT), position)
    forward, backward, order = feature_tables(width, HOLD)
    forward, backward, order = pick(forward, hidden), pick(backward, hidden), pick(order, hidden)
    shard = (slots, HOLD, rows, tokens)
    whole = (slots, HOLD, width, tokens)
    r1, ctok = call(
        mix_kernel, "mix", 1, [(shard, F32), (shard, LOW)],
        [
            ((slots, SPLIT, rows, piece), LOW), ((length, piece), LOW), ((length, piece), LOW),
            (shard, LOW), (shard, LOW), ((2 * rows, tokens), LOW),
            ((slots, 2) + shard[1:], LOW), ((slots, 2) + shard[1:], LOW), (shard, LOW), (shard, LOW), (shard, F32),
        ],
        (2,), 4 * 10**9, layer_input, cotangent, live, small, forward,
    )

    w1, w2 = weight_in.astype(LOW), weight_out.astype(LOW)

    norms = jnp.stack([gain_first, shift_first, bias_out, gain_second, shift_second])
    norms = lax.all_gather(norms, "hidden", axis=0).transpose(1, 0, 2).reshape(5, HOLD, rows, 1)
    lo, gm, wg1, wg2, sg = call(
        feed_kernel, "feed", 2,
        [(shard, LOW), (shard, LOW), ((width, units), F32), ((units, width), F32), ((HOLD, rows, 128), F32)],
        [
            (whole, LOW), ((slots, HOLD, units, tokens), LOW), ((slots, HOLD, units, tokens), LOW), (whole, LOW),
            (shard, F32), (shard, F32), (shard, F32), ((slots, 1, tokens), F32), ((6, HOLD, rows, 128), F32),
            ((2 * slots, 2) + shard[1:], LOW), ((2 * slots, 2) + shard[1:], LOW),
            ((2 * slots,) + shard[1:], LOW), ((2 * slots,) + shard[1:], LOW), ((2 * slots,) + shard[1:], F32),
        ],
        (), 12 * 10**9, r1, ctok, w1.T, w2.T, w1, w2, bias_in.reshape(units, 1), *norms,
    )
    heavy = lax.psum(jnp.stack([wg1, wg2]).astype(LOW), "batch").astype(F32)
    sg = sg.reshape(width, 128)
    light = lax.psum_scatter(sg[:, :5].T.reshape(5, HOLD, rows), "hidden", scatter_dimension=1, tiled=False)
    light, bias_in_grad = lax.psum((light, sg[:, 5]), "batch")
    outputs, in_grads = call(
        back_kernel, "back", 3, [(layer_input.shape, F32), (layer_input.shape, F32)],
        [
            ((slots, HOLD) + shard[1:], LOW), ((slots, SPLIT, pad, piece), LOW), (shard, LOW), ((length, piece), LOW),
            ((pad, piece), F32), ((slots, pad, piece), LOW), ((slots, pad, piece), LOW),
            ((slots, rows, piece), LOW), ((slots, rows, piece), LOW),
        ],
        (2,), 4 * 10**9, gm, lo, live, small, backward, order,
    )
    return (
        outputs, in_grads, light[3], light[4], heavy[0], bias_in_grad, heavy[1], light[2], light[0], light[1],
    )


def solution(mesh):
    return jax.shard_map(
        local,
        mesh=mesh,
        in_specs=(
            P(None, "hidden", "batch"),
            P("hidden"),
            P("hidden"),
            P(None, "hidden"),
            P("hidden"),
            P("hidden", None),
            P("hidden"),
            P("hidden"),
            P("hidden"),
            P(None, "hidden", "batch"),
            P("batch"),
        ),
        out_specs=(
            P(None, "hidden", "batch"),
            P(None, "hidden", "batch"),
            P("hidden"),
            P("hidden"),
            P(None, "hidden"),
            P("hidden"),
            P("hidden", None),
            P("hidden"),
            P("hidden"),
            P("hidden"),
        ),
        check_vma=False,
    )
```

```python
import functools
import math

import jax
import jax.numpy as jnp
import ml_dtypes
import numpy as np
from jax import lax
from jax.experimental import pallas as pl
from jax.experimental.pallas import tpu as pltpu
from jax.sharding import PartitionSpec as P

SPLIT = 4
HOLD = 4
EPS = 1e-06
FINE = 64
LOW = jnp.bfloat16
F32 = jnp.float32
MESH = pl.DeviceIdType.MESH
VMEM_LIMIT = 63 * 2**20


def dot(left, right):
    return jnp.dot(left, right, preferred_element_type=F32)


def dot_rows(left, right):
    return lax.dot_general(left, right, (((1,), (1,)), ((), ())), preferred_element_type=F32)


@functools.cache
def sequence_tables(length, split):
    column = np.arange(length)
    coarse = 2 * np.pi * ((FINE * np.arange(length // FINE)[:, None] * column) % length) / length
    fine = 2 * np.pi * ((np.arange(FINE)[:, None] * column) % length) / length
    factor = 1 / math.sqrt(length)
    whole = np.stack([np.cos(coarse), np.sin(coarse), factor * np.cos(fine), factor * np.sin(fine)])
    return np.ascontiguousarray(
        whole.reshape(4, FINE, split, length // split).transpose(2, 0, 1, 3).astype(np.float32)
    )


@functools.cache
def feature_tables(width, parts):
    index = np.arange(width)
    angle = 2 * np.pi * ((index[:, None] * index) % width) / width
    factor = 1 / math.sqrt(width)
    cos = (np.cos(angle) * factor).astype(np.float32).astype(ml_dtypes.bfloat16)
    sin = (np.sin(angle) * factor).astype(np.float32).astype(ml_dtypes.bfloat16)
    part = width // parts
    pad = part + 16
    forward = np.zeros((parts, parts, part, 2 * part), ml_dtypes.bfloat16)
    backward = np.zeros((parts, pad, width), ml_dtypes.bfloat16)
    order = np.zeros((parts, part, pad), ml_dtypes.bfloat16)
    for h in range(parts):
        chip = slice((h // 2) * 2 * part, (h // 2 + 1) * 2 * part)
        forward[h] = (cos if h % 2 == 0 else -sin)[:, chip].reshape(parts, part, 2 * part)
        first = (h // 2) * part
        backward[h, : part + 1] = (cos, sin)[h % 2][first : first + part + 1]
        for i in range(part):
            order[h, i, i if h in (0, 3) else part - i] = 1
    return forward, backward, order


class Place:
    def __init__(self, bits):
        h = lax.axis_index("hidden")
        b = lax.axis_index("batch")
        self.h, self.b = h, b
        self.c = lax.rem(h, 2)
        self.x = lax.div(h, 2)
        self.hc = h + 1 - 2 * self.c
        self.hx = lax.rem(h + 2, 4)
        self.hd = lax.rem(self.hc + 2, 4)
        self.p = lax.rem(b, 4)
        self.bit = [lax.rem(lax.div(b, 2**k), 2) for k in range(bits)]
        self.py = self.p + 1 - 2 * self.bit[0]
        self.pz = lax.rem(self.p + 2, 4)
        self.pd = lax.rem(self.py + 2, 4)
        self.core = {"hidden": self.hc}
        self.side = {"hidden": self.hx}
        self.cross = {"hidden": self.hd}
        self.flip = [{"batch": b + 2**k - 2 ** (k + 1) * self.bit[k]} for k in range(bits)]
        self.ydev, self.zdev = self.flip[:2]


class Links:
    def __init__(self, send, recv, near):
        self.send, self.recv, self.near = send, recv, near
        self.used, self.fetched, self.open = 0, 0, []

    def copy(self, src, dst, device):
        i = self.used
        self.used += 1
        made = pltpu.make_async_remote_copy(
            src_ref=src,
            dst_ref=dst,
            send_sem=self.send.at[i],
            recv_sem=self.recv.at[i],
            device_id=device,
            device_id_type=MESH,
        )
        made.start()
        self.open.append(made)
        return made

    def settle(self, some):
        for made in some:
            made.wait_send()
            self.drop(made)

    def drop(self, made):
        self.open = [other for other in self.open if other is not made]

    def fetch(self, src, dst):
        made = pltpu.make_async_copy(src, dst, self.near.at[self.fetched])
        self.fetched += 1
        made.start()
        return made


def greet(devices):
    barrier = pltpu.get_barrier_semaphore()
    for device in devices:
        pl.semaphore_signal(barrier, inc=1, device_id=device, device_id_type=MESH)
    pl.semaphore_wait(barrier, len(devices))


class GatherHidden:
    def __init__(self, me, links, view):
        self.me, self.links, self.view = me, links, view

    def start(self):
        own = self.view(self.me.h)
        self.by_side = self.links.copy(own, own, self.me.side)
        self.by_core = self.links.copy(own, own, self.me.core)

    def forward(self):
        self.by_side.wait_recv()
        far = self.view(self.me.hx)
        self.by_far = self.links.copy(far, far, self.me.core)


class GatherBatch:
    def __init__(self, me, links, view):
        self.me, self.links, self.view = me, links, view

    def start(self):
        own = self.view(self.me.p)
        self.by_y = self.links.copy(own, own, self.me.ydev)
        self.by_z = self.links.copy(own, own, self.me.zdev)

    def forward(self):
        self.by_y.wait_recv()
        part = self.view(self.me.py, 0)
        self.on_z = self.links.copy(part, part, self.me.zdev)
        self.by_z.wait_recv()
        part = self.view(self.me.pz, 1)
        self.on_y = self.links.copy(part, part, self.me.ydev)

    def finish(self):
        self.on_z.wait_recv()
        self.on_y.wait_recv()


class Scatter:
    def __init__(self, me, links, rows, sc, rc, sx, rx, acc):
        self.me, self.links, self.rows, self.sent = me, links, rows, []
        self.sc, self.rc, self.sx, self.rx, self.acc = sc, rc, sx, rx, acc

    def run(self, block):
        x, c = self.me.x, self.me.c
        far, near, cut = 2 * (1 - x), 2 * x, pl.ds(0, self.rows)
        self.links.settle(self.sent)
        self.sent = []
        for k, t in enumerate((far + 1 - c, far + c, near + 1 - c, near + c)):
            n, first = k // 2, k % 2 == 0

            def sink(i, value):
                if first:
                    self.sc[n, i, cut] = value.astype(LOW)
                    return
                if i == 0:
                    self.by_core.wait_recv()
                value = value + self.rc[n, i, cut].astype(F32)
                if n == 0:
                    self.sx[i] = value.astype(LOW)
                else:
                    self.acc[i, cut] = value

            block(t, sink)
            if first:
                self.by_core = self.links.copy(self.sc.at[n, :, cut], self.rc.at[n, :, cut], self.me.core)
                self.sent.append(self.by_core)
            elif n == 0:
                self.by_side = self.links.copy(self.sx, self.rx, self.me.side)
                self.sent.append(self.by_side)

    def wait(self):
        self.by_side.wait_recv()

    def value(self, i):
        return self.acc[i, 0 : self.rows] + self.rx[i].astype(F32)


class Reduce:
    def __init__(self, me, links, total, low, landing, whole):
        self.me, self.links = me, links
        self.total, self.low, self.landing, self.whole = total, low, landing, whole
        self.blocks = total.shape[1] // whole.shape[2]
        bits, size, self.halvings = len(me.bit), total.shape[0], 0
        while self.halvings < bits and (size >> (self.halvings + 1)) % 16 == 0:
            self.halvings += 1
        self.plan = [(self.halve, k) for k in range(self.halvings)]
        self.plan += [(self.double, k) for k in range(self.halvings, bits)]
        self.plan += [(self.gather, k) for k in reversed(range(self.halvings))]
        self.at, self.used, self.lows, self.after = 0, 0, [0], None

    def span(self, first, size):
        return pl.ds(pl.multiple_of(first, 16), size)

    def step(self):
        if self.after is not None:
            self.after()
            self.after = None
        if self.at == len(self.plan):
            return False
        kind, k = self.plan[self.at]
        self.at += 1
        kind(k)
        return True

    def land(self, size):
        self.used += size
        return pl.ds(self.used - size, size)

    def halve(self, k):
        half = self.total.shape[0] >> (k + 1)
        u = self.me.bit[k]
        keep = self.lows[-1] + u * half
        give = self.span(self.lows[-1] + (1 - u) * half, half)
        self.lows.append(keep)
        place = self.land(half)
        self.low[give, :] = self.total[give, :].astype(LOW)
        made = self.links.copy(self.low.at[give], self.landing.at[place], self.me.flip[k])

        def after():
            made.wait_recv()
            self.links.settle([made])
            mine = self.span(keep, half)
            self.total[mine, :] += self.landing[place, :].astype(F32)
            if k + 1 == self.halvings:
                self.low[mine, :] = self.total[mine, :].astype(LOW)

        self.after = after

    def double(self, k):
        size = self.total.shape[0] >> self.halvings
        mine = self.span(self.lows[-1], size)
        place = self.land(size)
        made = self.links.copy(self.low.at[mine], self.landing.at[place], self.me.flip[k])

        def after():
            made.wait_recv()
            self.links.settle([made])
            self.low[mine, :] = (self.low[mine, :].astype(F32) + self.landing[place, :].astype(F32)).astype(LOW)

        self.after = after

    def gather(self, k):
        size = self.total.shape[0] >> (k + 1)
        mine = self.span(self.lows[k + 1], size)
        blocks, wide = self.blocks, self.whole.shape[2]
        if k + 1 == self.halvings:
            for n in range(blocks):
                self.whole[n, mine, :] = self.low[mine, n * wide : (n + 1) * wide]
        part = self.whole.at[pl.ds(0, blocks), mine]
        self.after = self.links.copy(part, part, self.me.flip[k]).wait_recv


def landing_rows(size, bits):
    halvings, used = 0, 0
    while halvings < bits and (size >> (halvings + 1)) % 16 == 0:
        halvings += 1
        used += size >> halvings
    return used + (bits - halvings) * (size >> halvings)


def columns(t, size):
    return pl.ds(pl.multiple_of(t * size, size), size)


ROOT = math.sqrt(2 / math.pi)
CUBE = 0.044715


def gelu_both(v):
    square = v * v
    t = jnp.tanh(v * (ROOT + ROOT * CUBE * square))
    half = 0.5 + 0.5 * t
    slope = half + (0.5 * v) * (1 - t * t) * (ROOT + 3 * ROOT * CUBE * square)
    return v * half, slope


def up(value):
    return jnp.sum(value, 0, keepdims=True)


def layer_kernel(
    bits,
    x_hbm, cot_hbm, w1_hbm, w2_hbm, small_hbm, ht_hbm, gt_hbm, order_hbm, vec_ref, live_ref,
    out_hbm, grad_hbm, wg1_hbm, wg2_hbm, light_ref,
    tab, small, ht, gt, order, xg, cs, ct, ab, sc, rc, sx, rx, acc, yf, hf, df, zf, u1, gr2, inv1, lanes,
    w1, w1t, w2, w2t, wg1, wg2, low, landing, ug, pn, lsend, lrecv, ltot, lnext, send, recv, near,
):
    slots, _, piece = x_hbm.shape
    parts, rows, tokens = cs.shape[1:]
    width = parts * rows
    units = w1.shape[1]
    pad = gt.shape[0]
    me = Place(bits)
    links = Links(send, recv, near)
    is_cos = me.c == 0

    def fetch_tokens(src, dst, s):
        return [links.fetch(src.at[s, :, pl.ds(t * tokens, tokens)], dst.at[s, t]) for t in range(parts)]

    x_in = [fetch_tokens(x_hbm, u1, s) for s in range(slots)]
    small_in = links.fetch(small_hbm.at[me.p], small)
    w1_in, w2_in = links.fetch(w1_hbm, wg1), links.fetch(w2_hbm, wg2)
    cot_in = [fetch_tokens(cot_hbm, gr2, s) for s in range(slots)]
    ht_in = links.fetch(ht_hbm.at[me.h], ht)
    gt_in = links.fetch(gt_hbm.at[me.h], gt)
    order_in = links.fetch(order_hbm.at[me.h], order)
    greet([me.core, me.side, me.cross] + me.flip)

    def input_view(s):
        def view(q, half=None):
            return xg.at[s, q, slice(None) if half is None else pl.ds(half * 2, 2), me.c]

        return view

    spread = [GatherBatch(me, links, input_view(s)) for s in range(slots)]
    over = [[] for _ in range(slots)]

    def hand_over(s, q):
        block = input_view(s)(q)
        over[s].append(links.copy(block, block, me.core))

    for s in range(slots):
        for t in range(parts):
            x_in[s][t].wait()
            xg[s, me.p, t, me.c] = u1[s, t].astype(LOW)
        if s == 0:
            spread[0].start()
        hand_over(s, me.p)
    pn[me.h] = vec_ref[...]
    params = [links.copy(pn.at[me.h], pn.at[me.h], device) for device in (me.core, me.side, me.cross)]

    small_in.wait()

    def make_rows(i, carry):
        big_cos, big_sin = small[0, pl.ds(i, 1), :], small[1, pl.ds(i, 1), :]
        by_cos = jnp.where(is_cos, big_cos, big_sin)
        by_sin = jnp.where(is_cos, -big_sin, big_cos)
        at = pl.ds(pl.multiple_of(i * FINE, FINE), FINE)
        for n in range(piece // 256):
            cut = slice(n * 256, (n + 1) * 256)
            tab[at, cut] = (by_cos[:, cut] * small[2, :, cut] + by_sin[:, cut] * small[3, :, cut]).astype(LOW)
        return carry

    lax.fori_loop(0, FINE, make_rows, 0)
    spread[0].forward()
    hand_over(0, me.py)
    hand_over(0, me.pz)
    if slots > 1:
        spread[1].start()
    moved = []
    for s in range(slots):
        for t in range(parts):
            cot_in[s][t].wait()
            cs[s, t] = (gr2[s, t] * live_ref[s]).astype(LOW)
        ct[s, me.h] = cs[s, me.h]
        for to, device in ((me.hc, me.core), (me.hx, me.side), (me.hd, me.cross)):
            moved.append(links.copy(cs.at[s, to], ct.at[s, me.h], device))
    w1_in.wait()
    w2_in.wait()

    def make_weights(r, carry):
        at = columns(r, 256)
        for n in range(units // 256):
            cut = slice(n * 256, (n + 1) * 256)
            for whole, plain, turned in ((wg1, w1, w1t), (wg2, w2, w2t)):
                tile = whole[at, cut]
                plain[at, cut] = tile.astype(LOW)
                turned[cut, at] = tile.T.astype(LOW)
        return carry

    lax.fori_loop(0, width // 256, make_weights, 0)
    ht_in.wait()

    sums = [
        Scatter(me, links, rows, sc.at[s], rc.at[s], sx.at[s], rx.at[s], acc.at[s]) for s in range(slots)
    ]

    def transform(s, t, sink):
        at = columns(t, tokens)
        total = None
        for q in range(SPLIT):
            for n in range(parts):
                first = q * piece + n * tokens
                share = dot(xg[s, q, n].reshape(2 * rows, tokens), tab[first : first + tokens, at])
                total = share if total is None else total + share
        ab[...] = total.astype(LOW)
        for i in range(parts):
            own = jnp.where(me.h == i, 1.0, 0.0).astype(F32)
            sink(i, dot(ht[i], ab[...]) + own * u1[s, t])

    for s in range(slots):
        if s > 0:
            spread[s].forward()
            hand_over(s, me.py)
            hand_over(s, me.pz)
        spread[s].finish()
        hand_over(s, me.pd)
        for made in over[s]:
            made.wait_recv()
        sums[s].run(functools.partial(transform, s))
        links.settle(over[s] + [spread[s].by_y, spread[s].by_z, spread[s].on_y, spread[s].on_z])
    for made in params:
        made.wait_recv()

    def param(k, i):
        return pn[i, :, k : k + 1]

    def lane_sum(k, i, s, value):
        folded = value[:, :128] + value[:, 128:]
        lanes[k, i] = folded if s == 0 else lanes[k, i] + folded

    def norm_first(s):
        whole = sums[s].acc
        total, squares = 0.0, 0.0
        for i in range(parts):
            v = sums[s].value(i)
            whole[i, 0:rows] = v
            total, squares = total + up(v), squares + up(v * v)
        mean = total / width
        inverse = lax.rsqrt(squares / width - mean * mean + EPS)
        inv1[s] = inverse
        for i in range(parts):
            u = (whole[i, 0:rows] - mean) * inverse
            u1[s, i] = u
            yf[s, me.h, i * rows : (i + 1) * rows, :] = (u * param(0, i) + param(1, i)).astype(LOW)

    def forward_in(s, t):
        for i in range(parts):
            at = slice(i * rows, (i + 1) * rows)
            h, slope = gelu_both(dot(w1t[at, :], yf[s, t]) + vec_ref[:, 5 + i : 6 + i])
            hf[s, t, at, :] = h.astype(LOW)
            df[s, t, at, :] = slope.astype(LOW)

    def forward_out(s, t, sink):
        for i in range(parts):
            sink(i, dot(w2t[i * rows : (i + 1) * rows, :], hf[s, t]))

    def norm_second(s):
        whole = sums[s].acc
        total, squares = 0.0, 0.0
        for i in range(parts):
            v = u1[s, i] * param(0, i) + param(1, i) + sums[s].value(i) + param(2, i)
            whole[i, 0:rows] = v
            total, squares = total + up(v), squares + up(v * v)
        mean = total / width
        inverse = lax.rsqrt(squares / width - mean * mean + EPS)
        total, cross = 0.0, 0.0
        for i in range(parts):
            u = (whole[i, 0:rows] - mean) * inverse
            whole[i, 0:rows] = u
            cs[s, i] = (u * param(3, i) + param(4, i)).astype(LOW)
            g = ct[s, i].astype(F32)
            lane_sum(0, i, s, g * u)
            lane_sum(1, i, s, g)
            q = g * param(3, i)
            total, cross = total + up(q), cross + up(q * u)
        total, cross = total / width, cross / width
        for i in range(parts):
            q = ct[s, i].astype(F32) * param(3, i)
            grad = inverse * (q - total - whole[i, 0:rows] * cross)
            gr2[s, i] = grad
            lane_sum(2, i, s, grad)
            zf[s, me.h, i * rows : (i + 1) * rows, :] = grad.astype(LOW)

    def backward_in(s, t, fresh):
        for i in range(parts):
            at = slice(i * rows, (i + 1) * rows)
            gp = dot(w2[at, :], zf[s, t]) * df[s, t, at, :].astype(F32)
            lane_sum(5, i, 0 if fresh else 1, gp)
            df[s, t, at, :] = gp.astype(LOW)

    def backward_out(s, t, sink):
        for i in range(parts):
            sink(i, dot(w1[i * rows : (i + 1) * rows, :], df[s, t]))

    def weight_grads(s):
        def one(r, carry):
            at = columns(r, 256)
            for n in range(units // 256):
                cut = slice(n * 256, (n + 1) * 256)
                first, second = 0.0, 0.0
                for t in range(parts):
                    first = first + dot_rows(yf[s, t, at, :], df[s, t, cut, :])
                    second = second + dot_rows(hf[s, t, at, :], zf[s, t, cut, :])
                wg1[at, cut] = first if s == 0 else wg1[at, cut] + first
                wg2[at, cut] = second if s == 0 else wg2[at, cut] + second
            return carry

        lax.fori_loop(0, units // 256, one, 0)

    def norm_first_back(s):
        whole = sums[s].acc
        total, cross = 0.0, 0.0
        for i in range(parts):
            grad = gr2[s, i] + sums[s].value(i)
            whole[i, 0:rows] = grad
            u = u1[s, i]
            lane_sum(3, i, s, grad * u)
            lane_sum(4, i, s, grad)
            q = grad * param(0, i)
            total, cross = total + up(q), cross + up(q * u)
        total, cross = total / width, cross / width
        for i in range(parts):
            q = whole[i, 0:rows] * param(0, i)
            xg[s, me.h, i, 0] = (inv1[s] * (q - total - u1[s, i] * cross)).astype(LOW)

    def rows_of(whole, s):
        return lambda t: whole.at[s, t]

    firsts = [GatherHidden(me, links, rows_of(yf, s)) for s in range(slots)]
    for s in range(slots):
        sums[s].wait()
        norm_first(s)
        firsts[s].start()
        forward_in(s, me.h)
        firsts[s].by_core.wait_recv()
        forward_in(s, me.hc)
    for s in range(slots):
        firsts[s].forward()
        forward_in(s, me.hx)
        firsts[s].by_far.wait_recv()
        forward_in(s, me.hd)
        sums[s].run(functools.partial(forward_out, s))
    for made in moved:
        made.wait_recv()
    links.settle(moved)
    seconds = [GatherHidden(me, links, rows_of(zf, s)) for s in range(slots)]
    for s in range(slots):
        sums[s].wait()
        norm_second(s)
        seconds[s].start()
        backward_in(s, me.h, s == 0)
        seconds[s].by_core.wait_recv()
        backward_in(s, me.hc, False)
    for s in range(slots):
        seconds[s].forward()
        backward_in(s, me.hx, False)
        seconds[s].by_far.wait_recv()
        backward_in(s, me.hd, False)
        sums[s].run(functools.partial(backward_out, s))

    def mix_view(s):
        return lambda t: xg.at[s, t, :, 0]

    def freq_view(s):
        cuts = (pl.ds(0, pad // 32 * 16), pl.ds(pad // 32 * 16, pad - pad // 32 * 16))

        def view(q, half=None):
            return ug.at[s, q] if half is None else ug.at[s, q, cuts[half]]

        return view

    gathers = [GatherHidden(me, links, mix_view(s)) for s in range(slots)]
    spreads = [GatherBatch(me, links, freq_view(s)) for s in range(slots)]
    heavy = [
        Reduce(me, links, wg2, low.at[0], landing.at[0], hf.at[0]),
        Reduce(me, links, wg1, low.at[1], landing.at[1], df.at[0]),
    ]

    def features(s, t):
        whole = jnp.concatenate([xg[s, t, i, 0] for i in range(parts)], 0)
        ug[s, me.p, :, columns(t, tokens)] = dot(gt[...], whole).astype(LOW)

    for s in range(slots):
        weight_grads(s)
        if s == slots - 1:
            for one in heavy:
                one.step()
        sums[s].wait()
        norm_first_back(s)
        gathers[s].start()
    outs = []
    for s in range(slots):
        ct[s, me.h] = cs[s, me.h]
        for to, device in ((me.hc, me.core), (me.hx, me.side), (me.hd, me.cross)):
            outs.append(links.copy(cs.at[s, to], ct.at[s, me.h], device))
    gt_in.wait()
    order_in.wait()
    for s in range(slots):
        features(s, me.h)
        gathers[s].by_core.wait_recv()
        features(s, me.hc)
        gathers[s].forward()
        features(s, me.hx)
        gathers[s].by_far.wait_recv()
        features(s, me.hd)
        spreads[s].start()
        heavy[s % 2].step()

    ones = jnp.ones((8, 128), F32)

    def lane_total(k, i):
        return lax.dot_general(
            ones, lanes[k, i], (((1,), (1,)), ((), ())), precision=lax.Precision.HIGHEST, preferred_element_type=F32
        )

    row = lax.broadcasted_iota(jnp.int32, (8, rows), 0)
    for i in range(parts):
        packed = jnp.zeros((8, rows), F32)
        for k in range(5):
            packed = jnp.where(row == k, lane_total(k, i), packed)
        lsend[i] = packed
    packed = jnp.zeros((8, rows), F32)
    for i in range(parts):
        packed = jnp.where(row == i, lane_total(5, i), packed)
    light = [
        links.copy(lsend.at[to], lrecv.at[me.h], device)
        for to, device in ((me.hc, me.core), (me.hx, me.side), (me.hd, me.cross))
    ]
    ltot[0, 8:16] = packed

    sign = jnp.where((me.h == 0) | (me.h == 3), -1.0, 1.0).astype(F32)
    mine = jnp.where(is_cos, 1.0, sign)
    theirs = jnp.where(is_cos, sign, 1.0)
    stored = []

    def sequence(s):
        for t in range(parts):
            at = slice(t * tokens, (t + 1) * tokens)
            total = None
            for q in range(SPLIT):
                share = dot(ug[s, q], tab[q * piece : (q + 1) * piece, at])
                total = share if total is None else total + share
            acc[s, t] = total
            sc[s, 0, t] = total.astype(LOW)
        return links.copy(sc.at[s, 0], rc.at[s, 0], me.core)

    def ordered(s):
        for t in range(parts):
            pair = (mine * acc[s, t] + theirs * rc[s, 0, t].astype(F32)).astype(LOW)
            sx[s, t] = dot(order[...], pair).astype(LOW)

        @pl.when(is_cos)
        def _():
            for t in range(parts):
                rx[s, t] = sx[s, t]

        @pl.when(jnp.logical_not(is_cos))
        def _():
            made = links.copy(sx.at[s], rx.at[s], me.side)
            links.drop(made)
            made.wait()

        for t in range(parts):
            u1[s, t] = rx[s, t].astype(F32) + xg[s, t, me.h, 0].astype(F32)
            stored.append(links.fetch(u1.at[s, t], grad_hbm.at[s, :, pl.ds(t * tokens, tokens)]))

    for s in range(slots):
        links.settle(sums[s].sent)
    for s in range(slots):
        spreads[s].forward()
        heavy[s % 2].step()
        if s == 0:
            for made in light:
                made.wait_recv()
            ltot[0, 0:8] = lsend[me.h] + lrecv[me.hc] + lrecv[me.hx] + lrecv[me.hd]
        spreads[s].finish()
        swap = sequence(s)
        heavy[(s + 1) % 2].step()
        swap.wait_recv()
        ordered(s)
    for made in outs:
        made.wait_recv()
    for s in range(slots):
        for t in range(parts):
            stored.append(links.fetch(ct.at[s, t], out_hbm.at[s, :, pl.ds(t * tokens, tokens)]))
    busy, k = True, 0
    while busy or k < bits:
        if k < bits:
            pair = links.copy(ltot.at[k], lnext.at[k], me.flip[k])
        steps = [one.step() for one in heavy]
        busy = any(steps)
        if k < bits:
            pair.wait_recv()
            ltot[k + 1] = ltot[k] + lnext[k]
            k += 1
    for one, dst in zip(heavy, (wg2_hbm, wg1_hbm)):
        for n in range(one.blocks):
            stored.append(links.fetch(one.whole.at[n], dst.at[:, pl.ds(n * tokens, tokens)]))
    light_ref[...] = ltot[bits]
    for made in stored:
        made.wait()
    for made in list(links.open):
        made.wait_send()


def local(
    n_batch,
    layer_input,
    gain_first,
    shift_first,
    weight_in,
    bias_in,
    weight_out,
    bias_out,
    gain_second,
    shift_second,
    cotangent,
    live_counts,
):
    slots, rows, piece = layer_input.shape
    width = rows * HOLD
    tokens = piece // HOLD
    units = weight_in.shape[1]
    length = piece * SPLIT
    pad = rows + 16
    bits = n_batch.bit_length() - 1
    live = (jnp.arange(slots) < live_counts[0]).astype(F32)
    vectors = jnp.stack([gain_first, shift_first, bias_out, gain_second, shift_second])
    vectors = jnp.concatenate([vectors, bias_in.reshape(HOLD, rows), jnp.zeros((128 - 5 - HOLD, rows), F32)]).T
    small = sequence_tables(length, SPLIT)
    forward, backward, order = feature_tables(width, HOLD)
    any_, vmem = pl.BlockSpec(memory_space=pl.ANY), pl.BlockSpec(memory_space=pltpu.VMEM)
    block = (HOLD, rows, tokens)
    padded = (HOLD, pad, tokens)
    shard = (slots,) + block
    landing = landing_rows(width, bits)
    scratch = [
        ((length, piece), LOW), ((4, FINE, piece), F32), (forward.shape[1:], LOW), (backward.shape[1:], LOW),
        (order.shape[1:], LOW), ((slots, SPLIT, HOLD, 2, rows, tokens), LOW), (shard, LOW), (shard, LOW),
        ((2 * rows, tokens), LOW), ((slots, 2) + padded, LOW), ((slots, 2) + padded, LOW), (shard, LOW), (shard, LOW),
        ((slots,) + padded, F32), ((slots, HOLD, width, tokens), LOW), ((slots, HOLD, units, tokens), LOW),
        ((slots, HOLD, units, tokens), LOW), ((slots, HOLD, width, tokens), LOW), (shard, F32), (shard, F32),
        ((slots, 1, tokens), F32), ((6, HOLD, rows, 128), F32),
        ((width, units), LOW), ((units, width), LOW), ((units, width), LOW), ((width, units), LOW),
        ((width, units), F32), ((units, width), F32), ((2, width, units), LOW), ((2, landing, units), LOW),
        ((slots, SPLIT, pad, piece), LOW), ((HOLD, rows, 128), F32), ((HOLD, 8, rows), F32), ((HOLD, 8, rows), F32),
        ((bits + 1, 16, rows), F32), ((bits, 16, rows), F32),
    ]
    outs = [(layer_input.shape, LOW), (layer_input.shape, F32), ((width, units), LOW), ((units, width), LOW), ((16, rows), F32)]
    out, grad, wg1, wg2, light = pl.pallas_call(
        functools.partial(layer_kernel, bits),
        name="layer",
        out_shape=[jax.ShapeDtypeStruct(shape, kind) for shape, kind in outs],
        in_specs=[any_] * 8 + [vmem, pl.BlockSpec(memory_space=pltpu.SMEM)],
        out_specs=[any_] * 4 + [vmem],
        scratch_shapes=[pltpu.VMEM(shape, kind) for shape, kind in scratch]
        + [pltpu.SemaphoreType.DMA((128,)), pltpu.SemaphoreType.DMA((128,)), pltpu.SemaphoreType.DMA((64,))],
        compiler_params=pltpu.CompilerParams(
            collective_id=1, has_side_effects=True, vmem_limit_bytes=VMEM_LIMIT
        ),
    )(
        layer_input, cotangent, weight_in, weight_out, jnp.asarray(small), jnp.asarray(forward),
        jnp.asarray(backward), jnp.asarray(order), vectors, live,
    )
    out = out.astype(F32) * live[:, None, None]
    return (
        out, grad, light[3], light[4], wg1.astype(F32), light[8 : 8 + HOLD].reshape(units), wg2.astype(F32),
        light[2], light[0], light[1],
    )


def solution(mesh):
    return jax.shard_map(
        functools.partial(local, mesh.shape["batch"]),
        mesh=mesh,
        in_specs=(
            P(None, "hidden", "batch"),
            P("hidden"),
            P("hidden"),
            P(None, "hidden"),
            P("hidden"),
            P("hidden", None),
            P("hidden"),
            P("hidden"),
            P("hidden"),
            P(None, "hidden", "batch"),
            P("batch"),
        ),
        out_specs=(
            P(None, "hidden", "batch"),
            P(None, "hidden", "batch"),
            P("hidden"),
            P("hidden"),
            P(None, "hidden"),
            P("hidden"),
            P("hidden", None),
            P("hidden"),
            P("hidden"),
            P("hidden"),
        ),
        check_vma=False,
    )
```

```python
import functools
import math

import jax
import jax.numpy as jnp
import ml_dtypes
import numpy as np
from jax import lax
from jax.experimental import pallas as pl
from jax.experimental.pallas import tpu as pltpu
from jax.sharding import PartitionSpec as P

SPLIT = 4
HOLD = 4
EPS = 1e-06
FINE = 64
LOW = jnp.bfloat16
F32 = jnp.float32
MESH = pl.DeviceIdType.MESH
VMEM_LIMIT = 63 * 2**20


def dot(left, right):
    return jnp.dot(left, right, preferred_element_type=F32)


def dot_rows(left, right):
    return lax.dot_general(left, right, (((1,), (1,)), ((), ())), preferred_element_type=F32)


@functools.cache
def sequence_tables(length, split):
    column = np.arange(length)
    coarse = 2 * np.pi * ((FINE * np.arange(length // FINE)[:, None] * column) % length) / length
    fine = 2 * np.pi * ((np.arange(FINE)[:, None] * column) % length) / length
    factor = 1 / math.sqrt(length)
    whole = np.stack([np.cos(coarse), np.sin(coarse), factor * np.cos(fine), factor * np.sin(fine)])
    return np.ascontiguousarray(
        whole.reshape(4, FINE, split, length // split).transpose(2, 0, 1, 3).astype(np.float32)
    )


@functools.cache
def feature_tables(width, parts):
    index = np.arange(width)
    angle = 2 * np.pi * ((index[:, None] * index) % width) / width
    factor = 1 / math.sqrt(width)
    cos = (np.cos(angle) * factor).astype(np.float32).astype(ml_dtypes.bfloat16)
    sin = (np.sin(angle) * factor).astype(np.float32).astype(ml_dtypes.bfloat16)
    part = width // parts
    pad = part + 16
    forward = np.zeros((parts, parts, part, 2 * part), ml_dtypes.bfloat16)
    backward = np.zeros((parts, pad, width), ml_dtypes.bfloat16)
    order = np.zeros((parts, part, pad), ml_dtypes.bfloat16)
    for h in range(parts):
        chip = slice((h // 2) * 2 * part, (h // 2 + 1) * 2 * part)
        forward[h] = (cos if h % 2 == 0 else -sin)[:, chip].reshape(parts, part, 2 * part)
        first = (h // 2) * part
        backward[h, : part + 1] = (cos, sin)[h % 2][first : first + part + 1]
        for i in range(part):
            order[h, i, i if h in (0, 3) else part - i] = 1
    return forward, backward, order


class Place:
    def __init__(self, bits):
        h = lax.axis_index("hidden")
        b = lax.axis_index("batch")
        self.h, self.b = h, b
        self.c = lax.rem(h, 2)
        self.x = lax.div(h, 2)
        self.hc = h + 1 - 2 * self.c
        self.hx = lax.rem(h + 2, 4)
        self.hd = lax.rem(self.hc + 2, 4)
        self.p = lax.rem(b, 4)
        self.bit = [lax.rem(lax.div(b, 2**k), 2) for k in range(bits)]
        self.py = self.p + 1 - 2 * self.bit[0]
        self.pz = lax.rem(self.p + 2, 4)
        self.pd = lax.rem(self.py + 2, 4)
        self.core = {"hidden": self.hc}
        self.side = {"hidden": self.hx}
        self.cross = {"hidden": self.hd}
        self.flip = [{"batch": b + 2**k - 2 ** (k + 1) * self.bit[k]} for k in range(bits)]
        self.ydev, self.zdev = self.flip[:2]


class Links:
    def __init__(self, send, recv, near):
        self.send, self.recv, self.near = send, recv, near
        self.used, self.fetched, self.open = 0, 0, []

    def describe(self, src, dst, device):
        i = self.used
        self.used += 1
        return pltpu.make_async_remote_copy(
            src_ref=src,
            dst_ref=dst,
            send_sem=self.send.at[i],
            recv_sem=self.recv.at[i],
            device_id=device,
            device_id_type=MESH,
        )

    def copy(self, src, dst, device):
        made = self.describe(src, dst, device)
        made.start()
        self.open.append(made)
        return made

    def settle(self, some):
        for made in some:
            made.wait_send()
            self.drop(made)

    def drop(self, made):
        self.open = [other for other in self.open if other is not made]

    def fetch(self, src, dst):
        made = pltpu.make_async_copy(src, dst, self.near.at[self.fetched])
        self.fetched += 1
        made.start()
        return made


def greet(devices):
    barrier = pltpu.get_barrier_semaphore()
    for device in devices:
        pl.semaphore_signal(barrier, inc=1, device_id=device, device_id_type=MESH)
    pl.semaphore_wait(barrier, len(devices))


class GatherHidden:
    def __init__(self, me, links, view):
        self.me, self.links, self.view = me, links, view

    def start(self):
        own = self.view(self.me.h)
        self.by_side = self.links.copy(own, own, self.me.side)
        self.by_core = self.links.copy(own, own, self.me.core)

    def forward(self):
        self.by_side.wait_recv()
        far = self.view(self.me.hx)
        self.by_far = self.links.copy(far, far, self.me.core)


class GatherBatch:
    def __init__(self, me, links, view):
        self.me, self.links, self.view = me, links, view

    def start(self):
        own = self.view(self.me.p)
        self.by_y = self.links.copy(own, own, self.me.ydev)
        self.by_z = self.links.copy(own, own, self.me.zdev)

    def forward(self):
        self.by_y.wait_recv()
        part = self.view(self.me.py, 0)
        self.on_z = self.links.copy(part, part, self.me.zdev)
        self.by_z.wait_recv()
        part = self.view(self.me.pz, 1)
        self.on_y = self.links.copy(part, part, self.me.ydev)

    def finish(self):
        self.on_z.wait_recv()
        self.on_y.wait_recv()


class Scatter:
    def __init__(self, me, links, rows, sc, rc, sx, rx, acc):
        self.me, self.links, self.rows, self.sent = me, links, rows, []
        self.sc, self.rc, self.sx, self.rx, self.acc = sc, rc, sx, rx, acc

    def run(self, block, hook=lambda k: None):
        x, c = self.me.x, self.me.c
        far, near, cut = 2 * (1 - x), 2 * x, pl.ds(0, self.rows)
        self.links.settle(self.sent)
        self.sent = []
        for k, t in enumerate((far + 1 - c, far + c, near + 1 - c, near + c)):
            n, first = k // 2, k % 2 == 0

            def sink(i, value):
                if first:
                    self.sc[n, i, cut] = value.astype(LOW)
                    return
                if i == 0:
                    self.by_core.wait_recv()
                value = value + self.rc[n, i, cut].astype(F32)
                if n == 0:
                    self.sx[i] = value.astype(LOW)
                else:
                    self.acc[i, cut] = value

            block(t, sink)
            if first:
                self.by_core = self.links.copy(self.sc.at[n, :, cut], self.rc.at[n, :, cut], self.me.core)
                self.sent.append(self.by_core)
            elif n == 0:
                self.by_side = self.links.copy(self.sx, self.rx, self.me.side)
                self.sent.append(self.by_side)
            hook(k)

    def wait(self):
        self.by_side.wait_recv()

    def value(self, i):
        return self.acc[i, 0 : self.rows] + self.rx[i].astype(F32)


class Share:
    def __init__(self, me, links, rows, sc, rc, acc):
        self.me, self.links, self.cut = me, links, pl.ds(0, rows)
        self.sc, self.rc, self.acc = sc, rc, acc

    def away(self, block):
        def sink(i, value):
            self.sc[i, self.cut] = value.astype(LOW)

        block(1 - self.me.c, sink)
        self.by_core = self.links.copy(self.sc.at[:, self.cut], self.rc.at[:, self.cut], self.me.core)

    def home(self, block):
        def sink(i, value):
            self.acc[i, self.cut] = value

        block(self.me.c, sink)

    def wait(self):
        self.by_core.wait_recv()

    def value(self, i):
        return self.acc[i, self.cut] + self.rc[i, self.cut].astype(F32)


class Reduce:
    def __init__(self, me, links, given, given_landing, total, low, landing, whole):
        self.me, self.links = me, links
        self.given, self.given_landing = given, given_landing
        self.total, self.low, self.landing, self.whole = total, low, landing, whole
        self.blocks = total.shape[1] // whole.shape[2]
        bits, size = len(me.bit), total.shape[0]
        self.halvings = halvings(size, bits)
        self.plan = [(self.cross, 0), (self.halve, 0), (self.quarter, 0)]
        self.plan += [(self.halve, k) for k in range(3, self.halvings)]
        self.plan += [(self.double, k) for k in range(self.halvings, bits)]
        self.plan += [(self.gather, k) for k in reversed(range(3, self.halvings))]
        self.plan += [(self.gather_quarters, 0), (self.gather, 0)]
        self.at, self.used, self.lows, self.after = 0, 0, [0], None

    def span(self, first, size):
        return pl.ds(pl.multiple_of(first, 16), size)

    def end(self):
        if self.after is not None:
            self.after()
            self.after = None

    def step(self):
        self.end()
        if self.at == len(self.plan):
            return False
        kind, k = self.plan[self.at]
        self.at += 1
        kind(k)
        return True

    def land(self, size):
        self.used += size
        return pl.ds(self.used - size, size)

    def cross(self, _):
        made = self.links.copy(self.given, self.given_landing, self.me.side)

        def after():
            made.wait_recv()
            self.total[...] += self.given_landing[...].astype(F32)

        self.after = after

    def halve(self, k):
        half = self.total.shape[0] >> (k + 1)
        u = self.me.bit[k]
        keep = self.lows[-1] + u * half
        give = self.span(self.lows[-1] + (1 - u) * half, half)
        self.lows.append(keep)
        place = self.land(half)
        self.low[give, :] = self.total[give, :].astype(LOW)
        made = self.links.copy(self.low.at[give], self.landing.at[place], self.me.flip[k])

        def after():
            made.wait_recv()
            mine = self.span(keep, half)
            self.total[mine, :] += self.landing[place, :].astype(F32)
            if k + 1 == self.halvings:
                self.low[mine, :] = self.total[mine, :].astype(LOW)

        self.after = after

    def column(self, d):
        v = self.me.bit[1] + 2 * self.me.bit[2]
        w = lax.rem(v + d, 4)
        return w, {"batch": self.me.b + 2 * (w - v)}

    def quarter(self, _):
        size = self.total.shape[0] >> 3
        first = self.lows[-1]
        keep = first + (self.me.bit[1] + 2 * self.me.bit[2]) * size
        self.lows += [None, keep]
        made, places = [], []
        for d in (2, 1, 3):
            w, device = self.column(d)
            give = self.span(first + w * size, size)
            place = self.land(size)
            self.low[give, :] = self.total[give, :].astype(LOW)
            made.append(self.links.copy(self.low.at[give], self.landing.at[place], device))
            places.append(place)

        def after():
            mine = self.span(keep, size)
            total = self.total[mine, :]
            for one, place in zip(made, places):
                one.wait_recv()
                total += self.landing[place, :].astype(F32)
            self.total[mine, :] = total
            if self.halvings == 3:
                self.low[mine, :] = total.astype(LOW)

        self.after = after

    def gather_quarters(self, _):
        size = self.total.shape[0] >> 3
        mine = self.span(self.lows[3], size)
        if self.halvings == 3:
            self.spread_out(mine)
        part = self.whole.at[pl.ds(0, self.blocks), mine]
        made = [self.links.copy(part, part, self.column(d)[1]) for d in (2, 1, 3)]

        def after():
            for one in made:
                one.wait_recv()

        self.after = after

    def spread_out(self, mine):
        wide = self.whole.shape[2]
        for n in range(self.blocks):
            self.whole[n, mine, :] = self.low[mine, n * wide : (n + 1) * wide]

    def double(self, k):
        size = self.total.shape[0] >> self.halvings
        mine = self.span(self.lows[-1], size)
        place = self.land(size)
        made = self.links.copy(self.low.at[mine], self.landing.at[place], self.me.flip[k])

        def after():
            made.wait_recv()
            self.links.settle([made])
            self.low[mine, :] = (self.low[mine, :].astype(F32) + self.landing[place, :].astype(F32)).astype(LOW)

        self.after = after

    def gather(self, k):
        size = self.total.shape[0] >> (k + 1)
        mine = self.span(self.lows[k + 1], size)
        if k + 1 == self.halvings:
            self.spread_out(mine)
        part = self.whole.at[pl.ds(0, self.blocks), mine]
        self.after = self.links.copy(part, part, self.me.flip[k]).wait_recv


def halvings(size, bits):
    count = 0
    while count < bits and (size >> (count + 1)) % 16 == 0:
        count += 1
    return count


def chunk_rows(units):
    half = units // 2
    return (half, half), (half, units // 3, units - half - units // 3)


def landing_rows(size, bits):
    count = halvings(size, bits)
    taken = [size >> 1, 3 * (size >> 3)] + [size >> (k + 1) for k in range(3, count)]
    return sum(taken) + (bits - count) * (size >> count)


def columns(t, size):
    return pl.ds(pl.multiple_of(t * size, size), size)


ROOT = math.sqrt(2 / math.pi)
CUBE = 0.044715


def gelu_both(v):
    square = v * v
    t = jnp.tanh(v * (ROOT + ROOT * CUBE * square))
    half = 0.5 + 0.5 * t
    slope = half + (0.5 * v) * (1 - t * t) * (ROOT + 3 * ROOT * CUBE * square)
    return v * half, slope


def up(value):
    return jnp.sum(value, 0, keepdims=True)


def layer_kernel(
    bits,
    x_hbm, cot_hbm, w1_hbm, w2_hbm, small_hbm, ht_hbm, gt_hbm, order_hbm,
    g1_ref, s1_ref, bo_ref, g2_ref, s2_ref, bin_ref, live_ref,
    out_hbm, grad_hbm, wg1_hbm, wg2_hbm, light_ref,
    tab, small, ht, gt, order, xg, cs, ct, ab, sc, rc, sx, rx, acc, yf, hf, df, zf, u1, gr2, inv1, lanes,
    wr, wt, wg, given, landing, ug, rowv, pn, lsend, lrecv, lbias, ltot, lnext, send, recv, near,
):
    slots, _, piece = x_hbm.shape
    parts, rows, tokens = cs.shape[1:]
    width = parts * rows
    units = wg.shape[1]
    pad = gt.shape[0]
    me = Place(bits)
    links = Links(send, recv, near)
    is_cos = me.c == 0

    def fetch_tokens(src, dst, s):
        return [links.fetch(src.at[s, :, pl.ds(t * tokens, tokens)], dst.at[s, t]) for t in range(parts)]

    x_in = [fetch_tokens(x_hbm, u1, s) for s in range(slots)]
    w1_in, w2_in = links.fetch(w1_hbm, wg.at[0]), links.fetch(w2_hbm, wg.at[1])
    small_in = links.fetch(small_hbm.at[me.p], small)
    cot_in = [fetch_tokens(cot_hbm, gr2, s) for s in range(slots)]
    ht_in = links.fetch(ht_hbm.at[me.h], ht)
    gt_in = links.fetch(gt_hbm.at[me.h], gt)
    order_in = links.fetch(order_hbm.at[me.h], order)
    greet([me.core, me.side, me.cross] + me.flip)

    def input_view(s):
        def view(q, half=None):
            return xg.at[s, q, slice(None) if half is None else pl.ds(half * 2, 2), me.c]

        return view

    spread = [GatherBatch(me, links, input_view(s)) for s in range(slots)]
    over = [[] for _ in range(slots)]

    def hand_over(s, q):
        block = input_view(s)(q)
        over[s].append(links.copy(block, block, me.core))

    for s in range(slots):
        for t in range(parts):
            x_in[s][t].wait()
            xg[s, me.p, t, me.c] = u1[s, t].astype(LOW)
        if s == 0:
            spread[0].start()
        hand_over(s, me.p)

    far = 1 - me.x
    quarter, straight = units // SPLIT, width - 256

    def weight_view(q, half=None):
        at = pl.ds(pl.multiple_of(q * quarter, 16), quarter)
        return wr.at[slice(None) if half is None else pl.ds(half, 1), far, at, pl.ds(0, straight)]

    weights = GatherBatch(me, links, weight_view)
    w1_in.wait()
    w2_in.wait()

    def own_weights(r, carry):
        at = columns(r, 256)
        for n in range(units // 256):
            cut = slice(n * 256, (n + 1) * 256)
            first, second = wg[0, at, cut], wg[1, at, cut]
            wt[0, me.x, at, cut] = first.astype(LOW)
            wr[0, me.x, cut, at] = first.T.astype(LOW)
            wr[1, me.x, at, cut] = second.astype(LOW)
            wt[1, me.x, cut, at] = second.T.astype(LOW)
        return carry

    lax.fori_loop(0, units // 256, own_weights, 0)
    quarter_at = pl.ds(pl.multiple_of(me.p * quarter, 16), quarter)
    mine_w = wr.at[:, me.x, quarter_at, pl.ds(0, straight)]
    by_side = links.copy(mine_w, mine_w, me.side)
    mine_w = wr.at[:, me.x, :, pl.ds(straight, 256)]
    direct = links.copy(mine_w, mine_w, me.side)

    vectors = (g1_ref, s1_ref, bo_ref, g2_ref, s2_ref)
    rowv[...] = jnp.zeros_like(rowv)
    for k, ref in enumerate(vectors):
        rowv[k : k + 1, 0:rows] = ref[...]
    for i in range(parts):
        rowv[5 + i : 6 + i, 0:rows] = bin_ref[:, i * rows : (i + 1) * rows]
    pn[me.h] = rowv[...].T[0:rows, :]
    params = [links.copy(pn.at[me.h], pn.at[me.h], device) for device in (me.core, me.side, me.cross)]

    small_in.wait()

    def make_rows(i, carry):
        big_cos, big_sin = small[0, pl.ds(i, 1), :], small[1, pl.ds(i, 1), :]
        by_cos = jnp.where(is_cos, big_cos, big_sin)
        by_sin = jnp.where(is_cos, -big_sin, big_cos)
        at = pl.ds(pl.multiple_of(i * FINE, FINE), FINE)
        for n in range(piece // 256):
            cut = slice(n * 256, (n + 1) * 256)
            tab[at, cut] = (by_cos[:, cut] * small[2, :, cut] + by_sin[:, cut] * small[3, :, cut]).astype(LOW)
        return carry

    lax.fori_loop(0, FINE, make_rows, 0)
    for s in range(slots):
        for t in range(parts):
            cot_in[s][t].wait()
            cs[s, t] = (gr2[s, t] * live_ref[s]).astype(LOW)
        ct[s, me.h] = cs[s, me.h]
    ht_in.wait()

    sums = [
        Scatter(me, links, rows, sc.at[s], rc.at[s], sx.at[s], rx.at[s], acc.at[s]) for s in range(slots)
    ]

    def transform(s, t, sink):
        at = columns(t, tokens)
        total = None
        for q in range(SPLIT):
            for n in range(parts):
                first = q * piece + n * tokens
                share = dot(xg[s, q, n].reshape(2 * rows, tokens), tab[first : first + tokens, at])
                total = share if total is None else total + share
        ab[...] = total.astype(LOW)
        for i in range(parts):
            own = jnp.where(me.h == i, 1.0, 0.0).astype(F32)
            sink(i, dot(ht[i], ab[...]) + own * u1[s, t])

    def next_input(k):
        if k == 2:
            spread[1].forward()
            hand_over(1, me.py)
            hand_over(1, me.pz)
            by_side.wait_recv()
            weights.start()

    def next_weights(k):
        if k == 2:
            weights.forward()

    spread[0].forward()
    spread[1].start()
    hand_over(0, me.py)
    hand_over(0, me.pz)
    for s, hook in enumerate((next_input, next_weights)):
        spread[s].finish()
        hand_over(s, me.pd)
        for made in over[s]:
            made.wait_recv()
        sums[s].run(functools.partial(transform, s), hook)
        links.settle(over[s] + [spread[s].by_y, spread[s].by_z, spread[s].on_y, spread[s].on_z])
    moved = []
    for s in range(slots):
        for to, device in ((me.hc, me.core), (me.hx, me.side), (me.hd, me.cross)):
            moved.append(links.copy(cs.at[s, to], ct.at[s, me.h], device))
    for made in params:
        made.wait_recv()

    def param(k, i):
        return pn[i, :, k : k + 1]

    def folded(value):
        return value[:, :128] + value[:, 128:]

    def lane_sum(k, i, s, value):
        lanes[k, i] = folded(value) if s == 0 else lanes[k, i] + folded(value)

    def norm_first(s):
        whole = sums[s].acc
        total, squares = 0.0, 0.0
        for i in range(parts):
            v = sums[s].value(i)
            whole[i, 0:rows] = v
            total, squares = total + up(v), squares + up(v * v)
        mean = total / width
        inverse = lax.rsqrt(squares / width - mean * mean + EPS)
        inv1[s] = inverse
        for i in range(parts):
            u = (whole[i, 0:rows] - mean) * inverse
            u1[s, i] = u
            yf[s, me.c, i * rows : (i + 1) * rows, :] = (u * param(0, i) + param(1, i)).astype(LOW)

    def forward_in(s, k, unit):
        for i in range(parts):
            at = slice(i * rows, (i + 1) * rows)
            bias = pn[2 * unit + me.c, :, 5 + i : 6 + i]
            h, slope = gelu_both(dot(wr[0, unit, at, :], yf[s, k]) + bias)
            hf[s, 2 * k + unit, at, :] = h.astype(LOW)
            df[s, 2 * k + unit, at, :] = slope.astype(LOW)

    def forward_out(s, k, sink):
        for i in range(parts):
            at = slice(i * rows, (i + 1) * rows)
            sink(i, dot(wt[1, 0, at, :], hf[s, 2 * k]) + dot(wt[1, 1, at, :], hf[s, 2 * k + 1]))

    def norm_second(s, shared):
        whole = shared.acc
        total, squares = 0.0, 0.0
        for i in range(parts):
            v = u1[s, i] * param(0, i) + param(1, i) + shared.value(i) + param(2, i)
            whole[i, 0:rows] = v
            total, squares = total + up(v), squares + up(v * v)
        mean = total / width
        inverse = lax.rsqrt(squares / width - mean * mean + EPS)
        total, cross = 0.0, 0.0
        for i in range(parts):
            u = (whole[i, 0:rows] - mean) * inverse
            whole[i, 0:rows] = u
            cs[s, i] = (u * param(3, i) + param(4, i)).astype(LOW)
            g = ct[s, i].astype(F32)
            lane_sum(0, i, s, g * u)
            lane_sum(1, i, s, g)
            q = g * param(3, i)
            total, cross = total + up(q), cross + up(q * u)
        total, cross = total / width, cross / width
        for i in range(parts):
            q = ct[s, i].astype(F32) * param(3, i)
            grad = inverse * (q - total - whole[i, 0:rows] * cross)
            gr2[s, i] = grad
            lane_sum(2, i, s, grad)
            zf[s, me.c, i * rows : (i + 1) * rows, :] = grad.astype(LOW)

    def backward_in(s, k, fresh):
        for unit in range(2):
            for i in range(parts):
                at = slice(i * rows, (i + 1) * rows)
                gp = dot(wr[1, unit, at, :], zf[s, k]) * df[s, 2 * k + unit, at, :].astype(F32)
                place = 5 + unit
                lanes[place, i] = folded(gp) if fresh else lanes[place, i] + folded(gp)
                df[s, 2 * k + unit, at, :] = gp.astype(LOW)

    def backward_out(s, k, sink):
        for i in range(parts):
            at = slice(i * rows, (i + 1) * rows)
            sink(i, dot(wt[0, 0, at, :], df[s, 2 * k]) + dot(wt[0, 1, at, :], df[s, 2 * k + 1]))

    def weight_grad(which, unit, store):
        def one(r, carry):
            at = columns(r, 256)
            for n in range(units // 256):
                cut = slice(n * 256, (n + 1) * 256)
                total = 0.0
                for s in range(slots):
                    for k in range(2):
                        if which == 0:
                            total = total + dot_rows(hf[s, 2 * k + unit, at, :], zf[s, k, cut, :])
                        else:
                            total = total + dot_rows(yf[s, k, at, :], df[s, 2 * k + unit, cut, :])
                store(which, at, cut, total)
            return carry

        lax.fori_loop(0, units // 256, one, 0)

    def norm_first_back(s, shared):
        whole = shared.acc
        total, cross = 0.0, 0.0
        for i in range(parts):
            grad = gr2[s, i] + shared.value(i)
            whole[i, 0:rows] = grad
            u = u1[s, i]
            lane_sum(3, i, s, grad * u)
            lane_sum(4, i, s, grad)
            q = grad * param(0, i)
            total, cross = total + up(q), cross + up(q * u)
        total, cross = total / width, cross / width
        for i in range(parts):
            q = whole[i, 0:rows] * param(0, i)
            xg[s, me.h, i, 0] = (inv1[s] * (q - total - u1[s, i] * cross)).astype(LOW)

    def to_core(block):
        return links.copy(block, block, me.core)

    outward = [Share(me, links, rows, sc.at[s, 0], rc.at[s, 0], acc.at[s]) for s in range(slots)]
    inward = [Share(me, links, rows, sc.at[s, 1], rc.at[s, 1], acc.at[s]) for s in range(slots)]

    def enter(s):
        sums[s].wait()
        norm_first(s)
        got = to_core(yf.at[s, me.c])
        forward_in(s, me.c, me.x)
        got.wait_recv()
        forward_in(s, 1 - me.c, me.x)

    def leave(s):
        links.settle(sums[s].sent)
        forward_in(s, 1 - me.c, far)
        forward_in(s, me.c, far)
        outward[s].away(functools.partial(forward_out, s))
        outward[s].home(functools.partial(forward_out, s))

    def far_weights(r, carry):
        at = columns(r, 256)
        for n in range(units // 256):
            cut = slice(n * 256, (n + 1) * 256)
            wt[0, far, cut, at] = wr[0, far, at, cut].astype(F32).T.astype(LOW)
            wt[1, far, cut, at] = wr[1, far, at, cut].astype(F32).T.astype(LOW)
        return carry

    enter(0)
    weights.finish()
    direct.wait_recv()
    lax.fori_loop(0, units // 256, far_weights, 0)
    links.settle([by_side, direct, weights.by_y, weights.by_z, weights.on_y, weights.on_z])
    leave(0)
    enter(1)
    leave(1)
    for made in moved:
        made.wait_recv()
    links.settle(moved)
    seconds = []
    for s in range(slots):
        outward[s].wait()
        norm_second(s, outward[s])
        seconds.append(to_core(zf.at[s, me.c]))

    def mix_view(s):
        return lambda t: xg.at[s, t, :, 0]

    def freq_view(s):
        cuts = (pl.ds(0, pad // 32 * 16), pl.ds(pad // 32 * 16, pad - pad // 32 * 16))

        def view(q, half=None):
            return ug.at[s, q] if half is None else ug.at[s, q, cuts[half]]

        return view

    gathers = [GatherHidden(me, links, mix_view(s)) for s in range(slots)]
    spreads = [GatherBatch(me, links, freq_view(s)) for s in range(slots)]
    heavy, chunks, outs = [], [], []
    for which, whole in ((0, hf), (1, df)):
        low, used = 0, 0
        for size in chunk_rows(units)[which]:
            at, place = pl.ds(low, size), pl.ds(used, landing_rows(size, bits))
            low, used = low + size, used + landing_rows(size, bits)
            chunks.append((which, at))
            heavy.append(
                Reduce(
                    me, links, wr.at[0, which, at], given.at[which, at], wg.at[which, at], wt.at[1, which, at],
                    landing.at[which, place], whole.at[0, :, at],
                )
            )

    def features(s, t):
        whole = jnp.concatenate([xg[s, t, i, 0] for i in range(parts)], 0)
        ug[s, me.p, :, columns(t, tokens)] = dot(gt[...], whole).astype(LOW)

    def store_given(which, at, cut, value):
        wr[0, which, at, cut] = value.astype(LOW)

    def store_kept(which, at, cut, value):
        wg[which, at, cut] = value

    for made in seconds:
        made.wait_recv()
    weight_grad(0, far, store_given)
    heavy[0].step()
    for s in range(slots):
        backward_in(s, me.c, s == 0)
        backward_in(s, 1 - me.c, False)
        inward[s].away(functools.partial(backward_out, s))
        inward[s].home(functools.partial(backward_out, s))
        if s > 0:
            inward[s - 1].wait()
            norm_first_back(s - 1, inward[s - 1])
            gathers[s - 1].start()
    inward[slots - 1].wait()
    norm_first_back(slots - 1, inward[slots - 1])
    gathers[slots - 1].start()
    weight_grad(1, far, store_given)
    weight_grad(0, me.x, store_kept)
    heavy[0].step()
    gt_in.wait()
    order_in.wait()

    def near_features(s):
        features(s, me.h)
        gathers[s].by_core.wait_recv()
        features(s, me.hc)

    def far_features(s):
        gathers[s].forward()
        features(s, me.hx)
        gathers[s].by_far.wait_recv()
        features(s, me.hd)

    ones = jnp.ones((8, 128), F32)

    def lane_total(k, i):
        return lax.dot_general(
            ones, lanes[k, i], (((1,), (1,)), ((), ())), precision=lax.Precision.HIGHEST, preferred_element_type=F32
        )

    row = lax.broadcasted_iota(jnp.int32, (8, rows), 0)
    for i in range(parts):
        packed = jnp.zeros((8, rows), F32)
        for k in range(5):
            packed = jnp.where(row == k, lane_total(k, i), packed)
        lsend[i] = packed
    for unit in range(2):
        packed = jnp.zeros((8, rows), F32)
        for i in range(parts):
            packed = jnp.where(row == i, lane_total(5 + unit, i), packed)
        lbias[unit] = packed
    light = []

    def start_small_sums():
        for to, device in ((me.hc, me.core), (me.hx, me.side), (me.hd, me.cross)):
            light.append(links.copy(lsend.at[to], lrecv.at[me.h], device))
        light.append(links.copy(lbias.at[far], lbias.at[2], me.side))

    sign = jnp.where((me.h == 0) | (me.h == 3), -1.0, 1.0).astype(F32)
    mine = jnp.where(is_cos, 1.0, sign)
    theirs = jnp.where(is_cos, sign, 1.0)
    stored = []

    def sequence(s):
        for t in range(parts):
            at = slice(t * tokens, (t + 1) * tokens)
            total = None
            for q in range(SPLIT):
                share = dot(ug[s, q], tab[q * piece : (q + 1) * piece, at])
                total = share if total is None else total + share
            acc[s, t] = total
            sc[s, 0, t] = total.astype(LOW)
        return links.copy(sc.at[s, 0], rc.at[s, 0], me.core)

    swaps, across = [], []

    def ordered(s):
        swaps[s].wait_recv()
        for t in range(parts):
            pair = (mine * acc[s, t] + theirs * rc[s, 0, t].astype(F32)).astype(LOW)
            sx[s, t] = dot(order[...], pair).astype(LOW)
        made = links.describe(sx.at[s], rx.at[s], me.side)
        across.append(made)

        @pl.when(jnp.logical_not(is_cos))
        def _():
            made.start()

    def store_grad(s):
        def store(part):
            for t in range(parts):
                u1[s, t] = part[s, t].astype(F32) + xg[s, t, me.h, 0].astype(F32)

        @pl.when(is_cos)
        def _():
            store(sx)

        @pl.when(jnp.logical_not(is_cos))
        def _():
            across[s].wait()
            store(rx)

        for t in range(parts):
            stored.append(links.fetch(u1.at[s, t], grad_hbm.at[s, :, pl.ds(t * tokens, tokens)]))

    for s in range(slots):
        links.settle([outward[s].by_core, inward[s].by_core])
    def start_outs():
        for s in range(slots):
            ct[s, me.h] = cs[s, me.h]
            for to, device in ((me.hc, me.core), (me.hx, me.side), (me.hd, me.cross)):
                outs.append(links.copy(cs.at[s, to], ct.at[s, me.h], device))

    def small_sums():
        for made in light:
            made.wait_recv()
        ltot[0, 0:8] = lsend[me.h] + lrecv[me.hc] + lrecv[me.hx] + lrecv[me.hd]
        ltot[0, 8:16] = lbias[me.x] + lbias[2]

    rounds = []

    def small_round():
        if rounds:
            k = len(rounds) - 1
            rounds[k].wait_recv()
            ltot[k + 1] = ltot[k] + lnext[k]
        k = len(rounds)
        if k < bits:
            rounds.append(links.copy(ltot.at[k], lnext.at[k], me.flip[k]))
            return True
        return False

    def pace(names):
        for n in names:
            heavy[n].step()

    start_small_sums()
    for one in heavy[1:]:
        one.step()
    weight_grad(1, me.x, store_kept)
    near_features(0)
    near_features(1)
    far_features(0)
    spreads[0].start()
    pace((0,))
    far_features(1)
    spreads[0].forward()
    spreads[1].start()
    small_sums()
    small_round()
    pace((0,))
    spreads[0].finish()
    swaps.append(sequence(0))
    ordered(0)
    spreads[1].forward()
    pace((1, 0))
    small_round()
    spreads[1].finish()
    swaps.append(sequence(1))
    ordered(1)
    start_outs()
    pace((1, 2, 1, 2, 3, 0, 4, 1, 2, 3, 4, 1, 2, 3, 4))
    store_grad(0)
    store_grad(1)
    busy = True
    while busy:
        busy = False
        for n in range(len(heavy)):
            busy = heavy[n].step() or busy
        if len(rounds) < bits:
            busy = small_round() or busy
    k = bits - 1
    rounds[k].wait_recv()
    ltot[bits] = ltot[k] + lnext[k]
    for made in outs:
        made.wait_recv()
    for s in range(slots):
        for t in range(parts):
            stored.append(links.fetch(ct.at[s, t], out_hbm.at[s, :, pl.ds(t * tokens, tokens)]))
    for one, (which, at) in zip(heavy, chunks):
        dst = (wg2_hbm, wg1_hbm)[which].at[at]
        for m in range(one.blocks):
            stored.append(links.fetch(one.whole.at[m], dst.at[:, pl.ds(m * tokens, tokens)]))
    light_ref[...] = ltot[bits]
    for made in stored:
        made.wait()
    for made in list(links.open):
        made.wait_send()


def local(
    n_batch,
    layer_input,
    gain_first,
    shift_first,
    weight_in,
    bias_in,
    weight_out,
    bias_out,
    gain_second,
    shift_second,
    cotangent,
    live_counts,
):
    slots, rows, piece = layer_input.shape
    width = rows * HOLD
    tokens = piece // HOLD
    units = weight_in.shape[1]
    length = piece * SPLIT
    pad = rows + 16
    bits = n_batch.bit_length() - 1
    live = (jnp.arange(slots) < live_counts[0]).astype(F32)
    vectors = (gain_first, shift_first, bias_out, gain_second, shift_second, bias_in)
    small = sequence_tables(length, SPLIT)
    forward, backward, order = feature_tables(width, HOLD)
    any_, vmem = pl.BlockSpec(memory_space=pl.ANY), pl.BlockSpec(memory_space=pltpu.VMEM)
    block = (HOLD, rows, tokens)
    padded = (HOLD, pad, tokens)
    shard = (slots,) + block
    landing = max(sum(landing_rows(size, bits) for size in sizes) for sizes in chunk_rows(units))
    scratch = [
        ((length, piece), LOW), ((4, FINE, piece), F32), (forward.shape[1:], LOW), (backward.shape[1:], LOW),
        (order.shape[1:], LOW), ((slots, SPLIT, HOLD, 2, rows, tokens), LOW), (shard, LOW), (shard, LOW),
        ((2 * rows, tokens), LOW), ((slots, 2) + padded, LOW), ((slots, 2) + padded, LOW), (shard, LOW), (shard, LOW),
        ((slots,) + padded, F32), ((slots, 2, width, tokens), LOW), ((slots, 4, units, tokens), LOW),
        ((slots, 4, units, tokens), LOW), ((slots, 2, width, tokens), LOW), (shard, F32), (shard, F32),
        ((slots, 1, tokens), F32), ((7, HOLD, rows, 128), F32),
        ((2, 2, units, width), LOW), ((2, 2, width, units), LOW), ((2, units, width), F32),
        ((2, units, width), LOW), ((2, landing, width), LOW),
        ((slots, SPLIT, pad, piece), LOW), ((128, 256), F32), ((HOLD, rows, 128), F32), ((HOLD, 8, rows), F32),
        ((HOLD, 8, rows), F32), ((3, 8, rows), F32), ((bits + 1, 16, rows), F32), ((bits, 16, rows), F32),
    ]
    outs = [(layer_input.shape, LOW), (layer_input.shape, F32), ((width, units), LOW), ((units, width), LOW), ((16, rows), F32)]
    out, grad, wg1, wg2, light = pl.pallas_call(
        functools.partial(layer_kernel, bits),
        name="layer",
        out_shape=[jax.ShapeDtypeStruct(shape, kind) for shape, kind in outs],
        in_specs=[any_] * 8 + [vmem] * 6 + [pl.BlockSpec(memory_space=pltpu.SMEM)],
        out_specs=[any_] * 4 + [vmem],
        scratch_shapes=[pltpu.VMEM(shape, kind) for shape, kind in scratch]
        + [pltpu.SemaphoreType.DMA((128,)), pltpu.SemaphoreType.DMA((128,)), pltpu.SemaphoreType.DMA((64,))],
        compiler_params=pltpu.CompilerParams(
            collective_id=1, has_side_effects=True, vmem_limit_bytes=VMEM_LIMIT
        ),
    )(
        layer_input, cotangent, weight_in, weight_out, jnp.asarray(small), jnp.asarray(forward),
        jnp.asarray(backward), jnp.asarray(order), *(v.reshape(1, -1) for v in vectors), live,
    )
    out = out.astype(F32) * live[:, None, None]
    return (
        out, grad, light[3], light[4], wg1.astype(F32), light[8 : 8 + HOLD].reshape(units), wg2.astype(F32),
        light[2], light[0], light[1],
    )


def solution(mesh):
    return jax.shard_map(
        functools.partial(local, mesh.shape["batch"]),
        mesh=mesh,
        in_specs=(
            P(None, "hidden", "batch"),
            P("hidden"),
            P("hidden"),
            P(None, "hidden"),
            P("hidden"),
            P("hidden", None),
            P("hidden"),
            P("hidden"),
            P("hidden"),
            P(None, "hidden", "batch"),
            P("batch"),
        ),
        out_specs=(
            P(None, "hidden", "batch"),
            P(None, "hidden", "batch"),
            P("hidden"),
            P("hidden"),
            P(None, "hidden"),
            P("hidden"),
            P("hidden", None),
            P("hidden"),
            P("hidden"),
            P("hidden"),
        ),
        check_vma=False,
    )
```

```python
import functools
import math

import jax
import jax.numpy as jnp
import ml_dtypes
import numpy as np
from jax import lax
from jax.experimental import pallas as pl
from jax.experimental.pallas import tpu as pltpu
from jax.sharding import PartitionSpec as P

SPLIT = 4
HOLD = 4
EPS = 1e-06
FINE = 64
LOW = jnp.bfloat16
F32 = jnp.float32
MESH = pl.DeviceIdType.MESH
VMEM_LIMIT = 63 * 2**20


def dot(left, right):
    return jnp.dot(left, right, preferred_element_type=F32)


def dot_rows(left, right):
    return lax.dot_general(left, right, (((1,), (1,)), ((), ())), preferred_element_type=F32)


@functools.cache
def sequence_tables(length, split):
    column = np.arange(length)
    coarse = 2 * np.pi * ((FINE * np.arange(length // FINE)[:, None] * column) % length) / length
    fine = 2 * np.pi * ((np.arange(FINE)[:, None] * column) % length) / length
    factor = 1 / math.sqrt(length)
    whole = np.stack([np.cos(coarse), np.sin(coarse), factor * np.cos(fine), factor * np.sin(fine)])
    return np.ascontiguousarray(
        whole.reshape(4, FINE, split, length // split).transpose(2, 0, 1, 3).astype(np.float32)
    )


@functools.cache
def feature_tables(width, parts):
    index = np.arange(width)
    angle = 2 * np.pi * ((index[:, None] * index) % width) / width
    factor = 1 / math.sqrt(width)
    cos = (np.cos(angle) * factor).astype(np.float32).astype(ml_dtypes.bfloat16)
    sin = (np.sin(angle) * factor).astype(np.float32).astype(ml_dtypes.bfloat16)
    part = width // parts
    pad = part + 16
    forward = np.zeros((parts, parts, part, 2 * part), ml_dtypes.bfloat16)
    backward = np.zeros((parts, pad, width), ml_dtypes.bfloat16)
    order = np.zeros((parts, part, pad), ml_dtypes.bfloat16)
    for h in range(parts):
        chip = slice((h // 2) * 2 * part, (h // 2 + 1) * 2 * part)
        forward[h] = (cos if h % 2 == 0 else -sin)[:, chip].reshape(parts, part, 2 * part)
        first = (h // 2) * part
        backward[h, : part + 1] = (cos, sin)[h % 2][first : first + part + 1]
        for i in range(part):
            order[h, i, i if h in (0, 3) else part - i] = 1
    return forward, backward, order


class Place:
    def __init__(self, bits):
        h = lax.axis_index("hidden")
        b = lax.axis_index("batch")
        self.h, self.b = h, b
        self.c = lax.rem(h, 2)
        self.x = lax.div(h, 2)
        self.hc = h + 1 - 2 * self.c
        self.hx = lax.rem(h + 2, 4)
        self.hd = lax.rem(self.hc + 2, 4)
        self.p = lax.rem(b, 4)
        self.bit = [lax.rem(lax.div(b, 2**k), 2) for k in range(bits)]
        self.py = self.p + 1 - 2 * self.bit[0]
        self.pz = lax.rem(self.p + 2, 4)
        self.pd = lax.rem(self.py + 2, 4)
        self.core = {"hidden": self.hc}
        self.side = {"hidden": self.hx}
        self.cross = {"hidden": self.hd}
        self.flip = [{"batch": b + 2**k - 2 ** (k + 1) * self.bit[k]} for k in range(bits)]
        self.ydev, self.zdev = self.flip[:2]


class Links:
    def __init__(self, send, recv, near):
        self.send, self.recv, self.near = send, recv, near
        self.used, self.fetched, self.open = 0, 0, []

    def describe(self, src, dst, device):
        i = self.used
        self.used += 1
        return pltpu.make_async_remote_copy(
            src_ref=src,
            dst_ref=dst,
            send_sem=self.send.at[i],
            recv_sem=self.recv.at[i],
            device_id=device,
            device_id_type=MESH,
        )

    def copy(self, src, dst, device):
        made = self.describe(src, dst, device)
        made.start()
        self.open.append(made)
        return made

    def settle(self, some):
        for made in some:
            made.wait_send()
            self.drop(made)

    def drop(self, made):
        self.open = [other for other in self.open if other is not made]

    def fetch(self, src, dst):
        made = pltpu.make_async_copy(src, dst, self.near.at[self.fetched])
        self.fetched += 1
        made.start()
        return made


def greet(devices):
    barrier = pltpu.get_barrier_semaphore()
    for device in devices:
        pl.semaphore_signal(barrier, inc=1, device_id=device, device_id_type=MESH)
    pl.semaphore_wait(barrier, len(devices))


class GatherHidden:
    def __init__(self, me, links, view):
        self.me, self.links, self.view = me, links, view

    def start(self):
        own = self.view(self.me.h)
        self.by_side = self.links.copy(own, own, self.me.side)
        self.by_core = self.links.copy(own, own, self.me.core)

    def forward(self):
        self.by_side.wait_recv()
        far = self.view(self.me.hx)
        self.by_far = self.links.copy(far, far, self.me.core)


class GatherBatch:
    def __init__(self, me, links, view):
        self.me, self.links, self.view = me, links, view

    def start(self):
        ends = ((0, self.me.ydev), (1, self.me.zdev), (1, self.me.ydev), (0, self.me.zdev))
        own = [self.view(self.me.p, 0), self.view(self.me.p, 1)]
        self.y0, self.z1, self.y1, self.z0 = (self.links.copy(own[n], own[n], device) for n, device in ends)

    def forward(self):
        self.y0.wait_recv()
        part = self.view(self.me.py, 0)
        self.on_z = self.links.copy(part, part, self.me.zdev)
        self.z1.wait_recv()
        part = self.view(self.me.pz, 1)
        self.on_y = self.links.copy(part, part, self.me.ydev)

    def arrive(self):
        self.y1.wait_recv()
        self.z0.wait_recv()

    def finish(self):
        self.on_z.wait_recv()
        self.on_y.wait_recv()

    def sent(self):
        return [self.y0, self.y1, self.z0, self.z1, self.on_y, self.on_z]


class Scatter:
    def __init__(self, me, links, rows, sc, rc, sx, rx, acc):
        self.me, self.links, self.rows, self.sent = me, links, rows, []
        self.sc, self.rc, self.sx, self.rx, self.acc = sc, rc, sx, rx, acc

    def run(self, prepare, block, hook):
        x, c, cut = self.me.x, self.me.c, pl.ds(0, self.rows)
        for n, start in enumerate((2 * (1 - x), 2 * x)):
            away, home = start + 1 - c, start + c

            def send(i, value):
                self.sc[n, i, cut] = value.astype(LOW)

            def keep(i, value):
                value = value + self.rc[n, i, cut].astype(F32)
                if n == 0:
                    self.sx[i] = value.astype(LOW)
                else:
                    self.acc[i, cut] = value

            prepare(0, away)
            block(0, away, send)
            by_core = self.links.copy(self.sc.at[n, :, cut], self.rc.at[n, :, cut], self.me.core)
            self.sent.append(by_core)
            prepare(1, home)
            by_core.wait_recv()
            block(1, home, keep)
            if n == 0:
                self.by_side = self.links.copy(self.sx, self.rx, self.me.side)
                self.sent.append(self.by_side)
                hook()

    def wait(self):
        self.by_side.wait_recv()

    def value(self, i):
        return self.acc[i, 0 : self.rows] + self.rx[i].astype(F32)


class Share:
    def __init__(self, me, links, rows, sc, rc, acc):
        self.me, self.links, self.cut = me, links, pl.ds(0, rows)
        self.sc, self.rc, self.acc = sc, rc, acc

    def away(self, block):
        def sink(i, value):
            self.sc[i, self.cut] = value.astype(LOW)

        block(1 - self.me.c, sink)
        self.by_core = self.links.copy(self.sc.at[:, self.cut], self.rc.at[:, self.cut], self.me.core)

    def home(self, block):
        def sink(i, value):
            self.acc[i, self.cut] = value

        block(self.me.c, sink)

    def wait(self):
        self.by_core.wait_recv()

    def value(self, i):
        return self.acc[i, self.cut] + self.rc[i, self.cut].astype(F32)


class Reduce:
    def __init__(self, me, links, order, given, given_landing, total, low, landing, whole):
        self.me, self.links, self.order = me, links, order
        self.given, self.given_landing = given, given_landing
        self.total, self.low, self.landing, self.whole = total, low, landing, whole
        self.blocks = total.shape[1] // whole.shape[2]
        bits, size = len(me.bit), total.shape[0]
        kinds = {"x": self.cross, "y": self.halve, "z": self.quarter}
        self.plan = [(kinds[axis], 0) for axis in order]
        more = extra_halvings(size, bits)
        self.plan += [(self.halve, k) for k in range(3, 3 + more)]
        self.plan += [(self.double, k) for k in range(3 + more, bits)]
        back = [(self.gather_half, k) for k in reversed(range(3, 3 + more))]
        back += [({"y": self.gather_half, "z": self.gather_quarters}[axis], 0) for axis in reversed(order) if axis != "x"]
        self.plan += back
        self.first_back = len(self.plan) - len(back)
        self.doubled = bits > 3 + more
        self.at, self.used, self.spans, self.crossed, self.after = 0, 0, [(0, size)], False, None

    def span(self, first, size):
        return pl.ds(pl.multiple_of(first, 16), size)

    def end(self):
        if self.after is not None:
            self.after()
            self.after = None

    def step(self):
        self.end()
        if self.at == len(self.plan):
            return False
        if self.at == self.first_back:
            mine, wide = self.span(*self.spans[-1]), self.whole.shape[2]
            own = self.low if self.doubled else self.total
            for n in range(self.blocks):
                self.whole[n, mine, :] = own[mine, n * wide : (n + 1) * wide].astype(LOW)
        kind, k = self.plan[self.at]
        self.at += 1
        kind(k)
        return True

    def land(self, size):
        self.used += size
        return pl.ds(self.used - size, size)

    def add(self, made, mine, place):
        made.wait_recv()
        self.add_rows(mine, self.landing, place.start)

    def add_rows(self, mine, landing, start):
        def some(at, i, step):
            self.total[pl.ds(at, step), :] += landing[pl.ds(start + i, step), :].astype(F32)

        by_rows(mine.start, mine.size, some)

    def send(self, first, size, device):
        give, place = self.span(first, size), self.land(size)

        def some(at, i, step):
            self.low[pl.ds(at, step), :] = self.total[pl.ds(at, step), :].astype(LOW)

        by_rows(first, size, some)
        return self.links.copy(self.low.at[give], self.landing.at[place], device), place

    def cross(self, _):
        first, size = self.spans[-1]
        mine, place = self.span(first, size), pl.ds(self.given.shape[0] - size, size)
        made = self.links.copy(self.given.at[mine], self.given_landing.at[place], self.me.side)
        self.crossed = True

        def after():
            made.wait_recv()
            self.add_rows(mine, self.given_landing, place.start)

        self.after = after

    def halve(self, k):
        first, size = self.spans[-1]
        half, u = size // 2, self.me.bit[k]
        keep, away = first + u * half, first + (1 - u) * half
        mine = self.span(keep, half)
        self.spans.append((keep, half))
        far = None
        if not self.crossed:
            far = self.links.copy(self.given.at[self.span(away, half)], self.given_landing.at[pl.ds(0, half)], self.me.flip[k])
        made, place = self.send(away, half, self.me.flip[k])

        def after():
            if far is not None:
                far.wait_recv()

                def some(at, i, step):
                    rows = pl.ds(at, step)
                    total = self.given[rows, :].astype(F32) + self.given_landing[pl.ds(i, step), :].astype(F32)
                    self.given[rows, :] = total.astype(LOW)

                by_rows(keep, half, some)
            self.add(made, mine, place)

        self.after = after

    def column(self, d):
        v = self.me.bit[1] + 2 * self.me.bit[2]
        w = lax.rem(v + d, 4)
        return w, {"batch": self.me.b + 2 * (w - v)}

    def quarter(self, _):
        first, size = self.spans[-1]
        part = size // 4
        keep = first + (self.me.bit[1] + 2 * self.me.bit[2]) * part
        self.spans.append((keep, part))
        made = []
        for d in (2, 1, 3):
            w, device = self.column(d)
            made.append(self.send(first + w * part, part, device))

        def after():
            for one, place in made:
                self.add(one, self.span(keep, part), place)

        self.after = after

    def double(self, k):
        mine = self.span(*self.spans[-1])
        place = self.land(self.spans[-1][1])
        if self.plan[self.at - 2][0] != self.double:
            self.low[mine, :] = self.total[mine, :].astype(LOW)
        made = self.links.copy(self.low.at[mine], self.landing.at[place], self.me.flip[k])

        def after():
            made.wait_recv()
            self.links.settle([made])
            self.low[mine, :] = (self.low[mine, :].astype(F32) + self.landing[place, :].astype(F32)).astype(LOW)

        self.after = after

    def gather(self, devices):
        part = self.whole.at[pl.ds(0, self.blocks), self.span(*self.spans.pop())]
        made = [self.links.copy(part, part, device) for device in devices]

        def after():
            for one in made:
                one.wait_recv()

        self.after = after

    def gather_half(self, k):
        self.gather([self.me.flip[k]])

    def gather_quarters(self, _):
        self.gather([self.column(d)[1] for d in (2, 1, 3)])


def extra_halvings(size, bits):
    count, left = 0, size // 8
    while 3 + count < bits and (left // 2) % 16 == 0:
        count, left = count + 1, left // 2
    return count


def landing_rows(size, bits):
    more, left = extra_halvings(size, bits), size // 8
    return 7 * left + sum(left >> (k + 1) for k in range(more)) + (bits - 3 - more) * (left >> more)


def chunk_rows(units):
    third = units // 3
    return (third,) * 3, (third,) * 3


def columns(t, size):
    return pl.ds(pl.multiple_of(t * size, size), size)


def loop(count, body):
    def one(i, carry):
        body(i)
        return carry

    lax.fori_loop(0, count, one, 0)


def by_rows(first, size, body):
    step = min(size, 32)

    def one(i):
        body(pl.multiple_of(first + i * step, 16), pl.multiple_of(i * step, 16), step)

    loop(size // step, one)


ROOT = math.sqrt(2 / math.pi)
CUBE = 0.044715


def gelu_both(v):
    square = v * v
    t = jnp.tanh(v * (ROOT + ROOT * CUBE * square))
    half = 0.5 + 0.5 * t
    slope = half + (0.5 * v) * (1 - t * t) * (ROOT + 3 * ROOT * CUBE * square)
    return v * half, slope


def up(value):
    return jnp.sum(value, 0, keepdims=True)


SCHEDULE = (
    ("keep", 0), ("give", 0), ("chunk", 1), ("chunk", 0), ("back", 0), ("norm", 0), ("back", 1), ("chunk", 1),
    ("give", 1), ("chunk", 4), ("chunk", 3), ("near", 0), ("far", 0), ("halves", 0), ("chunk", 0), ("chunk", 2),
    ("chunk", 1), ("keep", 1), ("chunk", 4), ("chunk", 3), ("chunk", 5), ("chunk", 1), ("norm", 1), ("pack", 0),
    ("chunk", 0), ("chunk", 2), ("chunk", 3), ("chunk", 0), ("ends", 0), ("near", 1), ("chunk", 4), ("far", 1),
    ("chunk", 1), ("chunk", 3), ("chunk", 2), ("chunk", 5), ("chunk", 5), ("chunk", 4), ("sequence", 0), ("order", 0),
    ("small", 0), ("chunk", 3), ("round", 0), ("chunk", 2), ("grad", 0), ("ends", 1), ("halves", 1), ("chunk", 0),
    ("chunk", 5), ("chunk", 4), ("chunk", 2), ("sequence", 1), ("order", 1), ("chunk", 5), ("chunk", 1), ("round", 0),
    ("chunk", 4), ("grad", 1), ("chunk", 3), ("chunk", 2), ("chunk", 0), ("chunk", 5),
)
ORDERS = ("yxz", "yxz", "yxz", "xyz", "xzy", "yxz")


def layer_kernel(
    bits,
    x_hbm, cot_hbm, w1_hbm, w2_hbm, small_hbm, ht_hbm, gt_hbm, order_hbm,
    g1_ref, s1_ref, bo_ref, g2_ref, s2_ref, bin_ref, live_ref,
    out_hbm, grad_hbm, wg1_hbm, wg2_hbm, light_ref, bias_ref,
    tab, small, ht, gt, order, xg, cs, ct, og, ab, sc, rc, sx, rx, acc, yf, hf, df, zf, u1, gr2, inv1, lanes,
    wr, wt, wg, given, landing, ug, rowv, rows_in, pn, lsend, lrecv, lbias, ltot, lnext, send, recv, near,
):
    slots, _, piece = x_hbm.shape
    parts, rows, tokens = cs.shape[1:]
    width = parts * rows
    units = wg.shape[1]
    pad = gt.shape[0]
    me = Place(bits)
    links = Links(send, recv, near)
    is_cos = me.c == 0

    def fetch_tokens(src, dst, s):
        return [links.fetch(src.at[s, :, pl.ds(t * tokens, tokens)], dst.at[s, t]) for t in range(parts)]

    x_in = [fetch_tokens(x_hbm, u1, s) for s in range(slots)]
    w1_in, w2_in = links.fetch(w1_hbm, wg.at[0]), links.fetch(w2_hbm, wg.at[1])
    small_in = links.fetch(small_hbm.at[me.p], small)
    cot_in = [fetch_tokens(cot_hbm, gr2, s) for s in range(slots)]
    ht_in = links.fetch(ht_hbm.at[me.h], ht)
    gt_in = links.fetch(gt_hbm.at[me.h], gt)
    order_in = links.fetch(order_hbm.at[me.h], order)
    greet([me.core, me.side, me.cross] + me.flip)

    def input_view(s):
        def view(q, half=None):
            return xg.at[s, q, slice(None) if half is None else pl.ds(half * 2, 2), me.c]

        return view

    spread = [GatherBatch(me, links, input_view(s)) for s in range(slots)]
    over = [[] for _ in range(slots)]

    def hand_over(s, q):
        block = input_view(s)(q)
        over[s].append(links.copy(block, block, me.core))

    for s in range(slots):
        for t in range(parts):
            x_in[s][t].wait()
            xg[s, me.p, t, me.c] = u1[s, t].astype(LOW)
        if s == 0:
            spread[0].start()
        hand_over(s, me.p)

    far = 1 - me.x
    quarter, straight = units // SPLIT, width - 128

    def weight_view(q, half=None):
        at = pl.ds(pl.multiple_of(q * quarter, 16), quarter)
        return wr.at[slice(None) if half is None else pl.ds(half, 1), far, at, pl.ds(0, straight)]

    weights = GatherBatch(me, links, weight_view)
    w1_in.wait()
    w2_in.wait()

    def own_weights(r, carry):
        at = columns(r, 256)
        for n in range(units // 256):
            cut = slice(n * 256, (n + 1) * 256)
            first, second = wg[0, at, cut], wg[1, at, cut]
            wt[0, me.x, at, cut] = first.astype(LOW)
            wr[0, me.x, cut, at] = first.T.astype(LOW)
            wr[1, me.x, at, cut] = second.astype(LOW)
            wt[1, me.x, cut, at] = second.T.astype(LOW)
        return carry

    lax.fori_loop(0, units // 256, own_weights, 0)
    quarter_at = pl.ds(pl.multiple_of(me.p * quarter, 16), quarter)
    mine_w = wr.at[:, me.x, quarter_at, pl.ds(0, straight)]
    by_side = links.copy(mine_w, mine_w, me.side)
    mine_w = wr.at[:, me.x, :, pl.ds(straight, 128)]
    direct = links.copy(mine_w, mine_w, me.side)

    vectors = (g1_ref, s1_ref, bo_ref, g2_ref, s2_ref)
    rowv[...] = jnp.zeros_like(rowv)
    for k, ref in enumerate(vectors):
        rowv[k : k + 1, 0:rows] = ref[...]
    for i in range(parts):
        rowv[5 + i : 6 + i, 0:rows] = bin_ref[:, i * rows : (i + 1) * rows]
    params = [links.copy(rowv, rows_in.at[me.h], device) for device in (me.core, me.side, me.cross)]

    small_in.wait()

    def make_rows(i, carry):
        big_cos, big_sin = small[0, pl.ds(i, 1), :], small[1, pl.ds(i, 1), :]
        by_cos = jnp.where(is_cos, big_cos, big_sin)
        by_sin = jnp.where(is_cos, -big_sin, big_cos)
        at = pl.ds(pl.multiple_of(i * FINE, FINE), FINE)
        for n in range(piece // 256):
            cut = slice(n * 256, (n + 1) * 256)
            tab[at, cut] = (by_cos[:, cut] * small[2, :, cut] + by_sin[:, cut] * small[3, :, cut]).astype(LOW)
        return carry

    lax.fori_loop(0, FINE, make_rows, 0)
    spread[0].forward()
    spread[1].start()
    for s in range(slots):
        for t in range(parts):
            cot_in[s][t].wait()
            cs[s, t] = (gr2[s, t] * live_ref[s]).astype(LOW)
        ct[s, me.h] = cs[s, me.h]
    ht_in.wait()

    sums = [
        Scatter(me, links, rows, sc.at[s], rc.at[s], sx.at[s], rx.at[s], acc.at[s]) for s in range(slots)
    ]

    def prepare(s, j, t):
        at = columns(t, tokens)
        total = None
        for q in range(SPLIT):
            for n in range(parts):
                first = q * piece + n * tokens
                share = dot(xg[s, q, n].reshape(2 * rows, tokens), tab[first : first + tokens, at])
                total = share if total is None else total + share
        ab[j] = total.astype(LOW)

    def transform(s, j, t, sink):
        def one(i):
            own = jnp.where(me.h == i, 1.0, 0.0).astype(F32)
            sink(i, dot(ht[i], ab[j]) + own * u1[s, t])

        loop(parts, one)

    moved = []

    def next_input():
        spread[1].forward()
        by_side.wait_recv()
        weights.start()

    def next_weights():
        weights.forward()

    for s, hook in enumerate((next_input, next_weights)):
        spread[s].arrive()
        hand_over(s, me.py)
        hand_over(s, me.pz)
        spread[s].finish()
        hand_over(s, me.pd)
        for made in over[s]:
            made.wait_recv()
        sums[s].run(functools.partial(prepare, s), functools.partial(transform, s), hook)
        for to, device in ((me.hc, me.core), (me.hx, me.side), (me.hd, me.cross)):
            moved.append(links.copy(cs.at[s, to], ct.at[s, me.h], device))
        links.settle(over[s] + spread[s].sent())
    for made in params:
        made.wait_recv()
    rows_in[me.h] = rowv[...]
    square = jnp.zeros((128 - rowv.shape[0], rowv.shape[1]), F32)
    for i in range(parts):
        pn[i] = jnp.concatenate([rows_in[i], square], 0).T[0:rows, :]

    def param(k, i):
        return pn[i, :, k : k + 1]

    def folded(value):
        return value[:, :128] + value[:, 128:]

    def lane_sum(k, i, s, value):
        lanes[k, i] = folded(value) if s == 0 else lanes[k, i] + folded(value)

    def row_sums(body):
        sums_of = [[up(value) for value in body(i)] for i in range(parts)]
        return [functools.reduce(jnp.add, values) for values in zip(*sums_of)]

    def each(body):
        for i in range(parts):
            body(i)

    def mean_and_inverse(total, squares):
        mean = total / width
        return mean, lax.rsqrt(squares / width - mean * mean + EPS)

    def part_rows(i):
        return pl.ds(i * rows, rows)

    def norm_first(s):
        whole = sums[s].acc

        def resid(i):
            v = sums[s].value(i)
            whole[i, 0:rows] = v
            return v, v * v

        mean, inverse = mean_and_inverse(*row_sums(resid))
        inv1[s] = inverse

        def one(i):
            u = (whole[i, 0:rows] - mean) * inverse
            u1[s, i] = u
            yf[s, me.c, part_rows(i), :] = (u * param(0, i) + param(1, i)).astype(LOW)

        each(one)

    def forward_in(s, k, unit):
        def one(i):
            at = part_rows(i)
            h, slope = gelu_both(dot(wr[0, unit, at, :], yf[s, k]) + pn[2 * unit + me.c, :, 5 + i : 6 + i])
            hf[s, 2 * k + unit, at, :] = h.astype(LOW)
            df[s, 2 * k + unit, at, :] = slope.astype(LOW)

        each(one)

    def forward_out(s, k, sink):
        def one(i):
            at = part_rows(i)
            sink(i, dot(wt[1, 0, at, :], hf[s, 2 * k]) + dot(wt[1, 1, at, :], hf[s, 2 * k + 1]))

        each(one)

    def norm_second(s, shared):
        whole = shared.acc

        def resid(i):
            v = u1[s, i] * param(0, i) + param(1, i) + shared.value(i) + param(2, i)
            whole[i, 0:rows] = v
            return v, v * v

        mean, inverse = mean_and_inverse(*row_sums(resid))

        def unit(i):
            u = (whole[i, 0:rows] - mean) * inverse
            whole[i, 0:rows] = u
            cs[s, i] = (u * param(3, i) + param(4, i)).astype(LOW)
            g = ct[s, i].astype(F32)
            lane_sum(0, i, s, g * u)
            lane_sum(1, i, s, g)
            q = g * param(3, i)
            return q, q * u

        total, cross = row_sums(unit)
        total, cross = total / width, cross / width

        def one(i):
            q = ct[s, i].astype(F32) * param(3, i)
            grad = inverse * (q - total - whole[i, 0:rows] * cross)
            gr2[s, i] = grad
            lane_sum(2, i, s, grad)
            zf[s, me.c, part_rows(i), :] = grad.astype(LOW)

        each(one)

    def backward_in(s, k, fresh):
        for unit in range(2):

            def one(i):
                at = part_rows(i)
                gp = dot(wr[1, unit, at, :], zf[s, k]) * df[s, 2 * k + unit, at, :].astype(F32)
                place = 5 + unit
                lanes[place, i] = folded(gp) if fresh else lanes[place, i] + folded(gp)
                df[s, 2 * k + unit, at, :] = gp.astype(LOW)

            each(one)

    def backward_out(s, k, sink):
        def one(i):
            at = part_rows(i)
            sink(i, dot(wt[0, 0, at, :], df[s, 2 * k]) + dot(wt[0, 1, at, :], df[s, 2 * k + 1]))

        each(one)

    def weight_grad(which, unit, store):
        def one(r, carry):
            at = columns(r, 256)
            for n in range(units // 256):
                cut = slice(n * 256, (n + 1) * 256)
                total = 0.0
                for s in range(slots):
                    for k in range(2):
                        if which == 0:
                            total = total + dot_rows(hf[s, 2 * k + unit, at, :], zf[s, k, cut, :])
                        else:
                            total = total + dot_rows(yf[s, k, at, :], df[s, 2 * k + unit, cut, :])
                store(which, at, cut, total)
            return carry

        lax.fori_loop(0, units // 256, one, 0)

    def norm_first_back(s, shared):
        whole = shared.acc

        def entry(i):
            grad = gr2[s, i] + shared.value(i)
            whole[i, 0:rows] = grad
            u = u1[s, i]
            lane_sum(3, i, s, grad * u)
            lane_sum(4, i, s, grad)
            q = grad * param(0, i)
            return q, q * u

        total, cross = row_sums(entry)
        total, cross = total / width, cross / width

        def one(i):
            q = whole[i, 0:rows] * param(0, i)
            xg[s, me.h, i, 0] = (inv1[s] * (q - total - u1[s, i] * cross)).astype(LOW)

        each(one)

    def to_core(block):
        return links.copy(block, block, me.core)

    outward = [Share(me, links, rows, sc.at[s, 0], rc.at[s, 0], acc.at[s]) for s in range(slots)]
    inward = [Share(me, links, rows, sc.at[s, 1], rc.at[s, 1], acc.at[s]) for s in range(slots)]

    def enter(s):
        sums[s].wait()
        norm_first(s)
        got = to_core(yf.at[s, me.c])
        forward_in(s, me.c, me.x)
        got.wait_recv()
        forward_in(s, 1 - me.c, me.x)

    def leave(s):
        links.settle(sums[s].sent)
        forward_in(s, 1 - me.c, far)
        forward_in(s, me.c, far)
        outward[s].away(functools.partial(forward_out, s))
        outward[s].home(functools.partial(forward_out, s))

    def far_weights(r, carry):
        at = columns(r, 256)
        for n in range(units // 256):
            cut = slice(n * 256, (n + 1) * 256)
            wt[0, far, cut, at] = wr[0, far, at, cut].astype(F32).T.astype(LOW)
            wt[1, far, cut, at] = wr[1, far, at, cut].astype(F32).T.astype(LOW)
        return carry

    enter(0)
    weights.arrive()
    weights.finish()
    direct.wait_recv()
    lax.fori_loop(0, units // 256, far_weights, 0)
    links.settle([by_side, direct] + weights.sent())
    leave(0)
    enter(1)
    leave(1)
    for made in moved:
        made.wait_recv()
    links.settle(moved)
    seconds, outs = [], {}
    for s in range(slots):
        outward[s].wait()
        norm_second(s, outward[s])
        seconds.append(to_core(zf.at[s, me.c]))
        og[s, me.h] = cs[s, me.h]
        outs[s] = [
            links.copy(cs.at[s, to], og.at[s, me.h], device)
            for to, device in ((me.hc, me.core), (me.hx, me.side), (me.hd, me.cross))
        ]

    def mix_view(s):
        return lambda t: xg.at[s, t, :, 0]

    def freq_view(s):
        cuts = (pl.ds(0, pad // 32 * 16), pl.ds(pad // 32 * 16, pad - pad // 32 * 16))

        def view(q, half=None):
            return ug.at[s, q] if half is None else ug.at[s, q, cuts[half]]

        return view

    gathers = [GatherHidden(me, links, mix_view(s)) for s in range(slots)]
    spreads = [GatherBatch(me, links, freq_view(s)) for s in range(slots)]
    heavy, chunks = [], []
    for which, whole in ((0, hf), (1, df)):
        low, used = 0, 0
        for size in chunk_rows(units)[which]:
            at, place = pl.ds(low, size), pl.ds(used, landing_rows(size, bits))
            low, used = low + size, used + landing_rows(size, bits)
            chunks.append((which, at))
            heavy.append(
                Reduce(
                    me, links, ORDERS[len(heavy)], wr.at[0, which, at], given.at[which, at], wg.at[which, at], wt.at[1, which, at],
                    landing.at[which, place], whole.at[0, :, at],
                )
            )

    def features(s, t):
        whole = jnp.concatenate([xg[s, t, i, 0] for i in range(parts)], 0)
        ug[s, me.p, :, columns(t, tokens)] = dot(gt[...], whole).astype(LOW)

    def store_given(which, at, cut, value):
        wr[0, which, at, cut] = value.astype(LOW)

    def store_kept(which, at, cut, value):
        wg[which, at, cut] = value

    for made in seconds:
        made.wait_recv()

    def backward(s):
        backward_in(s, me.c, s == 0)
        backward_in(s, 1 - me.c, False)
        inward[s].away(functools.partial(backward_out, s))
        inward[s].home(functools.partial(backward_out, s))

    def first_back(s):
        inward[s].wait()
        norm_first_back(s, inward[s])
        gathers[s].start()

    def near_features(s):
        features(s, me.h)
        gathers[s].by_core.wait_recv()
        features(s, me.hc)

    def far_features(s):
        gathers[s].forward()
        features(s, me.hx)
        gathers[s].by_far.wait_recv()
        features(s, me.hd)
        spreads[s].start()

    ones = jnp.ones((8, 128), F32)

    def lane_total(k, i):
        return lax.dot_general(
            ones, lanes[k, i], (((1,), (1,)), ((), ())), precision=lax.Precision.HIGHEST, preferred_element_type=F32
        )

    row = lax.broadcasted_iota(jnp.int32, (8, rows), 0)
    light = []

    def start_small_sums():
        for i in range(parts):
            packed = jnp.zeros((8, rows), F32)
            for k in range(5):
                packed = jnp.where(row == k, lane_total(k, i), packed)
            lsend[i] = packed
        for unit in range(2):
            packed = jnp.zeros((8, rows), F32)
            for i in range(parts):
                packed = jnp.where(row == i, lane_total(5 + unit, i), packed)
            lbias[unit] = packed
        for to, device in ((me.hc, me.core), (me.hx, me.side), (me.hd, me.cross)):
            light.append(links.copy(lsend.at[to], lrecv.at[me.h], device))
        light.append(links.copy(lbias.at[far], lbias.at[2], me.side))

    sign = jnp.where((me.h == 0) | (me.h == 3), -1.0, 1.0).astype(F32)
    mine = jnp.where(is_cos, 1.0, sign)
    theirs = jnp.where(is_cos, sign, 1.0)
    stored = []

    def sequence(s):
        spreads[s].arrive()
        spreads[s].finish()
        links.settle([outward[s].by_core])

        def one(t):
            at = columns(t, tokens)
            total = None
            for q in range(SPLIT):
                share = dot(ug[s, q], tab[q * piece : (q + 1) * piece, at])
                total = share if total is None else total + share
            acc[s, t] = total
            sc[s, 0, t] = total.astype(LOW)

        loop(parts, one)
        swaps[s] = links.copy(sc.at[s, 0], rc.at[s, 0], me.core)

    swaps, across = {}, {}

    def ordered(s):
        swaps[s].wait_recv()

        def one(t):
            pair = (mine * acc[s, t] + theirs * rc[s, 0, t].astype(F32)).astype(LOW)
            sx[s, t] = dot(order[...], pair).astype(LOW)

        loop(parts, one)
        made = links.describe(sx.at[s], rx.at[s], me.side)
        across[s] = made

        @pl.when(jnp.logical_not(is_cos))
        def _():
            made.start()

    def store_grad(s):
        def store(part):
            def one(t):
                u1[s, t] = part[s, t].astype(F32) + xg[s, t, me.h, 0].astype(F32)

            loop(parts, one)

        @pl.when(is_cos)
        def _():
            store(sx)

        @pl.when(jnp.logical_not(is_cos))
        def _():
            across[s].wait()
            store(rx)

        for t in range(parts):
            stored.append(links.fetch(u1.at[s, t], grad_hbm.at[s, :, pl.ds(t * tokens, tokens)]))

    def end_outs(s):
        for made in outs[s]:
            made.wait_recv()
        for t in range(parts):
            gr2[s, t] = og[s, t].astype(F32) * live_ref[s]
            stored.append(links.fetch(gr2.at[s, t], out_hbm.at[s, :, pl.ds(t * tokens, tokens)]))

    def small_sums():
        for made in light:
            made.wait_recv()
        ltot[0, 0:8] = lsend[me.h] + lrecv[me.hc] + lrecv[me.hx] + lrecv[me.hd]
        ltot[0, 8:16] = lbias[me.x] + lbias[2]
        small_round()

    rounds = []

    def small_round():
        k = len(rounds)
        if k:
            rounds[k - 1].wait_recv()
            ltot[k] = ltot[k - 1] + lnext[k - 1]
        if k < bits:
            rounds.append(links.copy(ltot.at[k], lnext.at[k], me.flip[k]))

    def store_chunk(n):
        which, at = chunks[n]
        dst = (wg2_hbm, wg1_hbm)[which].at[at]
        for m in range(heavy[n].blocks):
            stored.append(links.fetch(heavy[n].whole.at[m], dst.at[:, pl.ds(m * tokens, tokens)]))

    def step(n):
        if not heavy[n].step():
            store_chunk(n)
            return False
        return True

    acts = {
        "back": backward,
        "norm": first_back,
        "near": near_features,
        "far": far_features,
        "halves": lambda s: spreads[s].forward(),
        "sequence": sequence,
        "order": ordered,
        "grad": store_grad,
        "give": lambda which: weight_grad(which, far, store_given),
        "keep": lambda which: weight_grad(which, me.x, store_kept),
        "pack": lambda _: start_small_sums(),
        "small": lambda _: small_sums(),
        "round": lambda _: small_round(),
        "ends": end_outs,
        "chunk": lambda n: step(n),
    }
    going = [True] * len(heavy)
    gt_in.wait()
    order_in.wait()
    for kind, n in SCHEDULE:
        did = acts[kind](n)
        if kind == "chunk":
            going[n] = did
    while any(going):
        for n in range(len(heavy)):
            going[n] = going[n] and step(n)
        if len(rounds) < bits:
            small_round()
    while len(rounds) < bits:
        small_round()
    k = bits - 1
    if len(rounds) == bits:
        rounds[k].wait_recv()
        ltot[bits] = ltot[k] + lnext[k]
    light_ref[...] = ltot[bits, 0:8]
    for i in range(parts):
        bias_ref[:, i * rows : (i + 1) * rows] = ltot[bits, 8 + i : 9 + i]
    for made in stored:
        made.wait()
    for made in list(links.open):
        made.wait_send()


def local(
    n_batch,
    layer_input,
    gain_first,
    shift_first,
    weight_in,
    bias_in,
    weight_out,
    bias_out,
    gain_second,
    shift_second,
    cotangent,
    live_counts,
):
    slots, rows, piece = layer_input.shape
    width = rows * HOLD
    tokens = piece // HOLD
    units = weight_in.shape[1]
    length = piece * SPLIT
    pad = rows + 16
    bits = n_batch.bit_length() - 1
    live = (jnp.arange(slots) < live_counts[0]).astype(F32)
    vectors = (gain_first, shift_first, bias_out, gain_second, shift_second, bias_in)
    small = sequence_tables(length, SPLIT)
    forward, backward, order = feature_tables(width, HOLD)
    any_, vmem = pl.BlockSpec(memory_space=pl.ANY), pl.BlockSpec(memory_space=pltpu.VMEM)
    block = (HOLD, rows, tokens)
    padded = (HOLD, pad, tokens)
    shard = (slots,) + block
    landing = max(sum(landing_rows(size, bits) for size in sizes) for sizes in chunk_rows(units))
    scratch = [
        ((length, piece), LOW), ((4, FINE, piece), F32), (forward.shape[1:], LOW), (backward.shape[1:], LOW),
        (order.shape[1:], LOW), ((slots, SPLIT, HOLD, 2, rows, tokens), LOW), (shard, LOW), (shard, LOW), (shard, LOW),
        ((2, 2 * rows, tokens), LOW), ((slots, 2) + padded, LOW), ((slots, 2) + padded, LOW), (shard, LOW), (shard, LOW),
        ((slots,) + padded, F32), ((slots, 2, width, tokens), LOW), ((slots, 4, units, tokens), LOW),
        ((slots, 4, units, tokens), LOW), ((slots, 2, width, tokens), LOW), (shard, F32), (shard, F32),
        ((slots, 1, tokens), F32), ((7, HOLD, rows, 128), F32),
        ((2, 2, units, width), LOW), ((2, 2, width, units), LOW), ((2, units, width), F32),
        ((2, units, width), LOW), ((2, landing, width), LOW),
        ((slots, SPLIT, pad, piece), LOW), ((16, 256), F32), ((HOLD, 16, 256), F32), ((HOLD, rows, 128), F32), ((HOLD, 8, rows), F32),
        ((HOLD, 8, rows), F32), ((3, 8, rows), F32), ((bits + 1, 16, rows), F32), ((bits, 16, rows), F32),
    ]
    outs = [
        (layer_input.shape, F32), (layer_input.shape, F32), ((width, units), LOW), ((units, width), LOW),
        ((8, rows), F32), ((1, units), F32),
    ]
    out, grad, wg1, wg2, light, bias = pl.pallas_call(
        functools.partial(layer_kernel, bits),
        name="layer",
        out_shape=[jax.ShapeDtypeStruct(shape, kind) for shape, kind in outs],
        in_specs=[any_] * 8 + [vmem] * 6 + [pl.BlockSpec(memory_space=pltpu.SMEM)],
        out_specs=[any_] * 4 + [vmem] * 2,
        scratch_shapes=[pltpu.VMEM(shape, kind) for shape, kind in scratch]
        + [pltpu.SemaphoreType.DMA((192,)), pltpu.SemaphoreType.DMA((192,)), pltpu.SemaphoreType.DMA((96,))],
        compiler_params=pltpu.CompilerParams(
            collective_id=1, has_side_effects=True, vmem_limit_bytes=VMEM_LIMIT
        ),
    )(
        layer_input, cotangent, weight_in, weight_out, jnp.asarray(small), jnp.asarray(forward),
        jnp.asarray(backward), jnp.asarray(order), *(v.reshape(1, -1) for v in vectors), live,
    )
    return (
        out, grad, light[3], light[4], wg1.astype(F32), bias.reshape(units), wg2.astype(F32),
        light[2], light[0], light[1],
    )


def solution(mesh):
    return jax.shard_map(
        functools.partial(local, mesh.shape["batch"]),
        mesh=mesh,
        in_specs=(
            P(None, "hidden", "batch"),
            P("hidden"),
            P("hidden"),
            P(None, "hidden"),
            P("hidden"),
            P("hidden", None),
            P("hidden"),
            P("hidden"),
            P("hidden"),
            P(None, "hidden", "batch"),
            P("batch"),
        ),
        out_specs=(
            P(None, "hidden", "batch"),
            P(None, "hidden", "batch"),
            P("hidden"),
            P("hidden"),
            P(None, "hidden"),
            P("hidden"),
            P("hidden", None),
            P("hidden"),
            P("hidden"),
            P("hidden"),
        ),
        check_vma=False,
    )
```

```python
import functools
import math

import jax
import jax.numpy as jnp
import ml_dtypes
import numpy as np
from jax import lax
from jax.experimental import pallas as pl
from jax.experimental.pallas import tpu as pltpu
from jax.sharding import PartitionSpec as P

SPLIT = 4
HOLD = 4
EPS = 1e-06
FINE = 64
LOW = jnp.bfloat16
F32 = jnp.float32
MESH = pl.DeviceIdType.MESH
VMEM_LIMIT = 63 * 2**20


def dot(left, right):
    return jnp.dot(left, right, preferred_element_type=F32)


def dot_rows(left, right):
    return lax.dot_general(left, right, (((1,), (1,)), ((), ())), preferred_element_type=F32)


@functools.cache
def sequence_tables(length, split):
    column = np.arange(length)
    coarse = 2 * np.pi * ((FINE * np.arange(length // FINE)[:, None] * column) % length) / length
    fine = 2 * np.pi * ((np.arange(FINE)[:, None] * column) % length) / length
    factor = 1 / math.sqrt(length)
    whole = np.stack([np.cos(coarse), np.sin(coarse), factor * np.cos(fine), factor * np.sin(fine)])
    return np.ascontiguousarray(
        whole.reshape(4, FINE, split, length // split).transpose(2, 0, 1, 3).astype(np.float32)
    )


@functools.cache
def feature_tables(width, parts):
    index = np.arange(width)
    angle = 2 * np.pi * ((index[:, None] * index) % width) / width
    factor = 1 / math.sqrt(width)
    cos = (np.cos(angle) * factor).astype(np.float32).astype(ml_dtypes.bfloat16)
    sin = (np.sin(angle) * factor).astype(np.float32).astype(ml_dtypes.bfloat16)
    part = width // parts
    pad = part + 16
    forward = np.zeros((parts, parts, part, 2 * part), ml_dtypes.bfloat16)
    backward = np.zeros((parts, pad, width), ml_dtypes.bfloat16)
    order = np.zeros((parts, part, pad), ml_dtypes.bfloat16)
    for h in range(parts):
        chip = slice((h // 2) * 2 * part, (h // 2 + 1) * 2 * part)
        forward[h] = (cos if h % 2 == 0 else -sin)[:, chip].reshape(parts, part, 2 * part)
        first = (h // 2) * part
        backward[h, : part + 1] = (cos, sin)[h % 2][first : first + part + 1]
        for i in range(part):
            order[h, i, i if h in (0, 3) else part - i] = 1
    return forward, backward, order


class Place:
    def __init__(self, bits):
        h = lax.axis_index("hidden")
        b = lax.axis_index("batch")
        self.h, self.b = h, b
        self.c = lax.rem(h, 2)
        self.x = lax.div(h, 2)
        self.hc = h + 1 - 2 * self.c
        self.hx = lax.rem(h + 2, 4)
        self.hd = lax.rem(self.hc + 2, 4)
        self.p = lax.rem(b, 4)
        self.bit = [lax.rem(lax.div(b, 2**k), 2) for k in range(bits)]
        self.py = self.p + 1 - 2 * self.bit[0]
        self.pz = lax.rem(self.p + 2, 4)
        self.pd = lax.rem(self.py + 2, 4)
        self.core = {"hidden": self.hc}
        self.side = {"hidden": self.hx}
        self.cross = {"hidden": self.hd}
        self.flip = [{"batch": b + 2**k - 2 ** (k + 1) * self.bit[k]} for k in range(bits)]
        self.ydev, self.zdev = self.flip[:2]


class Links:
    def __init__(self, send, recv, near):
        self.send, self.recv, self.near = send, recv, near
        self.used, self.fetched, self.open = 0, 0, []

    def describe(self, src, dst, device):
        i = self.used
        self.used += 1
        return pltpu.make_async_remote_copy(
            src_ref=src,
            dst_ref=dst,
            send_sem=self.send.at[i],
            recv_sem=self.recv.at[i],
            device_id=device,
            device_id_type=MESH,
        )

    def copy(self, src, dst, device):
        made = self.describe(src, dst, device)
        made.start()
        self.open.append(made)
        return made

    def settle(self, some):
        for made in some:
            made.wait_send()
            self.drop(made)

    def drop(self, made):
        self.open = [other for other in self.open if other is not made]

    def fetch(self, src, dst):
        made = pltpu.make_async_copy(src, dst, self.near.at[self.fetched])
        self.fetched += 1
        made.start()
        return made


def greet(devices):
    barrier = pltpu.get_barrier_semaphore()
    for device in devices:
        pl.semaphore_signal(barrier, inc=1, device_id=device, device_id_type=MESH)
    pl.semaphore_wait(barrier, len(devices))


class GatherHidden:
    def __init__(self, me, links, view):
        self.me, self.links, self.view = me, links, view

    def start(self):
        own = self.view(self.me.h)
        self.by_side = self.links.copy(own, own, self.me.side)
        self.by_core = self.links.copy(own, own, self.me.core)

    def forward(self):
        self.by_side.wait_recv()
        far = self.view(self.me.hx)
        self.by_far = self.links.copy(far, far, self.me.core)


class GatherBatch:
    def __init__(self, me, links, view):
        self.me, self.links, self.view = me, links, view

    def start(self):
        ends = ((0, self.me.ydev), (1, self.me.zdev), (1, self.me.ydev), (0, self.me.zdev))
        own = [self.view(self.me.p, 0), self.view(self.me.p, 1)]
        self.y0, self.z1, self.y1, self.z0 = (self.links.copy(own[n], own[n], device) for n, device in ends)

    def forward(self):
        self.y0.wait_recv()
        part = self.view(self.me.py, 0)
        self.on_z = self.links.copy(part, part, self.me.zdev)
        self.z1.wait_recv()
        part = self.view(self.me.pz, 1)
        self.on_y = self.links.copy(part, part, self.me.ydev)

    def arrive(self):
        self.y1.wait_recv()
        self.z0.wait_recv()

    def finish(self):
        self.on_z.wait_recv()
        self.on_y.wait_recv()

    def sent(self):
        return [self.y0, self.y1, self.z0, self.z1, self.on_y, self.on_z]


class Scatter:
    def __init__(self, me, links, rows, sc, rc, sx, rx, acc):
        self.me, self.links, self.rows, self.sent = me, links, rows, []
        self.sc, self.rc, self.sx, self.rx, self.acc = sc, rc, sx, rx, acc

    def run(self, prepare, block, hook):
        x, c, cut = self.me.x, self.me.c, pl.ds(0, self.rows)
        for n, start in enumerate((2 * (1 - x), 2 * x)):
            away, home = start + 1 - c, start + c

            def send(i, value):
                self.sc[n, i, cut] = value.astype(LOW)

            def keep(i, value):
                value = value + self.rc[n, i, cut].astype(F32)
                if n == 0:
                    self.sx[i] = value.astype(LOW)
                else:
                    self.acc[i, cut] = value

            prepare(0, away)
            block(0, away, send)
            by_core = self.links.copy(self.sc.at[n, :, cut], self.rc.at[n, :, cut], self.me.core)
            self.sent.append(by_core)
            prepare(1, home)
            by_core.wait_recv()
            block(1, home, keep)
            if n == 0:
                self.by_side = self.links.copy(self.sx, self.rx, self.me.side)
                self.sent.append(self.by_side)
                hook()

    def wait(self):
        self.by_side.wait_recv()

    def value(self, i):
        return self.acc[i, 0 : self.rows] + self.rx[i].astype(F32)


class Share:
    def __init__(self, me, links, rows, sc, rc, acc):
        self.me, self.links, self.cut = me, links, pl.ds(0, rows)
        self.sc, self.rc, self.acc = sc, rc, acc

    def away(self, block):
        def sink(i, value):
            self.sc[i, self.cut] = value.astype(LOW)

        block(1 - self.me.c, sink)
        self.by_core = self.links.copy(self.sc.at[:, self.cut], self.rc.at[:, self.cut], self.me.core)

    def home(self, block):
        def sink(i, value):
            self.acc[i, self.cut] = value

        block(self.me.c, sink)

    def wait(self):
        self.by_core.wait_recv()

    def value(self, i):
        return self.acc[i, self.cut] + self.rc[i, self.cut].astype(F32)


class Reduce:
    def __init__(self, me, links, order, given, given_landing, total, low, landing, whole):
        self.me, self.links, self.order = me, links, order
        self.given, self.given_landing = given, given_landing
        self.total, self.low, self.landing, self.whole = total, low, landing, whole
        self.blocks = total.shape[1] // whole.shape[2]
        bits, size = len(me.bit), total.shape[0]
        kinds = {"x": self.cross, "y": self.halve, "z": self.quarter}
        self.plan = [(kinds[axis], 0) for axis in order]
        more = extra_halvings(size, bits)
        self.plan += [(self.halve, k) for k in range(3, 3 + more)]
        self.plan += [(self.double, k) for k in range(3 + more, bits)]
        back = [(self.gather_half, k) for k in reversed(range(3, 3 + more))]
        back += [({"y": self.gather_half, "z": self.gather_quarters}[axis], 0) for axis in reversed(order) if axis != "x"]
        self.plan += back
        self.first_back = len(self.plan) - len(back)
        self.doubled = bits > 3 + more
        self.at, self.used, self.spans, self.crossed, self.after = 0, 0, [(0, size)], False, None

    def span(self, first, size):
        return pl.ds(pl.multiple_of(first, 16), size)

    def end(self):
        if self.after is not None:
            self.after()
            self.after = None

    def step(self):
        self.end()
        if self.at == len(self.plan):
            return False
        if self.at == self.first_back:
            mine, wide = self.span(*self.spans[-1]), self.whole.shape[2]
            own = self.low if self.doubled else self.total
            for n in range(self.blocks):
                self.whole[n, mine, :] = own[mine, n * wide : (n + 1) * wide].astype(LOW)
        kind, k = self.plan[self.at]
        self.at += 1
        kind(k)
        return True

    def land(self, size):
        self.used += size
        return pl.ds(self.used - size, size)

    def add(self, made, mine, place):
        made.wait_recv()
        self.add_rows(mine, self.landing, place.start)

    def add_rows(self, mine, landing, start):
        def some(at, i, step):
            self.total[pl.ds(at, step), :] += landing[pl.ds(start + i, step), :].astype(F32)

        by_rows(mine.start, mine.size, some)

    def send(self, first, size, device):
        give, place = self.span(first, size), self.land(size)

        def some(at, i, step):
            self.low[pl.ds(at, step), :] = self.total[pl.ds(at, step), :].astype(LOW)

        by_rows(first, size, some)
        return self.links.copy(self.low.at[give], self.landing.at[place], device), place

    def cross(self, _):
        first, size = self.spans[-1]
        mine, place = self.span(first, size), pl.ds(self.given.shape[0] - size, size)
        made = self.links.copy(self.given.at[mine], self.given_landing.at[place], self.me.side)
        self.crossed = True

        def after():
            made.wait_recv()
            self.add_rows(mine, self.given_landing, place.start)

        self.after = after

    def halve(self, k):
        first, size = self.spans[-1]
        half, u = size // 2, self.me.bit[k]
        keep, away = first + u * half, first + (1 - u) * half
        mine = self.span(keep, half)
        self.spans.append((keep, half))
        far = None
        if not self.crossed:
            far = self.links.copy(self.given.at[self.span(away, half)], self.given_landing.at[pl.ds(0, half)], self.me.flip[k])
        made, place = self.send(away, half, self.me.flip[k])

        def after():
            if far is not None:
                far.wait_recv()

                def some(at, i, step):
                    rows = pl.ds(at, step)
                    total = self.given[rows, :].astype(F32) + self.given_landing[pl.ds(i, step), :].astype(F32)
                    self.given[rows, :] = total.astype(LOW)

                by_rows(keep, half, some)
            self.add(made, mine, place)

        self.after = after

    def column(self, d):
        v = self.me.bit[1] + 2 * self.me.bit[2]
        w = lax.rem(v + d, 4)
        return w, {"batch": self.me.b + 2 * (w - v)}

    def quarter(self, _):
        first, size = self.spans[-1]
        part = size // 4
        keep = first + (self.me.bit[1] + 2 * self.me.bit[2]) * part
        self.spans.append((keep, part))
        made = []
        for d in (2, 1, 3):
            w, device = self.column(d)
            made.append(self.send(first + w * part, part, device))

        def after():
            for one, place in made:
                self.add(one, self.span(keep, part), place)

        self.after = after

    def double(self, k):
        mine = self.span(*self.spans[-1])
        place = self.land(self.spans[-1][1])
        if self.plan[self.at - 2][0] != self.double:
            self.low[mine, :] = self.total[mine, :].astype(LOW)
        made = self.links.copy(self.low.at[mine], self.landing.at[place], self.me.flip[k])

        def after():
            made.wait_recv()
            self.links.settle([made])
            self.low[mine, :] = (self.low[mine, :].astype(F32) + self.landing[place, :].astype(F32)).astype(LOW)

        self.after = after

    def gather(self, devices):
        part = self.whole.at[pl.ds(0, self.blocks), self.span(*self.spans.pop())]
        made = [self.links.copy(part, part, device) for device in devices]

        def after():
            for one in made:
                one.wait_recv()

        self.after = after

    def gather_half(self, k):
        self.gather([self.me.flip[k]])

    def gather_quarters(self, _):
        self.gather([self.column(d)[1] for d in (2, 1, 3)])


def extra_halvings(size, bits):
    count, left = 0, size // 8
    while 3 + count < bits and (left // 2) % 16 == 0:
        count, left = count + 1, left // 2
    return count


def landing_rows(size, bits):
    more, left = extra_halvings(size, bits), size // 8
    return 7 * left + sum(left >> (k + 1) for k in range(more)) + (bits - 3 - more) * (left >> more)


def chunk_rows(units):
    third = units // 3
    return (third,) * 3, (third,) * 3


def columns(t, size):
    return pl.ds(pl.multiple_of(t * size, size), size)


def loop(count, body):
    def one(i, carry):
        body(i)
        return carry

    lax.fori_loop(0, count, one, 0)


def by_rows(first, size, body):
    step = min(size, 32)

    def one(i):
        body(pl.multiple_of(first + i * step, 16), pl.multiple_of(i * step, 16), step)

    loop(size // step, one)


ROOT = math.sqrt(2 / math.pi)
CUBE = 0.044715


def gelu_both(v):
    square = v * v
    t = jnp.tanh(v * (ROOT + ROOT * CUBE * square))
    half = 0.5 + 0.5 * t
    slope = half + (0.5 * v) * (1 - t * t) * (ROOT + 3 * ROOT * CUBE * square)
    return v * half, slope


def up(value):
    return jnp.sum(value, 0, keepdims=True)


SCHEDULE = (
    ("give", 0), ("chunk", 1), ("keep", 0), ("chunk", 2), ("back", 0), ("back", 1), ("norm", 0), ("give", 1),
    ("keep", 1), ("chunk", 5), ("chunk", 3), ("chunk", 2), ("chunk", 1), ("near", 0), ("far", 0), ("halves", 0),
    ("chunk", 3), ("chunk", 5), ("norm", 1), ("chunk", 4), ("chunk", 2), ("pack", 0), ("chunk", 5), ("chunk", 2),
    ("near", 1), ("chunk", 0), ("chunk", 3), ("chunk", 5), ("far", 1), ("chunk", 4), ("outs", 1), ("chunk", 0),
    ("chunk", 3), ("small", 0), ("outs", 0), ("sequence", 0), ("order", 0), ("chunk", 2), ("chunk", 4), ("chunk", 1),
    ("ends", 1), ("chunk", 0), ("halves", 1), ("chunk", 5), ("chunk", 4), ("chunk", 1), ("chunk", 3), ("chunk", 0),
    ("chunk", 2), ("chunk", 5), ("round", 0), ("chunk", 1), ("ends", 0), ("chunk", 4), ("sequence", 1), ("order", 1),
    ("chunk", 0), ("grad", 0), ("round", 0), ("chunk", 4), ("chunk", 3), ("grad", 1), ("chunk", 0), ("chunk", 1),
)
ORDERS = ("xyz", "xzy", "yxz", "xyz", "yxz", "yxz")


def layer_kernel(
    bits,
    x_hbm, cot_hbm, w1_hbm, w2_hbm, small_hbm, ht_hbm, gt_hbm, order_hbm,
    g1_ref, s1_ref, bo_ref, g2_ref, s2_ref, bin_ref, live_ref,
    out_hbm, grad_hbm, wg1_hbm, wg2_hbm, light_ref, bias_ref,
    tab, small, ht, gt, order, xg, cs, ct, og, ab, sc, rc, sx, rx, acc, yf, hf, df, zf, u1, gr2, inv1, lanes,
    wr, wt, wg, given, landing, ug, rowv, rows_in, pn, lsend, lrecv, lbias, ltot, lnext, send, recv, near,
):
    slots, _, piece = x_hbm.shape
    parts, rows, tokens = cs.shape[1:]
    width = parts * rows
    units = wg.shape[1]
    pad = gt.shape[0]
    me = Place(bits)
    links = Links(send, recv, near)
    is_cos = me.c == 0
    live = [jnp.where(live_ref[0] > s, 1.0, 0.0).astype(F32) for s in range(slots)]

    def fetch_tokens(src, dst, s):
        return [links.fetch(src.at[s, :, pl.ds(t * tokens, tokens)], dst.at[s, t]) for t in range(parts)]

    x_in = [fetch_tokens(x_hbm, u1, s) for s in range(slots)]
    w1_in, w2_in = links.fetch(w1_hbm, wg.at[0]), links.fetch(w2_hbm, wg.at[1])
    small_in = links.fetch(small_hbm.at[me.p], small)
    cot_in = [fetch_tokens(cot_hbm, gr2, s) for s in range(slots)]
    ht_in = links.fetch(ht_hbm.at[me.h], ht)
    gt_in = links.fetch(gt_hbm.at[me.h], gt)
    order_in = links.fetch(order_hbm.at[me.h], order)
    greet([me.core, me.side, me.cross] + me.flip)

    def input_view(s):
        def view(q, half=None):
            return xg.at[s, q, slice(None) if half is None else pl.ds(half * 2, 2), me.c]

        return view

    spread = [GatherBatch(me, links, input_view(s)) for s in range(slots)]
    over = [[] for _ in range(slots)]

    def hand_over(s, q):
        block = input_view(s)(q)
        over[s].append(links.copy(block, block, me.core))

    for s in range(slots):
        for t in range(parts):
            x_in[s][t].wait()
            xg[s, me.p, t, me.c] = u1[s, t].astype(LOW)
        if s == 0:
            spread[0].start()
        hand_over(s, me.p)

    far = 1 - me.x
    quarter, straight = units // SPLIT, width - 128

    def weight_view(q, half=None):
        at = pl.ds(pl.multiple_of(q * quarter, 16), quarter)
        return wr.at[slice(None) if half is None else pl.ds(half, 1), far, at, pl.ds(0, straight)]

    weights = GatherBatch(me, links, weight_view)
    w1_in.wait()
    w2_in.wait()

    def own_weights(r, carry):
        at = columns(r, 256)
        for n in range(units // 256):
            cut = slice(n * 256, (n + 1) * 256)
            first, second = wg[0, at, cut], wg[1, at, cut]
            wt[0, me.x, at, cut] = first.astype(LOW)
            wr[0, me.x, cut, at] = first.T.astype(LOW)
            wr[1, me.x, at, cut] = second.astype(LOW)
            wt[1, me.x, cut, at] = second.T.astype(LOW)
        return carry

    lax.fori_loop(0, units // 256, own_weights, 0)
    quarter_at = pl.ds(pl.multiple_of(me.p * quarter, 16), quarter)
    mine_w = wr.at[:, me.x, quarter_at, pl.ds(0, straight)]
    by_side = links.copy(mine_w, mine_w, me.side)
    mine_w = wr.at[:, me.x, :, pl.ds(straight, 128)]
    direct = links.copy(mine_w, mine_w, me.side)

    vectors = (g1_ref, s1_ref, bo_ref, g2_ref, s2_ref)
    rowv[...] = jnp.zeros_like(rowv)
    for k, ref in enumerate(vectors):
        rowv[k : k + 1, 0:rows] = ref[...]
    for i in range(parts):
        rowv[5 + i : 6 + i, 0:rows] = bin_ref[:, i * rows : (i + 1) * rows]
    params = [links.copy(rowv, rows_in.at[me.h], device) for device in (me.core, me.side, me.cross)]

    small_in.wait()

    def make_rows(i, carry):
        big_cos, big_sin = small[0, pl.ds(i, 1), :], small[1, pl.ds(i, 1), :]
        by_cos = jnp.where(is_cos, big_cos, big_sin)
        by_sin = jnp.where(is_cos, -big_sin, big_cos)
        at = pl.ds(pl.multiple_of(i * FINE, FINE), FINE)
        for n in range(piece // 256):
            cut = slice(n * 256, (n + 1) * 256)
            tab[at, cut] = (by_cos[:, cut] * small[2, :, cut] + by_sin[:, cut] * small[3, :, cut]).astype(LOW)
        return carry

    lax.fori_loop(0, FINE, make_rows, 0)
    spread[0].forward()
    spread[1].start()
    for s in range(slots):
        for t in range(parts):
            cot_in[s][t].wait()
            cs[s, t] = (gr2[s, t] * live[s]).astype(LOW)
        ct[s, me.h] = cs[s, me.h]
    ht_in.wait()

    sums = [
        Scatter(me, links, rows, sc.at[s], rc.at[s], sx.at[s], rx.at[s], acc.at[s]) for s in range(slots)
    ]

    def prepare(s, j, t):
        at = columns(t, tokens)
        total = None
        for q in range(SPLIT):
            for n in range(parts):
                first = q * piece + n * tokens
                share = dot(xg[s, q, n].reshape(2 * rows, tokens), tab[first : first + tokens, at])
                total = share if total is None else total + share
        ab[j] = total.astype(LOW)

    def transform(s, j, t, sink):
        def one(i):
            own = jnp.where(me.h == i, 1.0, 0.0).astype(F32)
            sink(i, dot(ht[i], ab[j]) + own * u1[s, t])

        loop(parts, one)

    moved = []

    def next_input():
        spread[1].forward()
        by_side.wait_recv()
        weights.start()

    def next_weights():
        weights.forward()

    for s, hook in enumerate((next_input, next_weights)):
        spread[s].arrive()
        hand_over(s, me.py)
        hand_over(s, me.pz)
        spread[s].finish()
        hand_over(s, me.pd)
        for made in over[s]:
            made.wait_recv()
        sums[s].run(functools.partial(prepare, s), functools.partial(transform, s), hook)
        for to, device in ((me.hc, me.core), (me.hx, me.side), (me.hd, me.cross)):
            moved.append(links.copy(cs.at[s, to], ct.at[s, me.h], device))
        links.settle(over[s] + spread[s].sent())
    for made in params:
        made.wait_recv()
    rows_in[me.h] = rowv[...]
    square = jnp.zeros((128 - rowv.shape[0], rowv.shape[1]), F32)
    for i in range(parts):
        pn[i] = jnp.concatenate([rows_in[i], square], 0).T[0:rows, :]

    def param(k, i):
        return pn[i, :, k : k + 1]

    def folded(value):
        return value[:, :128] + value[:, 128:]

    def lane_sum(k, i, s, value):
        lanes[k, i] = folded(value) if s == 0 else lanes[k, i] + folded(value)

    def row_sums(body):
        sums_of = [[up(value) for value in body(i)] for i in range(parts)]
        return [functools.reduce(jnp.add, values) for values in zip(*sums_of)]

    def each(body):
        for i in range(parts):
            body(i)

    def mean_and_inverse(total, squares):
        mean = total / width
        return mean, lax.rsqrt(squares / width - mean * mean + EPS)

    def part_rows(i):
        return pl.ds(i * rows, rows)

    def norm_first(s):
        whole = sums[s].acc

        def resid(i):
            v = sums[s].value(i)
            whole[i, 0:rows] = v
            return v, v * v

        mean, inverse = mean_and_inverse(*row_sums(resid))
        inv1[s] = inverse

        def one(i):
            u = (whole[i, 0:rows] - mean) * inverse
            u1[s, i] = u
            yf[s, me.c, part_rows(i), :] = (u * param(0, i) + param(1, i)).astype(LOW)

        each(one)

    def forward_in(s, k, unit):
        def one(i):
            at = part_rows(i)
            h, slope = gelu_both(dot(wr[0, unit, at, :], yf[s, k]) + pn[2 * unit + me.c, :, 5 + i : 6 + i])
            hf[s, 2 * k + unit, at, :] = h.astype(LOW)
            df[s, 2 * k + unit, at, :] = slope.astype(LOW)

        each(one)

    def forward_out(s, k, sink):
        def one(i):
            at = part_rows(i)
            sink(i, dot(wt[1, 0, at, :], hf[s, 2 * k]) + dot(wt[1, 1, at, :], hf[s, 2 * k + 1]))

        each(one)

    def norm_second(s, shared):
        whole = shared.acc

        def resid(i):
            v = u1[s, i] * param(0, i) + param(1, i) + shared.value(i) + param(2, i)
            whole[i, 0:rows] = v
            return v, v * v

        mean, inverse = mean_and_inverse(*row_sums(resid))

        def unit(i):
            u = (whole[i, 0:rows] - mean) * inverse
            whole[i, 0:rows] = u
            cs[s, i] = (u * param(3, i) + param(4, i)).astype(LOW)
            g = ct[s, i].astype(F32)
            lane_sum(0, i, s, g * u)
            lane_sum(1, i, s, g)
            q = g * param(3, i)
            return q, q * u

        total, cross = row_sums(unit)
        total, cross = total / width, cross / width

        def one(i):
            q = ct[s, i].astype(F32) * param(3, i)
            grad = inverse * (q - total - whole[i, 0:rows] * cross)
            gr2[s, i] = grad
            lane_sum(2, i, s, grad)
            zf[s, me.c, part_rows(i), :] = grad.astype(LOW)

        each(one)

    def backward_in(s, k, fresh):
        for unit in range(2):

            def one(i):
                at = part_rows(i)
                gp = dot(wr[1, unit, at, :], zf[s, k]) * df[s, 2 * k + unit, at, :].astype(F32)
                place = 5 + unit
                lanes[place, i] = folded(gp) if fresh else lanes[place, i] + folded(gp)
                df[s, 2 * k + unit, at, :] = gp.astype(LOW)

            each(one)

    def backward_out(s, k, sink):
        def one(i):
            at = part_rows(i)
            sink(i, dot(wt[0, 0, at, :], df[s, 2 * k]) + dot(wt[0, 1, at, :], df[s, 2 * k + 1]))

        each(one)

    def weight_grad(which, unit, store):
        def one(r, carry):
            at = columns(r, 256)
            for n in range(units // 256):
                cut = slice(n * 256, (n + 1) * 256)
                total = 0.0
                for s in range(slots):
                    for k in range(2):
                        if which == 0:
                            total = total + dot_rows(hf[s, 2 * k + unit, at, :], zf[s, k, cut, :])
                        else:
                            total = total + dot_rows(yf[s, k, at, :], df[s, 2 * k + unit, cut, :])
                store(which, at, cut, total)
            return carry

        lax.fori_loop(0, units // 256, one, 0)

    def norm_first_back(s, shared):
        whole = shared.acc

        def entry(i):
            grad = gr2[s, i] + shared.value(i)
            whole[i, 0:rows] = grad
            u = u1[s, i]
            lane_sum(3, i, s, grad * u)
            lane_sum(4, i, s, grad)
            q = grad * param(0, i)
            return q, q * u

        total, cross = row_sums(entry)
        total, cross = total / width, cross / width

        def one(i):
            q = whole[i, 0:rows] * param(0, i)
            xg[s, me.h, i, 0] = (inv1[s] * (q - total - u1[s, i] * cross)).astype(LOW)

        each(one)

    def to_core(block):
        return links.copy(block, block, me.core)

    outward = [Share(me, links, rows, sc.at[s, 0], rc.at[s, 0], acc.at[s]) for s in range(slots)]
    inward = [Share(me, links, rows, sc.at[s, 1], rc.at[s, 1], acc.at[s]) for s in range(slots)]

    def enter(s):
        sums[s].wait()
        norm_first(s)
        got = to_core(yf.at[s, me.c])
        forward_in(s, me.c, me.x)
        got.wait_recv()
        forward_in(s, 1 - me.c, me.x)

    def leave(s):
        links.settle(sums[s].sent)
        forward_in(s, 1 - me.c, far)
        forward_in(s, me.c, far)
        outward[s].away(functools.partial(forward_out, s))
        outward[s].home(functools.partial(forward_out, s))

    def far_weights(r, carry):
        at = columns(r, 256)
        for n in range(units // 256):
            cut = slice(n * 256, (n + 1) * 256)
            wt[0, far, cut, at] = wr[0, far, at, cut].astype(F32).T.astype(LOW)
            wt[1, far, cut, at] = wr[1, far, at, cut].astype(F32).T.astype(LOW)
        return carry

    enter(0)
    weights.arrive()
    weights.finish()
    direct.wait_recv()
    lax.fori_loop(0, units // 256, far_weights, 0)
    links.settle([by_side, direct] + weights.sent())
    leave(0)
    enter(1)
    leave(1)
    for made in moved:
        made.wait_recv()
    links.settle(moved)
    seconds, outs = [], {}
    for s in range(slots):
        outward[s].wait()
        norm_second(s, outward[s])
        seconds.append(to_core(zf.at[s, me.c]))

    def mix_view(s):
        return lambda t: xg.at[s, t, :, 0]

    def freq_view(s):
        cuts = (pl.ds(0, pad // 32 * 16), pl.ds(pad // 32 * 16, pad - pad // 32 * 16))

        def view(q, half=None):
            return ug.at[s, q] if half is None else ug.at[s, q, cuts[half]]

        return view

    gathers = [GatherHidden(me, links, mix_view(s)) for s in range(slots)]
    spreads = [GatherBatch(me, links, freq_view(s)) for s in range(slots)]
    heavy, chunks = [], []
    for which, whole in ((0, hf), (1, df)):
        low, used = 0, 0
        for size in chunk_rows(units)[which]:
            at, place = pl.ds(low, size), pl.ds(used, landing_rows(size, bits))
            low, used = low + size, used + landing_rows(size, bits)
            chunks.append((which, at))
            heavy.append(
                Reduce(
                    me, links, ORDERS[len(heavy)], wr.at[0, which, at], given.at[which, at], wg.at[which, at], wt.at[1, which, at],
                    landing.at[which, place], whole.at[0, :, at],
                )
            )

    def features(s, t):
        whole = jnp.concatenate([xg[s, t, i, 0] for i in range(parts)], 0)
        ug[s, me.p, :, columns(t, tokens)] = dot(gt[...], whole).astype(LOW)

    def store_given(which, at, cut, value):
        wr[0, which, at, cut] = value.astype(LOW)

    def store_kept(which, at, cut, value):
        wg[which, at, cut] = value

    for made in seconds:
        made.wait_recv()

    def backward(s):
        backward_in(s, me.c, s == 0)
        backward_in(s, 1 - me.c, False)
        inward[s].away(functools.partial(backward_out, s))
        inward[s].home(functools.partial(backward_out, s))

    def first_back(s):
        inward[s].wait()
        norm_first_back(s, inward[s])
        gathers[s].start()

    def near_features(s):
        features(s, me.h)
        gathers[s].by_core.wait_recv()
        features(s, me.hc)

    def far_features(s):
        gathers[s].forward()
        features(s, me.hx)
        gathers[s].by_far.wait_recv()
        features(s, me.hd)
        spreads[s].start()

    ones = jnp.ones((8, 128), F32)

    def lane_total(k, i):
        return lax.dot_general(
            ones, lanes[k, i], (((1,), (1,)), ((), ())), precision=lax.Precision.HIGHEST, preferred_element_type=F32
        )

    row = lax.broadcasted_iota(jnp.int32, (8, rows), 0)
    light = []

    def start_small_sums():
        for i in range(parts):
            packed = jnp.zeros((8, rows), F32)
            for k in range(5):
                packed = jnp.where(row == k, lane_total(k, i), packed)
            lsend[i] = packed
        for unit in range(2):
            packed = jnp.zeros((8, rows), F32)
            for i in range(parts):
                packed = jnp.where(row == i, lane_total(5 + unit, i), packed)
            lbias[unit] = packed
        for to, device in ((me.hc, me.core), (me.hx, me.side), (me.hd, me.cross)):
            light.append(links.copy(lsend.at[to], lrecv.at[me.h], device))
        light.append(links.copy(lbias.at[far], lbias.at[2], me.side))

    sign = jnp.where((me.h == 0) | (me.h == 3), -1.0, 1.0).astype(F32)
    mine = jnp.where(is_cos, 1.0, sign)
    theirs = jnp.where(is_cos, sign, 1.0)
    stored = []

    def sequence(s):
        spreads[s].arrive()
        spreads[s].finish()
        links.settle([outward[s].by_core])

        def one(t):
            at = columns(t, tokens)
            total = None
            for q in range(SPLIT):
                share = dot(ug[s, q], tab[q * piece : (q + 1) * piece, at])
                total = share if total is None else total + share
            acc[s, t] = total
            sc[s, 0, t] = total.astype(LOW)

        loop(parts, one)
        swaps[s] = links.copy(sc.at[s, 0], rc.at[s, 0], me.core)

    swaps, across = {}, {}

    def ordered(s):
        swaps[s].wait_recv()

        def one(t):
            pair = (mine * acc[s, t] + theirs * rc[s, 0, t].astype(F32)).astype(LOW)
            sx[s, t] = dot(order[...], pair).astype(LOW)

        loop(parts, one)
        made = links.describe(sx.at[s], rx.at[s], me.side)
        across[s] = made

        @pl.when(jnp.logical_not(is_cos))
        def _():
            made.start()

    def store_grad(s):
        def store(part):
            def one(t):
                u1[s, t] = part[s, t].astype(F32) + xg[s, t, me.h, 0].astype(F32)

            loop(parts, one)

        @pl.when(is_cos)
        def _():
            store(sx)

        @pl.when(jnp.logical_not(is_cos))
        def _():
            across[s].wait()
            store(rx)

        for t in range(parts):
            stored.append(links.fetch(u1.at[s, t], grad_hbm.at[s, :, pl.ds(t * tokens, tokens)]))

    def start_outs(s):
        og[s, me.h] = cs[s, me.h]
        outs[s] = [
            links.copy(cs.at[s, to], og.at[s, me.h], device)
            for to, device in ((me.hc, me.core), (me.hx, me.side), (me.hd, me.cross))
        ]

    def end_outs(s):
        for made in outs[s]:
            made.wait_recv()
        for t in range(parts):
            gr2[s, t] = og[s, t].astype(F32) * live[s]
            stored.append(links.fetch(gr2.at[s, t], out_hbm.at[s, :, pl.ds(t * tokens, tokens)]))

    def small_sums():
        for made in light:
            made.wait_recv()
        ltot[0, 0:8] = lsend[me.h] + lrecv[me.hc] + lrecv[me.hx] + lrecv[me.hd]
        ltot[0, 8:16] = lbias[me.x] + lbias[2]
        small_round()

    rounds = []

    def small_round():
        k = len(rounds)
        if k:
            rounds[k - 1].wait_recv()
            ltot[k] = ltot[k - 1] + lnext[k - 1]
        if k < bits:
            rounds.append(links.copy(ltot.at[k], lnext.at[k], me.flip[k]))

    def store_chunk(n):
        which, at = chunks[n]
        dst = (wg2_hbm, wg1_hbm)[which].at[at]
        for m in range(heavy[n].blocks):
            stored.append(links.fetch(heavy[n].whole.at[m], dst.at[:, pl.ds(m * tokens, tokens)]))

    def step(n):
        if not heavy[n].step():
            store_chunk(n)
            return False
        return True

    acts = {
        "back": backward,
        "norm": first_back,
        "near": near_features,
        "far": far_features,
        "halves": lambda s: spreads[s].forward(),
        "sequence": sequence,
        "order": ordered,
        "grad": store_grad,
        "give": lambda which: weight_grad(which, far, store_given),
        "keep": lambda which: weight_grad(which, me.x, store_kept),
        "pack": lambda _: start_small_sums(),
        "small": lambda _: small_sums(),
        "round": lambda _: small_round(),
        "outs": start_outs,
        "ends": end_outs,
        "chunk": lambda n: step(n),
    }
    going = [True] * len(heavy)
    gt_in.wait()
    order_in.wait()
    for kind, n in SCHEDULE:
        did = acts[kind](n)
        if kind == "chunk":
            going[n] = did
    while any(going):
        for n in range(len(heavy)):
            going[n] = going[n] and step(n)
        if len(rounds) < bits:
            small_round()
    while len(rounds) < bits:
        small_round()
    k = bits - 1
    if len(rounds) == bits:
        rounds[k].wait_recv()
        ltot[bits] = ltot[k] + lnext[k]
    light_ref[...] = ltot[bits, 0:8]
    for i in range(parts):
        bias_ref[:, i * rows : (i + 1) * rows] = ltot[bits, 8 + i : 9 + i]
    for made in stored:
        made.wait()
    for made in list(links.open):
        made.wait_send()


def local(
    n_batch,
    layer_input,
    gain_first,
    shift_first,
    weight_in,
    bias_in,
    weight_out,
    bias_out,
    gain_second,
    shift_second,
    cotangent,
    live_counts,
):
    slots, rows, piece = layer_input.shape
    width = rows * HOLD
    tokens = piece // HOLD
    units = weight_in.shape[1]
    length = piece * SPLIT
    pad = rows + 16
    bits = n_batch.bit_length() - 1
    vectors = (gain_first, shift_first, bias_out, gain_second, shift_second, bias_in)
    small = sequence_tables(length, SPLIT)
    forward, backward, order = feature_tables(width, HOLD)
    any_, vmem = pl.BlockSpec(memory_space=pl.ANY), pl.BlockSpec(memory_space=pltpu.VMEM)
    block = (HOLD, rows, tokens)
    padded = (HOLD, pad, tokens)
    shard = (slots,) + block
    landing = max(sum(landing_rows(size, bits) for size in sizes) for sizes in chunk_rows(units))
    scratch = [
        ((length, piece), LOW), ((4, FINE, piece), F32), (forward.shape[1:], LOW), (backward.shape[1:], LOW),
        (order.shape[1:], LOW), ((slots, SPLIT, HOLD, 2, rows, tokens), LOW), (shard, LOW), (shard, LOW), (shard, LOW),
        ((2, 2 * rows, tokens), LOW), ((slots, 2) + padded, LOW), ((slots, 2) + padded, LOW), (shard, LOW), (shard, LOW),
        ((slots,) + padded, F32), ((slots, 2, width, tokens), LOW), ((slots, 4, units, tokens), LOW),
        ((slots, 4, units, tokens), LOW), ((slots, 2, width, tokens), LOW), (shard, F32), (shard, F32),
        ((slots, 1, tokens), F32), ((7, HOLD, rows, 128), F32),
        ((2, 2, units, width), LOW), ((2, 2, width, units), LOW), ((2, units, width), F32),
        ((2, units, width), LOW), ((2, landing, width), LOW),
        ((slots, SPLIT, pad, piece), LOW), ((16, 256), F32), ((HOLD, 16, 256), F32), ((HOLD, rows, 128), F32), ((HOLD, 8, rows), F32),
        ((HOLD, 8, rows), F32), ((3, 8, rows), F32), ((bits + 1, 16, rows), F32), ((bits, 16, rows), F32),
    ]
    outs = [
        (layer_input.shape, F32), (layer_input.shape, F32), ((width, units), LOW), ((units, width), LOW),
        ((8, rows), F32), ((1, units), F32),
    ]
    out, grad, wg1, wg2, light, bias = pl.pallas_call(
        functools.partial(layer_kernel, bits),
        name="layer",
        out_shape=[jax.ShapeDtypeStruct(shape, kind) for shape, kind in outs],
        in_specs=[any_] * 8 + [vmem] * 6 + [pl.BlockSpec(memory_space=pltpu.SMEM)],
        out_specs=[any_] * 4 + [vmem] * 2,
        scratch_shapes=[pltpu.VMEM(shape, kind) for shape, kind in scratch]
        + [pltpu.SemaphoreType.DMA((192,)), pltpu.SemaphoreType.DMA((192,)), pltpu.SemaphoreType.DMA((96,))],
        compiler_params=pltpu.CompilerParams(
            collective_id=1, has_side_effects=True, vmem_limit_bytes=VMEM_LIMIT
        ),
    )(
        layer_input, cotangent, weight_in, weight_out, jnp.asarray(small), jnp.asarray(forward),
        jnp.asarray(backward), jnp.asarray(order), *(v.reshape(1, -1) for v in vectors), live_counts,
    )
    return (
        out, grad, light[3], light[4], wg1.astype(F32), bias.reshape(units), wg2.astype(F32),
        light[2], light[0], light[1],
    )


def solution(mesh):
    return jax.shard_map(
        functools.partial(local, mesh.shape["batch"]),
        mesh=mesh,
        in_specs=(
            P(None, "hidden", "batch"),
            P("hidden"),
            P("hidden"),
            P(None, "hidden"),
            P("hidden"),
            P("hidden", None),
            P("hidden"),
            P("hidden"),
            P("hidden"),
            P(None, "hidden", "batch"),
            P("batch"),
        ),
        out_specs=(
            P(None, "hidden", "batch"),
            P(None, "hidden", "batch"),
            P("hidden"),
            P("hidden"),
            P(None, "hidden"),
            P("hidden"),
            P("hidden", None),
            P("hidden"),
            P("hidden"),
            P("hidden"),
        ),
        check_vma=False,
    )
```

```python
import functools
import math

import jax
import jax.numpy as jnp
import ml_dtypes
import numpy as np
from jax import lax
from jax.experimental import pallas as pl
from jax.experimental.pallas import tpu as pltpu
from jax.sharding import PartitionSpec as P

SPLIT = 4
HOLD = 4
EPS = 1e-06
FINE = 64
LOW = jnp.bfloat16
F32 = jnp.float32
MESH = pl.DeviceIdType.MESH
VMEM_LIMIT = 63 * 2**20


def dot(left, right):
    return jnp.dot(left, right, preferred_element_type=F32)


def dot_rows(left, right):
    return lax.dot_general(left, right, (((1,), (1,)), ((), ())), preferred_element_type=F32)


@functools.cache
def sequence_tables(length, split):
    column = np.arange(length)
    coarse = 2 * np.pi * ((FINE * np.arange(length // FINE)[:, None] * column) % length) / length
    fine = 2 * np.pi * ((np.arange(FINE)[:, None] * column) % length) / length
    factor = 1 / math.sqrt(length)
    whole = np.stack([np.cos(coarse), np.sin(coarse), factor * np.cos(fine), factor * np.sin(fine)])
    return np.ascontiguousarray(
        whole.reshape(4, FINE, split, length // split).transpose(2, 0, 1, 3).astype(np.float32)
    )


@functools.cache
def feature_tables(width, parts):
    index = np.arange(width)
    angle = 2 * np.pi * ((index[:, None] * index) % width) / width
    factor = 1 / math.sqrt(width)
    cos = (np.cos(angle) * factor).astype(np.float32).astype(ml_dtypes.bfloat16)
    sin = (np.sin(angle) * factor).astype(np.float32).astype(ml_dtypes.bfloat16)
    part = width // parts
    pad = part + 16
    forward = np.zeros((parts, parts, part, 2 * part), ml_dtypes.bfloat16)
    backward = np.zeros((parts, pad, width), ml_dtypes.bfloat16)
    order = np.zeros((parts, part, pad), ml_dtypes.bfloat16)
    for h in range(parts):
        chip = slice((h // 2) * 2 * part, (h // 2 + 1) * 2 * part)
        forward[h] = (cos if h % 2 == 0 else -sin)[:, chip].reshape(parts, part, 2 * part)
        first = (h // 2) * part
        backward[h, : part + 1] = (cos, sin)[h % 2][first : first + part + 1]
        for i in range(part):
            order[h, i, i if h in (0, 3) else part - i] = 1
    return forward, backward, order


class Place:
    def __init__(self, bits):
        h = lax.axis_index("hidden")
        b = lax.axis_index("batch")
        self.h, self.b = h, b
        self.c = lax.rem(h, 2)
        self.x = lax.div(h, 2)
        self.hc = h + 1 - 2 * self.c
        self.hx = lax.rem(h + 2, 4)
        self.hd = lax.rem(self.hc + 2, 4)
        self.p = lax.rem(b, 4)
        self.bit = [lax.rem(lax.div(b, 2**k), 2) for k in range(bits)]
        self.py = self.p + 1 - 2 * self.bit[0]
        self.pz = lax.rem(self.p + 2, 4)
        self.pd = lax.rem(self.py + 2, 4)
        self.core = {"hidden": self.hc}
        self.side = {"hidden": self.hx}
        self.cross = {"hidden": self.hd}
        self.flip = [{"batch": b + 2**k - 2 ** (k + 1) * self.bit[k]} for k in range(bits)]
        self.ydev, self.zdev = self.flip[:2]


class Fetch:
    def __init__(self, made, place, free):
        self.made, self.place, self.free = made, place, free

    def wait(self):
        self.made.wait()
        self.free.append(self.place)


class Links:
    def __init__(self, send, recv, near):
        self.send, self.recv, self.near = send, recv, near
        self.used, self.sends, self.fetched = 0, 0, 0
        self.free_sends, self.free_near, self.open = [], [], []

    def describe(self, src, dst, device):
        i = self.used
        self.used += 1
        if not self.free_sends:
            self.free_sends.append(self.sends)
            self.sends += 1
        self.place = self.free_sends.pop()
        return pltpu.make_async_remote_copy(
            src_ref=src,
            dst_ref=dst,
            send_sem=self.send.at[self.place],
            recv_sem=self.recv.at[i],
            device_id=device,
            device_id_type=MESH,
        )

    def copy(self, src, dst, device):
        made = self.describe(src, dst, device)
        made.start()
        self.open.append((made, self.place))
        return made

    def settle(self, some):
        for made in some:
            for entry in self.open:
                if entry[0] is made:
                    made.wait_send()
                    self.free_sends.append(entry[1])
            self.open = [entry for entry in self.open if entry[0] is not made]

    def settle_all(self):
        self.settle([made for made, _ in self.open])

    def fetch(self, src, dst):
        if not self.free_near:
            self.free_near.append(self.fetched)
            self.fetched += 1
        place = self.free_near.pop()
        made = Fetch(pltpu.make_async_copy(src, dst, self.near.at[place]), place, self.free_near)
        made.made.start()
        return made


def semaphores(bits):
    return (94, 143, 34) if bits == 3 else (160, 192, 64)


def greet(devices):
    barrier = pltpu.get_barrier_semaphore()
    for device in devices:
        pl.semaphore_signal(barrier, inc=1, device_id=device, device_id_type=MESH)
    pl.semaphore_wait(barrier, len(devices))


class GatherHidden:
    def __init__(self, me, links, view):
        self.me, self.links, self.view = me, links, view

    def start(self):
        own = self.view(self.me.h)
        self.by_side = self.links.copy(own, own, self.me.side)
        self.by_core = self.links.copy(own, own, self.me.core)

    def forward(self):
        self.by_side.wait_recv()
        far = self.view(self.me.hx)
        self.by_far = self.links.copy(far, far, self.me.core)


class GatherBatch:
    def __init__(self, me, links, view):
        self.me, self.links, self.view = me, links, view

    def start(self):
        ends = ((0, self.me.ydev), (1, self.me.zdev), (1, self.me.ydev), (0, self.me.zdev))
        own = [self.view(self.me.p, 0), self.view(self.me.p, 1)]
        self.y0, self.z1, self.y1, self.z0 = (self.links.copy(own[n], own[n], device) for n, device in ends)

    def forward(self):
        self.y0.wait_recv()
        part = self.view(self.me.py, 0)
        self.on_z = self.links.copy(part, part, self.me.zdev)
        self.z1.wait_recv()
        part = self.view(self.me.pz, 1)
        self.on_y = self.links.copy(part, part, self.me.ydev)

    def arrive(self):
        self.y1.wait_recv()
        self.z0.wait_recv()

    def finish(self):
        self.on_z.wait_recv()
        self.on_y.wait_recv()

    def sent(self):
        return [self.y0, self.y1, self.z0, self.z1, self.on_y, self.on_z]


class Scatter:
    def __init__(self, me, links, rows, sc, rc, sx, rx, acc):
        self.me, self.links, self.rows, self.sent = me, links, rows, []
        self.sc, self.rc, self.sx, self.rx, self.acc = sc, rc, sx, rx, acc

    def run(self, prepare, block, hook):
        x, c, cut = self.me.x, self.me.c, pl.ds(0, self.rows)
        for n, start in enumerate((2 * (1 - x), 2 * x)):
            away, home = start + 1 - c, start + c

            def send(i, value):
                self.sc[n, i, cut] = value.astype(LOW)

            def keep(i, value):
                value = value + self.rc[n, i, cut].astype(F32)
                if n == 0:
                    self.sx[i] = value.astype(LOW)
                else:
                    self.acc[i, cut] = value

            prepare(0, away)
            block(0, away, send)
            by_core = self.links.copy(self.sc.at[n, :, cut], self.rc.at[n, :, cut], self.me.core)
            self.sent.append(by_core)
            prepare(1, home)
            by_core.wait_recv()
            block(1, home, keep)
            if n == 0:
                self.by_side = self.links.copy(self.sx, self.rx, self.me.side)
                self.sent.append(self.by_side)
                hook()

    def wait(self):
        self.by_side.wait_recv()

    def value(self, i):
        return self.acc[i, 0 : self.rows] + self.rx[i].astype(F32)


class Share:
    def __init__(self, me, links, rows, sc, rc, acc):
        self.me, self.links, self.cut = me, links, pl.ds(0, rows)
        self.sc, self.rc, self.acc = sc, rc, acc

    def away(self, block):
        def sink(i, value):
            self.sc[i, self.cut] = value.astype(LOW)

        block(1 - self.me.c, sink)
        self.by_core = self.links.copy(self.sc.at[:, self.cut], self.rc.at[:, self.cut], self.me.core)

    def home(self, block):
        def sink(i, value):
            self.acc[i, self.cut] = value

        block(self.me.c, sink)

    def wait(self):
        self.by_core.wait_recv()

    def value(self, i):
        return self.acc[i, self.cut] + self.rc[i, self.cut].astype(F32)


class Reduce:
    def __init__(self, me, links, order, given, given_landing, total, low, landing, whole):
        self.me, self.links, self.order = me, links, order
        self.given, self.given_landing = given, given_landing
        self.total, self.low, self.landing, self.whole = total, low, landing, whole
        self.blocks = total.shape[1] // whole.shape[2]
        bits, size = len(me.bit), total.shape[0]
        kinds = {"x": self.cross, "y": self.halve, "z": self.quarter}
        self.plan = [(kinds[axis], 0) for axis in order]
        more = extra_halvings(size, bits)
        self.plan += [(self.halve, k) for k in range(3, 3 + more)]
        self.plan += [(self.double, k) for k in range(3 + more, bits)]
        back = [(self.gather_half, k) for k in reversed(range(3, 3 + more))]
        back += [({"y": self.gather_half, "z": self.gather_quarters}[axis], 0) for axis in reversed(order) if axis != "x"]
        self.plan += back
        self.first_back = len(self.plan) - len(back)
        self.doubled = bits > 3 + more
        self.at, self.used, self.spans, self.crossed, self.after = 0, 0, [(0, size)], False, None

    def span(self, first, size):
        return pl.ds(pl.multiple_of(first, 16), size)

    def end(self):
        if self.after is not None:
            self.after()
            self.after = None

    def step(self):
        self.end()
        if self.at == len(self.plan):
            return False
        if self.at == self.first_back:
            mine, wide = self.span(*self.spans[-1]), self.whole.shape[2]
            own = self.low if self.doubled else self.total
            for n in range(self.blocks):
                self.whole[n, mine, :] = own[mine, n * wide : (n + 1) * wide].astype(LOW)
        kind, k = self.plan[self.at]
        self.at += 1
        kind(k)
        return True

    def land(self, size):
        self.used += size
        return pl.ds(self.used - size, size)

    def add(self, made, mine, place):
        made.wait_recv()
        self.add_rows(mine, self.landing, place.start)

    def add_rows(self, mine, landing, start):
        def some(at, i, step):
            self.total[pl.ds(at, step), :] += landing[pl.ds(start + i, step), :].astype(F32)

        by_rows(mine.start, mine.size, some)

    def send(self, first, size, device):
        give, place = self.span(first, size), self.land(size)

        def some(at, i, step):
            self.low[pl.ds(at, step), :] = self.total[pl.ds(at, step), :].astype(LOW)

        by_rows(first, size, some)
        return self.links.copy(self.low.at[give], self.landing.at[place], device), place

    def cross(self, _):
        first, size = self.spans[-1]
        mine, place = self.span(first, size), pl.ds(self.given.shape[0] - size, size)
        made = self.links.copy(self.given.at[mine], self.given_landing.at[place], self.me.side)
        self.crossed = True

        def after():
            made.wait_recv()
            self.add_rows(mine, self.given_landing, place.start)

        self.after = after

    def halve(self, k):
        first, size = self.spans[-1]
        half, u = size // 2, self.me.bit[k]
        keep, away = first + u * half, first + (1 - u) * half
        mine = self.span(keep, half)
        self.spans.append((keep, half))
        far = None
        if not self.crossed:
            far = self.links.copy(self.given.at[self.span(away, half)], self.given_landing.at[pl.ds(0, half)], self.me.flip[k])
        made, place = self.send(away, half, self.me.flip[k])

        def after():
            if far is not None:
                far.wait_recv()

                def some(at, i, step):
                    rows = pl.ds(at, step)
                    total = self.given[rows, :].astype(F32) + self.given_landing[pl.ds(i, step), :].astype(F32)
                    self.given[rows, :] = total.astype(LOW)

                by_rows(keep, half, some)
            self.add(made, mine, place)

        self.after = after

    def column(self, d):
        v = self.me.bit[1] + 2 * self.me.bit[2]
        w = lax.rem(v + d, 4)
        return w, {"batch": self.me.b + 2 * (w - v)}

    def quarter(self, _):
        first, size = self.spans[-1]
        part = size // 4
        keep = first + (self.me.bit[1] + 2 * self.me.bit[2]) * part
        self.spans.append((keep, part))
        made = []
        for d in (2, 1, 3):
            w, device = self.column(d)
            made.append(self.send(first + w * part, part, device))

        def after():
            for one, place in made:
                self.add(one, self.span(keep, part), place)

        self.after = after

    def double(self, k):
        mine = self.span(*self.spans[-1])
        place = self.land(self.spans[-1][1])
        if self.plan[self.at - 2][0] != self.double:
            self.low[mine, :] = self.total[mine, :].astype(LOW)
        made = self.links.copy(self.low.at[mine], self.landing.at[place], self.me.flip[k])

        def after():
            made.wait_recv()
            self.links.settle([made])
            self.low[mine, :] = (self.low[mine, :].astype(F32) + self.landing[place, :].astype(F32)).astype(LOW)

        self.after = after

    def gather(self, devices):
        part = self.whole.at[pl.ds(0, self.blocks), self.span(*self.spans.pop())]
        made = [self.links.copy(part, part, device) for device in devices]

        def after():
            for one in made:
                one.wait_recv()

        self.after = after

    def gather_half(self, k):
        self.gather([self.me.flip[k]])

    def gather_quarters(self, _):
        self.gather([self.column(d)[1] for d in (2, 1, 3)])


def extra_halvings(size, bits):
    count, left = 0, size // 8
    while 3 + count < bits and (left // 2) % 16 == 0:
        count, left = count + 1, left // 2
    return count


def landing_rows(size, bits):
    more, left = extra_halvings(size, bits), size // 8
    return 7 * left + sum(left >> (k + 1) for k in range(more)) + (bits - 3 - more) * (left >> more)


def chunk_rows(units):
    third = units // 3
    return (third,) * 3, (third,) * 3


def columns(t, size):
    return pl.ds(pl.multiple_of(t * size, size), size)


def loop(count, body):
    def one(i, carry):
        body(i)
        return carry

    lax.fori_loop(0, count, one, 0)


def by_rows(first, size, body):
    step = min(size, 32)

    def one(i):
        body(pl.multiple_of(first + i * step, 16), pl.multiple_of(i * step, 16), step)

    loop(size // step, one)


ROOT = math.sqrt(2 / math.pi)
CUBE = 0.044715


def gelu_both(v):
    square = v * v
    t = jnp.tanh(v * (ROOT + ROOT * CUBE * square))
    half = 0.5 + 0.5 * t
    slope = half + (0.5 * v) * (1 - t * t) * (ROOT + 3 * ROOT * CUBE * square)
    return v * half, slope


def up(value):
    return jnp.sum(value, 0, keepdims=True)


SCHEDULE = (
    ("give", 0), ("chunk", 1), ("keep", 0), ("chunk", 2), ("back", 0), ("back", 1), ("norm", 0), ("give", 1),
    ("keep", 1), ("chunk", 5), ("chunk", 3), ("chunk", 2), ("chunk", 1), ("near", 0), ("far", 0), ("halves", 0),
    ("chunk", 3), ("chunk", 5), ("norm", 1), ("chunk", 4), ("chunk", 2), ("pack", 0), ("chunk", 5), ("chunk", 2),
    ("near", 1), ("chunk", 0), ("chunk", 3), ("chunk", 5), ("far", 1), ("chunk", 4), ("outs", 1), ("chunk", 0),
    ("chunk", 3), ("small", 0), ("outs", 0), ("sequence", 0), ("order", 0), ("chunk", 2), ("chunk", 4), ("chunk", 1),
    ("ends", 1), ("chunk", 0), ("halves", 1), ("chunk", 5), ("chunk", 4), ("chunk", 1), ("chunk", 3), ("chunk", 0),
    ("chunk", 2), ("chunk", 5), ("round", 0), ("chunk", 1), ("ends", 0), ("chunk", 4), ("sequence", 1), ("order", 1),
    ("chunk", 0), ("grad", 0), ("round", 0), ("chunk", 4), ("chunk", 3), ("grad", 1), ("chunk", 0), ("chunk", 1),
)
ORDERS = ("xyz", "xzy", "yxz", "xyz", "yxz", "yxz")


def layer_kernel(
    bits,
    x_hbm, cot_hbm, w1_hbm, w2_hbm, small_hbm, ht_hbm, gt_hbm, order_hbm,
    g1_ref, s1_ref, bo_ref, g2_ref, s2_ref, bin_ref, live_ref,
    out_hbm, grad_hbm, wg1_hbm, wg2_hbm, light_ref, bias_ref,
    tab, small, ht, gt, order, xg, cs, ct, og, ab, sc, rc, sx, rx, acc, yf, hf, df, zf, u1, gr2, inv1, lanes,
    wr, wt, wg, given, landing, ug, flat, rowv, rows_in, pn, lsend, lrecv, lbias, ltot, lnext, send, recv, near,
):
    slots, _, piece = x_hbm.shape
    parts, rows, tokens = cs.shape[1:]
    width = parts * rows
    units = wg.shape[1]
    pad = gt.shape[0]
    me = Place(bits)
    links = Links(send, recv, near)
    is_cos = me.c == 0
    live = [jnp.where(live_ref[0] > s, 1.0, 0.0).astype(F32) for s in range(slots)]

    def fetch_tokens(src, dst, s):
        return [links.fetch(src.at[s, :, pl.ds(t * tokens, tokens)], dst.at[s, t]) for t in range(parts)]

    x_in = [fetch_tokens(x_hbm, u1, s) for s in range(slots)]
    w1_in, w2_in = links.fetch(w1_hbm, wg.at[0]), links.fetch(w2_hbm, wg.at[1])
    small_in = links.fetch(small_hbm.at[me.p], small)
    cot_in = [fetch_tokens(cot_hbm, gr2, s) for s in range(slots)]
    ht_in = links.fetch(ht_hbm.at[me.h], ht)
    gt_in = links.fetch(gt_hbm.at[me.h], gt)
    order_in = links.fetch(order_hbm.at[me.h], order)
    greet([me.core, me.side, me.cross] + me.flip)

    def input_view(s):
        def view(q, half=None):
            return xg.at[s, q, slice(None) if half is None else pl.ds(half * 2, 2), me.c]

        return view

    spread = [GatherBatch(me, links, input_view(s)) for s in range(slots)]
    over = [[] for _ in range(slots)]

    def hand_over(s, q):
        block = input_view(s)(q)
        over[s].append(links.copy(block, block, me.core))

    for s in range(slots):
        for t in range(parts):
            x_in[s][t].wait()
            xg[s, me.p, t, me.c] = u1[s, t].astype(LOW)
        if s == 0:
            spread[0].start()
        hand_over(s, me.p)

    far = 1 - me.x
    quarter, straight = units // SPLIT, width - 128

    def weight_view(q, half=None):
        at = pl.ds(pl.multiple_of(q * quarter, 16), quarter)
        return wr.at[slice(None) if half is None else pl.ds(half, 1), far, at, pl.ds(0, straight)]

    weights = GatherBatch(me, links, weight_view)
    w1_in.wait()
    w2_in.wait()

    def own_weights(r, carry):
        at = columns(r, 256)
        for n in range(units // 256):
            cut = slice(n * 256, (n + 1) * 256)
            first, second = wg[0, at, cut], wg[1, at, cut]
            wt[0, me.x, at, cut] = first.astype(LOW)
            wr[0, me.x, cut, at] = first.T.astype(LOW)
            wr[1, me.x, at, cut] = second.astype(LOW)
            wt[1, me.x, cut, at] = second.T.astype(LOW)
        return carry

    lax.fori_loop(0, units // 256, own_weights, 0)
    quarter_at = pl.ds(pl.multiple_of(me.p * quarter, 16), quarter)
    mine_w = wr.at[:, me.x, quarter_at, pl.ds(0, straight)]
    by_side = links.copy(mine_w, mine_w, me.side)
    mine_w = wr.at[:, me.x, :, pl.ds(straight, 128)]
    direct = links.copy(mine_w, mine_w, me.side)

    vectors = (g1_ref, s1_ref, bo_ref, g2_ref, s2_ref)
    rowv[...] = jnp.zeros_like(rowv)
    for r in range(units // 128):
        flat[:, r * 128 : (r + 1) * 128] = bin_ref[r : r + 1, :]
    for k, ref in enumerate(vectors):
        rowv[k : k + 1, 0:rows] = ref[...]
    for i in range(parts):
        rowv[5 + i : 6 + i, 0:rows] = flat[:, i * rows : (i + 1) * rows]
    params = [links.copy(rowv, rows_in.at[me.h], device) for device in (me.core, me.side, me.cross)]

    small_in.wait()

    def make_rows(i, carry):
        big_cos, big_sin = small[0, pl.ds(i, 1), :], small[1, pl.ds(i, 1), :]
        by_cos = jnp.where(is_cos, big_cos, big_sin)
        by_sin = jnp.where(is_cos, -big_sin, big_cos)
        at = pl.ds(pl.multiple_of(i * FINE, FINE), FINE)
        for n in range(piece // 256):
            cut = slice(n * 256, (n + 1) * 256)
            tab[at, cut] = (by_cos[:, cut] * small[2, :, cut] + by_sin[:, cut] * small[3, :, cut]).astype(LOW)
        return carry

    lax.fori_loop(0, FINE, make_rows, 0)
    spread[0].forward()
    spread[1].start()
    for s in range(slots):
        for t in range(parts):
            cot_in[s][t].wait()
            cs[s, t] = (gr2[s, t] * live[s]).astype(LOW)
        ct[s, me.h] = cs[s, me.h]
    ht_in.wait()

    sums = [
        Scatter(me, links, rows, sc.at[s], rc.at[s], sx.at[s], rx.at[s], acc.at[s]) for s in range(slots)
    ]

    def prepare(s, j, t):
        at = columns(t, tokens)
        total = None
        for q in range(SPLIT):
            for n in range(parts):
                first = q * piece + n * tokens
                share = dot(xg[s, q, n].reshape(2 * rows, tokens), tab[first : first + tokens, at])
                total = share if total is None else total + share
        ab[j] = total.astype(LOW)

    def transform(s, j, t, sink):
        def one(i):
            own = jnp.where(me.h == i, 1.0, 0.0).astype(F32)
            sink(i, dot(ht[i], ab[j]) + own * u1[s, t])

        loop(parts, one)

    moved = []

    def next_input():
        spread[1].forward()
        by_side.wait_recv()
        weights.start()

    def next_weights():
        weights.forward()

    for s, hook in enumerate((next_input, next_weights)):
        spread[s].arrive()
        hand_over(s, me.py)
        hand_over(s, me.pz)
        spread[s].finish()
        hand_over(s, me.pd)
        for made in over[s]:
            made.wait_recv()
        sums[s].run(functools.partial(prepare, s), functools.partial(transform, s), hook)
        for to, device in ((me.hc, me.core), (me.hx, me.side), (me.hd, me.cross)):
            moved.append(links.copy(cs.at[s, to], ct.at[s, me.h], device))
        links.settle(over[s] + spread[s].sent())
    for made in params:
        made.wait_recv()
    rows_in[me.h] = rowv[...]
    square = jnp.zeros((128 - rowv.shape[0], rowv.shape[1]), F32)
    for i in range(parts):
        pn[i] = jnp.concatenate([rows_in[i], square], 0).T[0:rows, :]

    def param(k, i):
        return pn[i, :, k : k + 1]

    def folded(value):
        return value[:, :128] + value[:, 128:]

    def lane_sum(k, i, s, value):
        lanes[k, i] = folded(value) if s == 0 else lanes[k, i] + folded(value)

    def row_sums(body):
        sums_of = [[up(value) for value in body(i)] for i in range(parts)]
        return [functools.reduce(jnp.add, values) for values in zip(*sums_of)]

    def each(body):
        for i in range(parts):
            body(i)

    def mean_and_inverse(total, squares):
        mean = total / width
        return mean, lax.rsqrt(squares / width - mean * mean + EPS)

    def part_rows(i):
        return pl.ds(i * rows, rows)

    def norm_first(s):
        whole = sums[s].acc

        def resid(i):
            v = sums[s].value(i)
            whole[i, 0:rows] = v
            return v, v * v

        mean, inverse = mean_and_inverse(*row_sums(resid))
        inv1[s] = inverse

        def one(i):
            u = (whole[i, 0:rows] - mean) * inverse
            u1[s, i] = u
            yf[s, me.c, part_rows(i), :] = (u * param(0, i) + param(1, i)).astype(LOW)

        each(one)

    def forward_in(s, k, unit):
        def one(i):
            at = part_rows(i)
            h, slope = gelu_both(dot(wr[0, unit, at, :], yf[s, k]) + pn[2 * unit + me.c, :, 5 + i : 6 + i])
            hf[s, 2 * k + unit, at, :] = h.astype(LOW)
            df[s, 2 * k + unit, at, :] = slope.astype(LOW)

        each(one)

    def forward_out(s, k, sink):
        def one(i):
            at = part_rows(i)
            sink(i, dot(wt[1, 0, at, :], hf[s, 2 * k]) + dot(wt[1, 1, at, :], hf[s, 2 * k + 1]))

        each(one)

    def norm_second(s, shared):
        whole = shared.acc

        def resid(i):
            v = u1[s, i] * param(0, i) + param(1, i) + shared.value(i) + param(2, i)
            whole[i, 0:rows] = v
            return v, v * v

        mean, inverse = mean_and_inverse(*row_sums(resid))

        def unit(i):
            u = (whole[i, 0:rows] - mean) * inverse
            whole[i, 0:rows] = u
            cs[s, i] = (u * param(3, i) + param(4, i)).astype(LOW)
            g = ct[s, i].astype(F32)
            lane_sum(0, i, s, g * u)
            lane_sum(1, i, s, g)
            q = g * param(3, i)
            return q, q * u

        total, cross = row_sums(unit)
        total, cross = total / width, cross / width

        def one(i):
            q = ct[s, i].astype(F32) * param(3, i)
            grad = inverse * (q - total - whole[i, 0:rows] * cross)
            gr2[s, i] = grad
            lane_sum(2, i, s, grad)
            zf[s, me.c, part_rows(i), :] = grad.astype(LOW)

        each(one)

    def backward_in(s, k, fresh):
        for unit in range(2):

            def one(i):
                at = part_rows(i)
                gp = dot(wr[1, unit, at, :], zf[s, k]) * df[s, 2 * k + unit, at, :].astype(F32)
                place = 5 + unit
                lanes[place, i] = folded(gp) if fresh else lanes[place, i] + folded(gp)
                df[s, 2 * k + unit, at, :] = gp.astype(LOW)

            each(one)

    def backward_out(s, k, sink):
        def one(i):
            at = part_rows(i)
            sink(i, dot(wt[0, 0, at, :], df[s, 2 * k]) + dot(wt[0, 1, at, :], df[s, 2 * k + 1]))

        each(one)

    def weight_grad(which, unit, store):
        def one(r, carry):
            at = columns(r, 256)
            for n in range(units // 256):
                cut = slice(n * 256, (n + 1) * 256)
                total = 0.0
                for s in range(slots):
                    for k in range(2):
                        if which == 0:
                            total = total + dot_rows(hf[s, 2 * k + unit, at, :], zf[s, k, cut, :])
                        else:
                            total = total + dot_rows(yf[s, k, at, :], df[s, 2 * k + unit, cut, :])
                store(which, at, cut, total)
            return carry

        lax.fori_loop(0, units // 256, one, 0)

    def norm_first_back(s, shared):
        whole = shared.acc

        def entry(i):
            grad = gr2[s, i] + shared.value(i)
            whole[i, 0:rows] = grad
            u = u1[s, i]
            lane_sum(3, i, s, grad * u)
            lane_sum(4, i, s, grad)
            q = grad * param(0, i)
            return q, q * u

        total, cross = row_sums(entry)
        total, cross = total / width, cross / width

        def one(i):
            q = whole[i, 0:rows] * param(0, i)
            xg[s, me.h, i, 0] = (inv1[s] * (q - total - u1[s, i] * cross)).astype(LOW)

        each(one)

    def to_core(block):
        return links.copy(block, block, me.core)

    outward = [Share(me, links, rows, sc.at[s, 0], rc.at[s, 0], acc.at[s]) for s in range(slots)]
    inward = [Share(me, links, rows, sc.at[s, 1], rc.at[s, 1], acc.at[s]) for s in range(slots)]

    def enter(s):
        sums[s].wait()
        norm_first(s)
        got = to_core(yf.at[s, me.c])
        forward_in(s, me.c, me.x)
        got.wait_recv()
        forward_in(s, 1 - me.c, me.x)

    def leave(s):
        links.settle(sums[s].sent)
        forward_in(s, 1 - me.c, far)
        forward_in(s, me.c, far)
        outward[s].away(functools.partial(forward_out, s))
        outward[s].home(functools.partial(forward_out, s))

    def far_weights(r, carry):
        at = columns(r, 256)
        for n in range(units // 256):
            cut = slice(n * 256, (n + 1) * 256)
            wt[0, far, cut, at] = wr[0, far, at, cut].astype(F32).T.astype(LOW)
            wt[1, far, cut, at] = wr[1, far, at, cut].astype(F32).T.astype(LOW)
        return carry

    enter(0)
    weights.arrive()
    weights.finish()
    direct.wait_recv()
    lax.fori_loop(0, units // 256, far_weights, 0)
    links.settle([by_side, direct] + weights.sent())
    leave(0)
    enter(1)
    leave(1)
    for made in moved:
        made.wait_recv()
    links.settle(moved)
    seconds, outs = [], {}
    for s in range(slots):
        outward[s].wait()
        norm_second(s, outward[s])
        seconds.append(to_core(zf.at[s, me.c]))

    def mix_view(s):
        return lambda t: xg.at[s, t, :, 0]

    def freq_view(s):
        cuts = (pl.ds(0, pad // 32 * 16), pl.ds(pad // 32 * 16, pad - pad // 32 * 16))

        def view(q, half=None):
            return ug.at[s, q] if half is None else ug.at[s, q, cuts[half]]

        return view

    gathers = [GatherHidden(me, links, mix_view(s)) for s in range(slots)]
    spreads = [GatherBatch(me, links, freq_view(s)) for s in range(slots)]
    heavy, chunks = [], []
    for which, whole in ((0, hf), (1, df)):
        low, used = 0, 0
        for size in chunk_rows(units)[which]:
            at, place = pl.ds(low, size), pl.ds(used, landing_rows(size, bits))
            low, used = low + size, used + landing_rows(size, bits)
            chunks.append((which, at))
            heavy.append(
                Reduce(
                    me, links, ORDERS[len(heavy)], wr.at[0, which, at], given.at[which, at], wg.at[which, at], wt.at[1, which, at],
                    landing.at[which, place], whole.at[0, :, at],
                )
            )

    def features(s, t):
        whole = jnp.concatenate([xg[s, t, i, 0] for i in range(parts)], 0)
        ug[s, me.p, :, columns(t, tokens)] = dot(gt[...], whole).astype(LOW)

    def store_given(which, at, cut, value):
        wr[0, which, at, cut] = value.astype(LOW)

    def store_kept(which, at, cut, value):
        wg[which, at, cut] = value

    for made in seconds:
        made.wait_recv()
    links.settle_all()

    def backward(s):
        backward_in(s, me.c, s == 0)
        backward_in(s, 1 - me.c, False)
        inward[s].away(functools.partial(backward_out, s))
        inward[s].home(functools.partial(backward_out, s))

    def first_back(s):
        inward[s].wait()
        norm_first_back(s, inward[s])
        gathers[s].start()

    def near_features(s):
        features(s, me.h)
        gathers[s].by_core.wait_recv()
        features(s, me.hc)

    def far_features(s):
        gathers[s].forward()
        features(s, me.hx)
        gathers[s].by_far.wait_recv()
        features(s, me.hd)
        spreads[s].start()

    ones = jnp.ones((8, 128), F32)

    def lane_total(k, i):
        return lax.dot_general(
            ones, lanes[k, i], (((1,), (1,)), ((), ())), precision=lax.Precision.HIGHEST, preferred_element_type=F32
        )

    row = lax.broadcasted_iota(jnp.int32, (8, rows), 0)
    light = []

    def start_small_sums():
        for i in range(parts):
            packed = jnp.zeros((8, rows), F32)
            for k in range(5):
                packed = jnp.where(row == k, lane_total(k, i), packed)
            lsend[i] = packed
        for unit in range(2):
            packed = jnp.zeros((8, rows), F32)
            for i in range(parts):
                packed = jnp.where(row == i, lane_total(5 + unit, i), packed)
            lbias[unit] = packed
        for to, device in ((me.hc, me.core), (me.hx, me.side), (me.hd, me.cross)):
            light.append(links.copy(lsend.at[to], lrecv.at[me.h], device))
        light.append(links.copy(lbias.at[far], lbias.at[2], me.side))

    sign = jnp.where((me.h == 0) | (me.h == 3), -1.0, 1.0).astype(F32)
    mine = jnp.where(is_cos, 1.0, sign)
    theirs = jnp.where(is_cos, sign, 1.0)
    stored = []

    def sequence(s):
        spreads[s].arrive()
        spreads[s].finish()
        links.settle([outward[s].by_core])

        def one(t):
            at = columns(t, tokens)
            total = None
            for q in range(SPLIT):
                share = dot(ug[s, q], tab[q * piece : (q + 1) * piece, at])
                total = share if total is None else total + share
            acc[s, t] = total
            sc[s, 0, t] = total.astype(LOW)

        loop(parts, one)
        swaps[s] = links.copy(sc.at[s, 0], rc.at[s, 0], me.core)

    swaps, across = {}, {}

    def ordered(s):
        swaps[s].wait_recv()

        def one(t):
            pair = (mine * acc[s, t] + theirs * rc[s, 0, t].astype(F32)).astype(LOW)
            sx[s, t] = dot(order[...], pair).astype(LOW)

        loop(parts, one)
        made = links.describe(sx.at[s], rx.at[s], me.side)
        across[s] = made

        @pl.when(jnp.logical_not(is_cos))
        def _():
            made.start()

    def store_grad(s):
        def store(part):
            def one(t):
                u1[s, t] = part[s, t].astype(F32) + xg[s, t, me.h, 0].astype(F32)

            loop(parts, one)

        @pl.when(is_cos)
        def _():
            store(sx)

        @pl.when(jnp.logical_not(is_cos))
        def _():
            across[s].wait()
            store(rx)

        for t in range(parts):
            stored.append(links.fetch(u1.at[s, t], grad_hbm.at[s, :, pl.ds(t * tokens, tokens)]))

    def start_outs(s):
        og[s, me.h] = cs[s, me.h]
        outs[s] = [
            links.copy(cs.at[s, to], og.at[s, me.h], device)
            for to, device in ((me.hc, me.core), (me.hx, me.side), (me.hd, me.cross))
        ]

    def end_outs(s):
        for made in outs[s]:
            made.wait_recv()
        for t in range(parts):
            gr2[s, t] = og[s, t].astype(F32) * live[s]
            stored.append(links.fetch(gr2.at[s, t], out_hbm.at[s, :, pl.ds(t * tokens, tokens)]))

    def small_sums():
        for made in light:
            made.wait_recv()
        ltot[0, 0:8] = lsend[me.h] + lrecv[me.hc] + lrecv[me.hx] + lrecv[me.hd]
        ltot[0, 8:16] = lbias[me.x] + lbias[2]
        small_round()

    rounds = []

    def small_round():
        k = len(rounds)
        if k:
            rounds[k - 1].wait_recv()
            ltot[k] = ltot[k - 1] + lnext[k - 1]
        if k < bits:
            rounds.append(links.copy(ltot.at[k], lnext.at[k], me.flip[k]))

    def store_chunk(n):
        which, at = chunks[n]
        dst = (wg2_hbm, wg1_hbm)[which].at[at]
        for m in range(heavy[n].blocks):
            stored.append(links.fetch(heavy[n].whole.at[m], dst.at[:, pl.ds(m * tokens, tokens)]))

    def step(n):
        if not heavy[n].step():
            store_chunk(n)
            return False
        return True

    acts = {
        "back": backward,
        "norm": first_back,
        "near": near_features,
        "far": far_features,
        "halves": lambda s: spreads[s].forward(),
        "sequence": sequence,
        "order": ordered,
        "grad": store_grad,
        "give": lambda which: weight_grad(which, far, store_given),
        "keep": lambda which: weight_grad(which, me.x, store_kept),
        "pack": lambda _: start_small_sums(),
        "small": lambda _: small_sums(),
        "round": lambda _: small_round(),
        "outs": start_outs,
        "ends": end_outs,
        "chunk": lambda n: step(n),
    }
    going = [True] * len(heavy)
    gt_in.wait()
    order_in.wait()
    for kind, n in SCHEDULE:
        did = acts[kind](n)
        if kind == "chunk":
            going[n] = did
    while any(going):
        for n in range(len(heavy)):
            going[n] = going[n] and step(n)
        if len(rounds) < bits:
            small_round()
    while len(rounds) < bits:
        small_round()
    k = bits - 1
    if len(rounds) == bits:
        rounds[k].wait_recv()
        ltot[bits] = ltot[k] + lnext[k]
    light_ref[...] = ltot[bits, 0:8]
    for i in range(parts):
        flat[:, i * rows : (i + 1) * rows] = ltot[bits, 8 + i : 9 + i]
    for r in range(units // 128):
        bias_ref[r : r + 1, :] = flat[:, r * 128 : (r + 1) * 128]
    for made in stored:
        made.wait()
    links.settle_all()


def local(
    n_batch,
    layer_input,
    gain_first,
    shift_first,
    weight_in,
    bias_in,
    weight_out,
    bias_out,
    gain_second,
    shift_second,
    cotangent,
    live_counts,
):
    slots, rows, piece = layer_input.shape
    width = rows * HOLD
    tokens = piece // HOLD
    units = weight_in.shape[1]
    length = piece * SPLIT
    pad = rows + 16
    bits = n_batch.bit_length() - 1
    vectors = (gain_first, shift_first, bias_out, gain_second, shift_second, bias_in)
    small = sequence_tables(length, SPLIT)
    forward, backward, order = feature_tables(width, HOLD)
    any_, vmem = pl.BlockSpec(memory_space=pl.ANY), pl.BlockSpec(memory_space=pltpu.VMEM)
    block = (HOLD, rows, tokens)
    padded = (HOLD, pad, tokens)
    shard = (slots,) + block
    landing = max(sum(landing_rows(size, bits) for size in sizes) for sizes in chunk_rows(units))
    scratch = [
        ((length, piece), LOW), ((4, FINE, piece), F32), (forward.shape[1:], LOW), (backward.shape[1:], LOW),
        (order.shape[1:], LOW), ((slots, SPLIT, HOLD, 2, rows, tokens), LOW), (shard, LOW), (shard, LOW), (shard, LOW),
        ((2, 2 * rows, tokens), LOW), ((slots, 2) + padded, LOW), ((slots, 2) + padded, LOW), (shard, LOW), (shard, LOW),
        ((slots,) + padded, F32), ((slots, 2, width, tokens), LOW), ((slots, 4, units, tokens), LOW),
        ((slots, 4, units, tokens), LOW), ((slots, 2, width, tokens), LOW), (shard, F32), (shard, F32),
        ((slots, 1, tokens), F32), ((7, HOLD, rows, 128), F32),
        ((2, 2, units, width), LOW), ((2, 2, width, units), LOW), ((2, units, width), F32),
        ((2, units, width), LOW), ((2, landing, width), LOW),
        ((slots, SPLIT, pad, piece), LOW), ((1, units), F32), ((16, 256), F32), ((HOLD, 16, 256), F32), ((HOLD, rows, 128), F32), ((HOLD, 8, rows), F32),
        ((HOLD, 8, rows), F32), ((3, 8, rows), F32), ((bits + 1, 16, rows), F32), ((bits, 16, rows), F32),
    ]
    outs = [
        (layer_input.shape, F32), (layer_input.shape, F32), ((width, units), LOW), ((units, width), LOW),
        ((8, rows), F32), ((units // 128, 128), F32),
    ]
    out, grad, wg1, wg2, light, bias = pl.pallas_call(
        functools.partial(layer_kernel, bits),
        name="layer",
        out_shape=[jax.ShapeDtypeStruct(shape, kind) for shape, kind in outs],
        in_specs=[any_] * 8 + [vmem] * 6 + [pl.BlockSpec(memory_space=pltpu.SMEM)],
        out_specs=[any_] * 4 + [vmem] * 2,
        scratch_shapes=[pltpu.VMEM(shape, kind) for shape, kind in scratch]
        + [pltpu.SemaphoreType.DMA((count,)) for count in semaphores(bits)],
        compiler_params=pltpu.CompilerParams(
            collective_id=1, has_side_effects=True, vmem_limit_bytes=VMEM_LIMIT
        ),
    )(
        layer_input, cotangent, weight_in, weight_out, jnp.asarray(small), jnp.asarray(forward),
        jnp.asarray(backward), jnp.asarray(order), *(v.reshape(1, -1) for v in vectors[:5]), bias_in.reshape(-1, 128), live_counts,
    )
    return (
        out, grad, light[3], light[4], wg1.astype(F32), bias.reshape(units), wg2.astype(F32),
        light[2], light[0], light[1],
    )


def solution(mesh):
    return jax.shard_map(
        functools.partial(local, mesh.shape["batch"]),
        mesh=mesh,
        in_specs=(
            P(None, "hidden", "batch"),
            P("hidden"),
            P("hidden"),
            P(None, "hidden"),
            P("hidden"),
            P("hidden", None),
            P("hidden"),
            P("hidden"),
            P("hidden"),
            P(None, "hidden", "batch"),
            P("batch"),
        ),
        out_specs=(
            P(None, "hidden", "batch"),
            P(None, "hidden", "batch"),
            P("hidden"),
            P("hidden"),
            P(None, "hidden"),
            P("hidden"),
            P("hidden", None),
            P("hidden"),
            P("hidden"),
            P("hidden"),
        ),
        check_vma=False,
    )
```

```python
import functools
import math

import jax
import jax.numpy as jnp
import ml_dtypes
import numpy as np
from jax import lax
from jax.experimental import pallas as pl
from jax.experimental.pallas import tpu as pltpu
from jax.sharding import PartitionSpec as P

SPLIT = 4
HOLD = 4
EPS = 1e-06
FINE = 64
LOW = jnp.bfloat16
F32 = jnp.float32
MESH = pl.DeviceIdType.MESH
VMEM_LIMIT = 63 * 2**20


def dot(left, right):
    return jnp.dot(left, right, preferred_element_type=F32)


def dot_rows(left, right):
    return lax.dot_general(left, right, (((1,), (1,)), ((), ())), preferred_element_type=F32)


@functools.cache
def sequence_tables(length, split):
    column = np.arange(length)
    coarse = 2 * np.pi * ((FINE * np.arange(length // FINE)[:, None] * column) % length) / length
    fine = 2 * np.pi * ((np.arange(FINE)[:, None] * column) % length) / length
    factor = 1 / math.sqrt(length)
    whole = np.stack([np.cos(coarse), np.sin(coarse), factor * np.cos(fine), factor * np.sin(fine)])
    return np.ascontiguousarray(
        whole.reshape(4, FINE, split, length // split).transpose(2, 0, 1, 3).astype(np.float32)
    )


@functools.cache
def feature_tables(width, parts):
    index = np.arange(width)
    angle = 2 * np.pi * ((index[:, None] * index) % width) / width
    factor = 1 / math.sqrt(width)
    cos = (np.cos(angle) * factor).astype(np.float32).astype(ml_dtypes.bfloat16)
    sin = (np.sin(angle) * factor).astype(np.float32).astype(ml_dtypes.bfloat16)
    part = width // parts
    pad = part + 16
    forward = np.zeros((parts, parts, part, 2 * part), ml_dtypes.bfloat16)
    backward = np.zeros((parts, pad, width), ml_dtypes.bfloat16)
    order = np.zeros((parts, part, pad), ml_dtypes.bfloat16)
    for h in range(parts):
        chip = slice((h // 2) * 2 * part, (h // 2 + 1) * 2 * part)
        forward[h] = (cos if h % 2 == 0 else -sin)[:, chip].reshape(parts, part, 2 * part)
        first = (h // 2) * part
        backward[h, : part + 1] = (cos, sin)[h % 2][first : first + part + 1]
        for i in range(part):
            order[h, i, i if h in (0, 3) else part - i] = 1
    return forward, backward, order


class Place:
    def __init__(self, bits):
        h = lax.axis_index("hidden")
        b = lax.axis_index("batch")
        self.h, self.b = h, b
        self.c = lax.rem(h, 2)
        self.x = lax.div(h, 2)
        self.hc = h + 1 - 2 * self.c
        self.hx = lax.rem(h + 2, 4)
        self.hd = lax.rem(self.hc + 2, 4)
        self.p = lax.rem(b, 4)
        self.bit = [lax.rem(lax.div(b, 2**k), 2) for k in range(bits)]
        self.py = self.p + 1 - 2 * self.bit[0]
        self.pz = lax.rem(self.p + 2, 4)
        self.pd = lax.rem(self.py + 2, 4)
        self.core = {"hidden": self.hc}
        self.side = {"hidden": self.hx}
        self.cross = {"hidden": self.hd}
        self.flip = [{"batch": b + 2**k - 2 ** (k + 1) * self.bit[k]} for k in range(bits)]
        self.ydev, self.zdev = self.flip[:2]


class Fetch:
    def __init__(self, made, place, free):
        self.made, self.place, self.free = made, place, free

    def wait(self):
        self.made.wait()
        self.free.append(self.place)


class Links:
    def __init__(self, send, recv, near):
        self.send, self.recv, self.near = send, recv, near
        self.used, self.sends, self.fetched = 0, 0, 0
        self.free_sends, self.free_near, self.open = [], [], []

    def describe(self, src, dst, device):
        i = self.used
        self.used += 1
        if not self.free_sends:
            self.free_sends.append(self.sends)
            self.sends += 1
        self.place = self.free_sends.pop()
        return pltpu.make_async_remote_copy(
            src_ref=src,
            dst_ref=dst,
            send_sem=self.send.at[self.place],
            recv_sem=self.recv.at[i],
            device_id=device,
            device_id_type=MESH,
        )

    def copy(self, src, dst, device):
        made = self.describe(src, dst, device)
        made.start()
        self.open.append((made, self.place))
        return made

    def settle(self, some):
        for made in some:
            for entry in self.open:
                if entry[0] is made:
                    made.wait_send()
                    self.free_sends.append(entry[1])
            self.open = [entry for entry in self.open if entry[0] is not made]

    def settle_all(self):
        self.settle([made for made, _ in self.open])

    def fetch(self, src, dst):
        if not self.free_near:
            self.free_near.append(self.fetched)
            self.fetched += 1
        place = self.free_near.pop()
        made = Fetch(pltpu.make_async_copy(src, dst, self.near.at[place]), place, self.free_near)
        made.made.start()
        return made


def semaphores(bits):
    return (47, 143, 34) if bits == 3 else (160, 192, 64)


def greet(devices):
    barrier = pltpu.get_barrier_semaphore()
    for device in devices:
        pl.semaphore_signal(barrier, inc=1, device_id=device, device_id_type=MESH)
    pl.semaphore_wait(barrier, len(devices))


class GatherHidden:
    def __init__(self, me, links, view):
        self.me, self.links, self.view = me, links, view

    def start(self):
        own = self.view(self.me.h)
        self.by_side = self.links.copy(own, own, self.me.side)
        self.by_core = self.links.copy(own, own, self.me.core)

    def forward(self):
        self.by_side.wait_recv()
        far = self.view(self.me.hx)
        self.by_far = self.links.copy(far, far, self.me.core)


class GatherBatch:
    def __init__(self, me, links, view):
        self.me, self.links, self.view = me, links, view

    def start(self):
        ends = ((0, self.me.ydev), (1, self.me.zdev), (1, self.me.ydev), (0, self.me.zdev))
        own = [self.view(self.me.p, 0), self.view(self.me.p, 1)]
        self.y0, self.z1, self.y1, self.z0 = (self.links.copy(own[n], own[n], device) for n, device in ends)

    def forward(self):
        self.y0.wait_recv()
        part = self.view(self.me.py, 0)
        self.on_z = self.links.copy(part, part, self.me.zdev)
        self.z1.wait_recv()
        part = self.view(self.me.pz, 1)
        self.on_y = self.links.copy(part, part, self.me.ydev)

    def arrive(self):
        self.y1.wait_recv()
        self.z0.wait_recv()

    def finish(self):
        self.on_z.wait_recv()
        self.on_y.wait_recv()

    def sent(self):
        return [self.y0, self.y1, self.z0, self.z1, self.on_y, self.on_z]


class Scatter:
    def __init__(self, me, links, rows, sc, rc, sx, rx, acc):
        self.me, self.links, self.rows, self.sent = me, links, rows, []
        self.sc, self.rc, self.sx, self.rx, self.acc = sc, rc, sx, rx, acc

    def run(self, prepare, block, hook):
        x, c, cut = self.me.x, self.me.c, pl.ds(0, self.rows)
        for n, start in enumerate((2 * (1 - x), 2 * x)):
            away, home = start + 1 - c, start + c

            def send(i, value):
                self.sc[n, i, cut] = value.astype(LOW)

            def keep(i, value):
                value = value + self.rc[n, i, cut].astype(F32)
                if n == 0:
                    self.sx[i] = value.astype(LOW)
                else:
                    self.acc[i, cut] = value

            prepare(0, away)
            block(0, away, send)
            by_core = self.links.copy(self.sc.at[n, :, cut], self.rc.at[n, :, cut], self.me.core)
            self.sent.append(by_core)
            prepare(1, home)
            by_core.wait_recv()
            block(1, home, keep)
            if n == 0:
                self.by_side = self.links.copy(self.sx, self.rx, self.me.side)
                self.sent.append(self.by_side)
                hook()

    def wait(self):
        self.by_side.wait_recv()

    def value(self, i):
        return self.acc[i, 0 : self.rows] + self.rx[i].astype(F32)


class Share:
    def __init__(self, me, links, rows, sc, rc, acc):
        self.me, self.links, self.cut = me, links, pl.ds(0, rows)
        self.sc, self.rc, self.acc = sc, rc, acc

    def away(self, block):
        def sink(i, value):
            self.sc[i, self.cut] = value.astype(LOW)

        block(1 - self.me.c, sink)
        self.by_core = self.links.copy(self.sc.at[:, self.cut], self.rc.at[:, self.cut], self.me.core)

    def home(self, block):
        def sink(i, value):
            self.acc[i, self.cut] = value

        block(self.me.c, sink)

    def wait(self):
        self.by_core.wait_recv()

    def value(self, i):
        return self.acc[i, self.cut] + self.rc[i, self.cut].astype(F32)


class Reduce:
    def __init__(self, me, links, order, given, given_landing, total, low, landing, whole):
        self.me, self.links, self.order = me, links, order
        self.given, self.given_landing = given, given_landing
        self.total, self.low, self.landing, self.whole = total, low, landing, whole
        self.blocks = total.shape[1] // whole.shape[2]
        bits, size = len(me.bit), total.shape[0]
        kinds = {"x": self.cross, "y": self.halve, "z": self.quarter}
        self.plan = [(kinds[axis], 0) for axis in order]
        more = extra_halvings(size, bits)
        self.plan += [(self.halve, k) for k in range(3, 3 + more)]
        self.plan += [(self.double, k) for k in range(3 + more, bits)]
        back = [(self.gather_half, k) for k in reversed(range(3, 3 + more))]
        back += [({"y": self.gather_half, "z": self.gather_quarters}[axis], 0) for axis in reversed(order) if axis != "x"]
        self.plan += back
        self.first_back = len(self.plan) - len(back)
        self.doubled = bits > 3 + more
        self.at, self.used, self.spans, self.crossed, self.after = 0, 0, [(0, size)], False, None

    def span(self, first, size):
        return pl.ds(pl.multiple_of(first, 16), size)

    def end(self):
        if self.after is not None:
            self.after()
            self.after = None

    def step(self):
        self.end()
        if self.at == len(self.plan):
            return False
        if self.at == self.first_back:
            mine, wide = self.span(*self.spans[-1]), self.whole.shape[2]
            own = self.low if self.doubled else self.total
            for n in range(self.blocks):
                self.whole[n, mine, :] = own[mine, n * wide : (n + 1) * wide].astype(LOW)
        kind, k = self.plan[self.at]
        self.at += 1
        kind(k)
        return True

    def land(self, size):
        self.used += size
        return pl.ds(self.used - size, size)

    def add(self, made, mine, place):
        made.wait_recv()
        self.add_rows(mine, self.landing, place.start)
        self.links.settle([made])

    def add_rows(self, mine, landing, start):
        def some(at, i, step):
            self.total[pl.ds(at, step), :] += landing[pl.ds(start + i, step), :].astype(F32)

        by_rows(mine.start, mine.size, some)

    def send(self, first, size, device):
        give, place = self.span(first, size), self.land(size)

        def some(at, i, step):
            self.low[pl.ds(at, step), :] = self.total[pl.ds(at, step), :].astype(LOW)

        by_rows(first, size, some)
        return self.links.copy(self.low.at[give], self.landing.at[place], device), place

    def cross(self, _):
        first, size = self.spans[-1]
        mine, place = self.span(first, size), pl.ds(self.given.shape[0] - size, size)
        made = self.links.copy(self.given.at[mine], self.given_landing.at[place], self.me.side)
        self.crossed = True

        def after():
            made.wait_recv()
            self.add_rows(mine, self.given_landing, place.start)
            self.links.settle([made])

        self.after = after

    def halve(self, k):
        first, size = self.spans[-1]
        half, u = size // 2, self.me.bit[k]
        keep, away = first + u * half, first + (1 - u) * half
        mine = self.span(keep, half)
        self.spans.append((keep, half))
        far = None
        if not self.crossed:
            far = self.links.copy(self.given.at[self.span(away, half)], self.given_landing.at[pl.ds(0, half)], self.me.flip[k])
        made, place = self.send(away, half, self.me.flip[k])

        def after():
            if far is not None:
                far.wait_recv()

                def some(at, i, step):
                    rows = pl.ds(at, step)
                    total = self.given[rows, :].astype(F32) + self.given_landing[pl.ds(i, step), :].astype(F32)
                    self.given[rows, :] = total.astype(LOW)

                by_rows(keep, half, some)
                self.links.settle([far])
            self.add(made, mine, place)

        self.after = after

    def column(self, d):
        v = self.me.bit[1] + 2 * self.me.bit[2]
        w = lax.rem(v + d, 4)
        return w, {"batch": self.me.b + 2 * (w - v)}

    def quarter(self, _):
        first, size = self.spans[-1]
        part = size // 4
        keep = first + (self.me.bit[1] + 2 * self.me.bit[2]) * part
        self.spans.append((keep, part))
        made = []
        for d in (2, 1, 3):
            w, device = self.column(d)
            made.append(self.send(first + w * part, part, device))

        def after():
            for one, place in made:
                self.add(one, self.span(keep, part), place)

        self.after = after

    def double(self, k):
        mine = self.span(*self.spans[-1])
        place = self.land(self.spans[-1][1])
        if self.plan[self.at - 2][0] != self.double:
            self.low[mine, :] = self.total[mine, :].astype(LOW)
        made = self.links.copy(self.low.at[mine], self.landing.at[place], self.me.flip[k])

        def after():
            made.wait_recv()
            self.links.settle([made])
            self.low[mine, :] = (self.low[mine, :].astype(F32) + self.landing[place, :].astype(F32)).astype(LOW)

        self.after = after

    def gather(self, devices):
        part = self.whole.at[pl.ds(0, self.blocks), self.span(*self.spans.pop())]
        made = [self.links.copy(part, part, device) for device in devices]

        def after():
            for one in made:
                one.wait_recv()
            self.links.settle(made)

        self.after = after

    def gather_half(self, k):
        self.gather([self.me.flip[k]])

    def gather_quarters(self, _):
        self.gather([self.column(d)[1] for d in (2, 1, 3)])


def extra_halvings(size, bits):
    count, left = 0, size // 8
    while 3 + count < bits and (left // 2) % 16 == 0:
        count, left = count + 1, left // 2
    return count


def landing_rows(size, bits):
    more, left = extra_halvings(size, bits), size // 8
    return 7 * left + sum(left >> (k + 1) for k in range(more)) + (bits - 3 - more) * (left >> more)


def chunk_rows(units):
    third = units // 3
    return (third,) * 3, (third,) * 3


def columns(t, size):
    return pl.ds(pl.multiple_of(t * size, size), size)


def loop(count, body):
    def one(i, carry):
        body(i)
        return carry

    lax.fori_loop(0, count, one, 0)


def by_rows(first, size, body):
    step = min(size, 32)

    def one(i):
        body(pl.multiple_of(first + i * step, 16), pl.multiple_of(i * step, 16), step)

    loop(size // step, one)


ROOT = math.sqrt(2 / math.pi)
CUBE = 0.044715


def gelu_both(v):
    square = v * v
    t = jnp.tanh(v * (ROOT + ROOT * CUBE * square))
    half = 0.5 + 0.5 * t
    slope = half + (0.5 * v) * (1 - t * t) * (ROOT + 3 * ROOT * CUBE * square)
    return v * half, slope


def up(value):
    return jnp.sum(value, 0, keepdims=True)


SCHEDULE = (
    ("give", 0), ("chunk", 1), ("keep", 0), ("chunk", 2), ("back", 0), ("back", 1), ("norm", 0), ("give", 1),
    ("keep", 1), ("chunk", 5), ("chunk", 3), ("chunk", 2), ("chunk", 1), ("near", 0), ("far", 0), ("halves", 0),
    ("chunk", 3), ("chunk", 5), ("norm", 1), ("chunk", 4), ("chunk", 2), ("pack", 0), ("chunk", 5), ("chunk", 2),
    ("near", 1), ("chunk", 0), ("chunk", 3), ("chunk", 5), ("far", 1), ("chunk", 4), ("outs", 1), ("chunk", 0),
    ("chunk", 3), ("small", 0), ("outs", 0), ("sequence", 0), ("order", 0), ("chunk", 2), ("chunk", 4), ("chunk", 1),
    ("ends", 1), ("chunk", 0), ("halves", 1), ("chunk", 5), ("chunk", 4), ("chunk", 1), ("chunk", 3), ("chunk", 0),
    ("chunk", 2), ("chunk", 5), ("round", 0), ("chunk", 1), ("ends", 0), ("chunk", 4), ("sequence", 1), ("order", 1),
    ("chunk", 0), ("grad", 0), ("round", 0), ("chunk", 4), ("chunk", 3), ("grad", 1), ("chunk", 0), ("chunk", 1),
)
ORDERS = ("xyz", "xzy", "yxz", "xyz", "yxz", "yxz")


def layer_kernel(
    bits,
    x_hbm, cot_hbm, w1_hbm, w2_hbm, small_hbm, ht_hbm, gt_hbm, order_hbm,
    g1_ref, s1_ref, bo_ref, g2_ref, s2_ref, bin_ref, live_ref,
    out_hbm, grad_hbm, wg1_hbm, wg2_hbm, light_ref, bias_ref,
    tab, small, ht, gt, order, xg, cs, ct, og, ab, sc, rc, sx, rx, acc, yf, hf, df, zf, u1, gr2, inv1, lanes,
    wr, wt, wg, given, landing, ug, flat, rowv, rows_in, pn, lsend, lrecv, lbias, ltot, lnext, send, recv, near,
):
    slots, _, piece = x_hbm.shape
    parts, rows, tokens = cs.shape[1:]
    width = parts * rows
    units = wg.shape[1]
    pad = gt.shape[0]
    me = Place(bits)
    links = Links(send, recv, near)
    is_cos = me.c == 0
    live = [jnp.where(live_ref[0] > s, 1.0, 0.0).astype(F32) for s in range(slots)]

    def fetch_tokens(src, dst, s):
        return [links.fetch(src.at[s, :, pl.ds(t * tokens, tokens)], dst.at[s, t]) for t in range(parts)]

    x_in = [fetch_tokens(x_hbm, u1, s) for s in range(slots)]
    w1_in, w2_in = links.fetch(w1_hbm, wg.at[0]), links.fetch(w2_hbm, wg.at[1])
    small_in = links.fetch(small_hbm.at[me.p], small)
    cot_in = [fetch_tokens(cot_hbm, gr2, s) for s in range(slots)]
    ht_in = links.fetch(ht_hbm.at[me.h], ht)
    gt_in = links.fetch(gt_hbm.at[me.h], gt)
    order_in = links.fetch(order_hbm.at[me.h], order)
    greet([me.core, me.side, me.cross] + me.flip)

    def input_view(s):
        def view(q, half=None):
            return xg.at[s, q, slice(None) if half is None else pl.ds(half * 2, 2), me.c]

        return view

    spread = [GatherBatch(me, links, input_view(s)) for s in range(slots)]
    over = [[] for _ in range(slots)]

    def hand_over(s, q):
        block = input_view(s)(q)
        over[s].append(links.copy(block, block, me.core))

    for s in range(slots):
        for t in range(parts):
            x_in[s][t].wait()
            xg[s, me.p, t, me.c] = u1[s, t].astype(LOW)
        if s == 0:
            spread[0].start()
        hand_over(s, me.p)

    far = 1 - me.x
    quarter, straight = units // SPLIT, width - 128

    def weight_view(q, half=None):
        at = pl.ds(pl.multiple_of(q * quarter, 16), quarter)
        return wr.at[slice(None) if half is None else pl.ds(half, 1), far, at, pl.ds(0, straight)]

    weights = GatherBatch(me, links, weight_view)
    w1_in.wait()
    w2_in.wait()

    def own_weights(r, carry):
        at = columns(r, 256)
        for n in range(units // 256):
            cut = slice(n * 256, (n + 1) * 256)
            first, second = wg[0, at, cut], wg[1, at, cut]
            wt[0, me.x, at, cut] = first.astype(LOW)
            wr[0, me.x, cut, at] = first.T.astype(LOW)
            wr[1, me.x, at, cut] = second.astype(LOW)
            wt[1, me.x, cut, at] = second.T.astype(LOW)
        return carry

    lax.fori_loop(0, units // 256, own_weights, 0)
    quarter_at = pl.ds(pl.multiple_of(me.p * quarter, 16), quarter)
    mine_w = wr.at[:, me.x, quarter_at, pl.ds(0, straight)]
    by_side = links.copy(mine_w, mine_w, me.side)
    mine_w = wr.at[:, me.x, :, pl.ds(straight, 128)]
    direct = links.copy(mine_w, mine_w, me.side)

    vectors = (g1_ref, s1_ref, bo_ref, g2_ref, s2_ref)
    rowv[...] = jnp.zeros_like(rowv)
    for r in range(units // 128):
        flat[:, r * 128 : (r + 1) * 128] = bin_ref[r : r + 1, :]
    for k, ref in enumerate(vectors):
        rowv[k : k + 1, 0:rows] = ref[...]
    for i in range(parts):
        rowv[5 + i : 6 + i, 0:rows] = flat[:, i * rows : (i + 1) * rows]
    params = [links.copy(rowv, rows_in.at[me.h], device) for device in (me.core, me.side, me.cross)]

    small_in.wait()

    def make_rows(i, carry):
        big_cos, big_sin = small[0, pl.ds(i, 1), :], small[1, pl.ds(i, 1), :]
        by_cos = jnp.where(is_cos, big_cos, big_sin)
        by_sin = jnp.where(is_cos, -big_sin, big_cos)
        at = pl.ds(pl.multiple_of(i * FINE, FINE), FINE)
        for n in range(piece // 256):
            cut = slice(n * 256, (n + 1) * 256)
            tab[at, cut] = (by_cos[:, cut] * small[2, :, cut] + by_sin[:, cut] * small[3, :, cut]).astype(LOW)
        return carry

    lax.fori_loop(0, FINE, make_rows, 0)
    spread[0].forward()
    spread[1].start()
    for s in range(slots):
        for t in range(parts):
            cot_in[s][t].wait()
            cs[s, t] = (gr2[s, t] * live[s]).astype(LOW)
        ct[s, me.h] = cs[s, me.h]
    ht_in.wait()

    sums = [
        Scatter(me, links, rows, sc.at[s], rc.at[s], sx.at[s], rx.at[s], acc.at[s]) for s in range(slots)
    ]

    def prepare(s, j, t):
        at = columns(t, tokens)
        total = None
        for q in range(SPLIT):
            for n in range(parts):
                first = q * piece + n * tokens
                share = dot(xg[s, q, n].reshape(2 * rows, tokens), tab[first : first + tokens, at])
                total = share if total is None else total + share
        ab[j] = total.astype(LOW)

    def transform(s, j, t, sink):
        def one(i):
            own = jnp.where(me.h == i, 1.0, 0.0).astype(F32)
            sink(i, dot(ht[i], ab[j]) + own * u1[s, t])

        loop(parts, one)

    moved = []

    def next_input():
        spread[1].forward()
        by_side.wait_recv()
        weights.start()

    def next_weights():
        weights.forward()

    for s, hook in enumerate((next_input, next_weights)):
        spread[s].arrive()
        hand_over(s, me.py)
        hand_over(s, me.pz)
        spread[s].finish()
        hand_over(s, me.pd)
        for made in over[s]:
            made.wait_recv()
        sums[s].run(functools.partial(prepare, s), functools.partial(transform, s), hook)
        for to, device in ((me.hc, me.core), (me.hx, me.side), (me.hd, me.cross)):
            moved.append(links.copy(cs.at[s, to], ct.at[s, me.h], device))
        links.settle(over[s] + spread[s].sent())
    for made in params:
        made.wait_recv()
    rows_in[me.h] = rowv[...]
    square = jnp.zeros((128 - rowv.shape[0], rowv.shape[1]), F32)
    for i in range(parts):
        pn[i] = jnp.concatenate([rows_in[i], square], 0).T[0:rows, :]

    def param(k, i):
        return pn[i, :, k : k + 1]

    def folded(value):
        return value[:, :128] + value[:, 128:]

    def lane_sum(k, i, s, value):
        lanes[k, i] = folded(value) if s == 0 else lanes[k, i] + folded(value)

    def row_sums(body):
        sums_of = [[up(value) for value in body(i)] for i in range(parts)]
        return [functools.reduce(jnp.add, values) for values in zip(*sums_of)]

    def each(body):
        for i in range(parts):
            body(i)

    def mean_and_inverse(total, squares):
        mean = total / width
        return mean, lax.rsqrt(squares / width - mean * mean + EPS)

    def part_rows(i):
        return pl.ds(i * rows, rows)

    def norm_first(s):
        whole = sums[s].acc

        def resid(i):
            v = sums[s].value(i)
            whole[i, 0:rows] = v
            return v, v * v

        mean, inverse = mean_and_inverse(*row_sums(resid))
        inv1[s] = inverse

        def one(i):
            u = (whole[i, 0:rows] - mean) * inverse
            u1[s, i] = u
            yf[s, me.c, part_rows(i), :] = (u * param(0, i) + param(1, i)).astype(LOW)

        each(one)

    def forward_in(s, k, unit):
        def one(i):
            at = part_rows(i)
            h, slope = gelu_both(dot(wr[0, unit, at, :], yf[s, k]) + pn[2 * unit + me.c, :, 5 + i : 6 + i])
            hf[s, 2 * k + unit, at, :] = h.astype(LOW)
            df[s, 2 * k + unit, at, :] = slope.astype(LOW)

        each(one)

    def forward_out(s, k, sink):
        def one(i):
            at = part_rows(i)
            sink(i, dot(wt[1, 0, at, :], hf[s, 2 * k]) + dot(wt[1, 1, at, :], hf[s, 2 * k + 1]))

        each(one)

    def norm_second(s, shared):
        whole = shared.acc

        def resid(i):
            v = u1[s, i] * param(0, i) + param(1, i) + shared.value(i) + param(2, i)
            whole[i, 0:rows] = v
            return v, v * v

        mean, inverse = mean_and_inverse(*row_sums(resid))

        def unit(i):
            u = (whole[i, 0:rows] - mean) * inverse
            whole[i, 0:rows] = u
            cs[s, i] = (u * param(3, i) + param(4, i)).astype(LOW)
            g = ct[s, i].astype(F32)
            lane_sum(0, i, s, g * u)
            lane_sum(1, i, s, g)
            q = g * param(3, i)
            return q, q * u

        total, cross = row_sums(unit)
        total, cross = total / width, cross / width

        def one(i):
            q = ct[s, i].astype(F32) * param(3, i)
            grad = inverse * (q - total - whole[i, 0:rows] * cross)
            gr2[s, i] = grad
            lane_sum(2, i, s, grad)
            zf[s, me.c, part_rows(i), :] = grad.astype(LOW)

        each(one)

    def backward_in(s, k, fresh):
        for unit in range(2):

            def one(i):
                at = part_rows(i)
                gp = dot(wr[1, unit, at, :], zf[s, k]) * df[s, 2 * k + unit, at, :].astype(F32)
                place = 5 + unit
                lanes[place, i] = folded(gp) if fresh else lanes[place, i] + folded(gp)
                df[s, 2 * k + unit, at, :] = gp.astype(LOW)

            each(one)

    def backward_out(s, k, sink):
        def one(i):
            at = part_rows(i)
            sink(i, dot(wt[0, 0, at, :], df[s, 2 * k]) + dot(wt[0, 1, at, :], df[s, 2 * k + 1]))

        each(one)

    def weight_grad(which, unit, store):
        def one(r, carry):
            at = columns(r, 256)
            for n in range(units // 256):
                cut = slice(n * 256, (n + 1) * 256)
                total = 0.0
                for s in range(slots):
                    for k in range(2):
                        if which == 0:
                            total = total + dot_rows(hf[s, 2 * k + unit, at, :], zf[s, k, cut, :])
                        else:
                            total = total + dot_rows(yf[s, k, at, :], df[s, 2 * k + unit, cut, :])
                store(which, at, cut, total)
            return carry

        lax.fori_loop(0, units // 256, one, 0)

    def norm_first_back(s, shared):
        whole = shared.acc

        def entry(i):
            grad = gr2[s, i] + shared.value(i)
            whole[i, 0:rows] = grad
            u = u1[s, i]
            lane_sum(3, i, s, grad * u)
            lane_sum(4, i, s, grad)
            q = grad * param(0, i)
            return q, q * u

        total, cross = row_sums(entry)
        total, cross = total / width, cross / width

        def one(i):
            q = whole[i, 0:rows] * param(0, i)
            xg[s, me.h, i, 0] = (inv1[s] * (q - total - u1[s, i] * cross)).astype(LOW)

        each(one)

    def to_core(block):
        return links.copy(block, block, me.core)

    outward = [Share(me, links, rows, sc.at[s, 0], rc.at[s, 0], acc.at[s]) for s in range(slots)]
    inward = [Share(me, links, rows, sc.at[s, 1], rc.at[s, 1], acc.at[s]) for s in range(slots)]

    def enter(s):
        sums[s].wait()
        norm_first(s)
        got = to_core(yf.at[s, me.c])
        forward_in(s, me.c, me.x)
        got.wait_recv()
        forward_in(s, 1 - me.c, me.x)

    def leave(s):
        links.settle(sums[s].sent)
        forward_in(s, 1 - me.c, far)
        forward_in(s, me.c, far)
        outward[s].away(functools.partial(forward_out, s))
        outward[s].home(functools.partial(forward_out, s))

    def far_weights(r, carry):
        at = columns(r, 256)
        for n in range(units // 256):
            cut = slice(n * 256, (n + 1) * 256)
            wt[0, far, cut, at] = wr[0, far, at, cut].astype(F32).T.astype(LOW)
            wt[1, far, cut, at] = wr[1, far, at, cut].astype(F32).T.astype(LOW)
        return carry

    enter(0)
    weights.arrive()
    weights.finish()
    direct.wait_recv()
    lax.fori_loop(0, units // 256, far_weights, 0)
    links.settle([by_side, direct] + weights.sent())
    leave(0)
    enter(1)
    leave(1)
    for made in moved:
        made.wait_recv()
    links.settle(moved)
    seconds, outs = [], {}
    for s in range(slots):
        outward[s].wait()
        norm_second(s, outward[s])
        seconds.append(to_core(zf.at[s, me.c]))

    def mix_view(s):
        return lambda t: xg.at[s, t, :, 0]

    def freq_view(s):
        cuts = (pl.ds(0, pad // 32 * 16), pl.ds(pad // 32 * 16, pad - pad // 32 * 16))

        def view(q, half=None):
            return ug.at[s, q] if half is None else ug.at[s, q, cuts[half]]

        return view

    gathers = [GatherHidden(me, links, mix_view(s)) for s in range(slots)]
    spreads = [GatherBatch(me, links, freq_view(s)) for s in range(slots)]
    heavy, chunks = [], []
    for which, whole in ((0, hf), (1, df)):
        low, used = 0, 0
        for size in chunk_rows(units)[which]:
            at, place = pl.ds(low, size), pl.ds(used, landing_rows(size, bits))
            low, used = low + size, used + landing_rows(size, bits)
            chunks.append((which, at))
            heavy.append(
                Reduce(
                    me, links, ORDERS[len(heavy)], wr.at[0, which, at], given.at[which, at], wg.at[which, at], wt.at[1, which, at],
                    landing.at[which, place], whole.at[0, :, at],
                )
            )

    def features(s, t):
        whole = jnp.concatenate([xg[s, t, i, 0] for i in range(parts)], 0)
        ug[s, me.p, :, columns(t, tokens)] = dot(gt[...], whole).astype(LOW)

    def store_given(which, at, cut, value):
        wr[0, which, at, cut] = value.astype(LOW)

    def store_kept(which, at, cut, value):
        wg[which, at, cut] = value

    for made in seconds:
        made.wait_recv()
    links.settle_all()

    def backward(s):
        backward_in(s, me.c, s == 0)
        backward_in(s, 1 - me.c, False)
        inward[s].away(functools.partial(backward_out, s))
        inward[s].home(functools.partial(backward_out, s))

    def first_back(s):
        inward[s].wait()
        norm_first_back(s, inward[s])
        gathers[s].start()

    def near_features(s):
        features(s, me.h)
        gathers[s].by_core.wait_recv()
        features(s, me.hc)

    def far_features(s):
        gathers[s].forward()
        features(s, me.hx)
        gathers[s].by_far.wait_recv()
        features(s, me.hd)
        spreads[s].start()

    ones = jnp.ones((8, 128), F32)

    def lane_total(k, i):
        return lax.dot_general(
            ones, lanes[k, i], (((1,), (1,)), ((), ())), precision=lax.Precision.HIGHEST, preferred_element_type=F32
        )

    row = lax.broadcasted_iota(jnp.int32, (8, rows), 0)
    light = []

    def start_small_sums():
        for i in range(parts):
            packed = jnp.zeros((8, rows), F32)
            for k in range(5):
                packed = jnp.where(row == k, lane_total(k, i), packed)
            lsend[i] = packed
        for unit in range(2):
            packed = jnp.zeros((8, rows), F32)
            for i in range(parts):
                packed = jnp.where(row == i, lane_total(5 + unit, i), packed)
            lbias[unit] = packed
        for to, device in ((me.hc, me.core), (me.hx, me.side), (me.hd, me.cross)):
            light.append(links.copy(lsend.at[to], lrecv.at[me.h], device))
        light.append(links.copy(lbias.at[far], lbias.at[2], me.side))

    sign = jnp.where((me.h == 0) | (me.h == 3), -1.0, 1.0).astype(F32)
    mine = jnp.where(is_cos, 1.0, sign)
    theirs = jnp.where(is_cos, sign, 1.0)
    stored = []

    def sequence(s):
        spreads[s].arrive()
        spreads[s].finish()
        links.settle([outward[s].by_core])

        def one(t):
            at = columns(t, tokens)
            total = None
            for q in range(SPLIT):
                share = dot(ug[s, q], tab[q * piece : (q + 1) * piece, at])
                total = share if total is None else total + share
            acc[s, t] = total
            sc[s, 0, t] = total.astype(LOW)

        loop(parts, one)
        swaps[s] = links.copy(sc.at[s, 0], rc.at[s, 0], me.core)

    swaps, across = {}, {}

    def ordered(s):
        swaps[s].wait_recv()

        def one(t):
            pair = (mine * acc[s, t] + theirs * rc[s, 0, t].astype(F32)).astype(LOW)
            sx[s, t] = dot(order[...], pair).astype(LOW)

        loop(parts, one)
        made = links.describe(sx.at[s], rx.at[s], me.side)
        across[s] = made

        @pl.when(jnp.logical_not(is_cos))
        def _():
            made.start()

    def store_grad(s):
        def store(part):
            def one(t):
                u1[s, t] = part[s, t].astype(F32) + xg[s, t, me.h, 0].astype(F32)

            loop(parts, one)

        @pl.when(is_cos)
        def _():
            store(sx)

        @pl.when(jnp.logical_not(is_cos))
        def _():
            across[s].wait()
            store(rx)

        for t in range(parts):
            stored.append(links.fetch(u1.at[s, t], grad_hbm.at[s, :, pl.ds(t * tokens, tokens)]))

    def start_outs(s):
        og[s, me.h] = cs[s, me.h]
        outs[s] = [
            links.copy(cs.at[s, to], og.at[s, me.h], device)
            for to, device in ((me.hc, me.core), (me.hx, me.side), (me.hd, me.cross))
        ]

    def end_outs(s):
        for made in outs[s]:
            made.wait_recv()
        for t in range(parts):
            gr2[s, t] = og[s, t].astype(F32) * live[s]
            stored.append(links.fetch(gr2.at[s, t], out_hbm.at[s, :, pl.ds(t * tokens, tokens)]))

    def small_sums():
        for made in light:
            made.wait_recv()
        ltot[0, 0:8] = lsend[me.h] + lrecv[me.hc] + lrecv[me.hx] + lrecv[me.hd]
        ltot[0, 8:16] = lbias[me.x] + lbias[2]
        small_round()

    rounds = []

    def small_round():
        k = len(rounds)
        if k:
            rounds[k - 1].wait_recv()
            ltot[k] = ltot[k - 1] + lnext[k - 1]
        if k < bits:
            rounds.append(links.copy(ltot.at[k], lnext.at[k], me.flip[k]))

    def store_chunk(n):
        which, at = chunks[n]
        dst = (wg2_hbm, wg1_hbm)[which].at[at]
        for m in range(heavy[n].blocks):
            stored.append(links.fetch(heavy[n].whole.at[m], dst.at[:, pl.ds(m * tokens, tokens)]))

    def step(n):
        if not heavy[n].step():
            store_chunk(n)
            return False
        return True

    acts = {
        "back": backward,
        "norm": first_back,
        "near": near_features,
        "far": far_features,
        "halves": lambda s: spreads[s].forward(),
        "sequence": sequence,
        "order": ordered,
        "grad": store_grad,
        "give": lambda which: weight_grad(which, far, store_given),
        "keep": lambda which: weight_grad(which, me.x, store_kept),
        "pack": lambda _: start_small_sums(),
        "small": lambda _: small_sums(),
        "round": lambda _: small_round(),
        "outs": start_outs,
        "ends": end_outs,
        "chunk": lambda n: step(n),
    }
    going = [True] * len(heavy)
    gt_in.wait()
    order_in.wait()
    for kind, n in SCHEDULE:
        did = acts[kind](n)
        if kind == "chunk":
            going[n] = did
    while any(going):
        for n in range(len(heavy)):
            going[n] = going[n] and step(n)
        if len(rounds) < bits:
            small_round()
    while len(rounds) < bits:
        small_round()
    k = bits - 1
    if len(rounds) == bits:
        rounds[k].wait_recv()
        ltot[bits] = ltot[k] + lnext[k]
    light_ref[...] = ltot[bits, 0:8]
    for i in range(parts):
        flat[:, i * rows : (i + 1) * rows] = ltot[bits, 8 + i : 9 + i]
    for r in range(units // 128):
        bias_ref[r : r + 1, :] = flat[:, r * 128 : (r + 1) * 128]
    for made in stored:
        made.wait()
    links.settle_all()


def local(
    n_batch,
    layer_input,
    gain_first,
    shift_first,
    weight_in,
    bias_in,
    weight_out,
    bias_out,
    gain_second,
    shift_second,
    cotangent,
    live_counts,
):
    slots, rows, piece = layer_input.shape
    width = rows * HOLD
    tokens = piece // HOLD
    units = weight_in.shape[1]
    length = piece * SPLIT
    pad = rows + 16
    bits = n_batch.bit_length() - 1
    vectors = (gain_first, shift_first, bias_out, gain_second, shift_second, bias_in)
    small = sequence_tables(length, SPLIT)
    forward, backward, order = feature_tables(width, HOLD)
    any_, vmem = pl.BlockSpec(memory_space=pl.ANY), pl.BlockSpec(memory_space=pltpu.VMEM)
    block = (HOLD, rows, tokens)
    padded = (HOLD, pad, tokens)
    shard = (slots,) + block
    landing = max(sum(landing_rows(size, bits) for size in sizes) for sizes in chunk_rows(units))
    scratch = [
        ((length, piece), LOW), ((4, FINE, piece), F32), (forward.shape[1:], LOW), (backward.shape[1:], LOW),
        (order.shape[1:], LOW), ((slots, SPLIT, HOLD, 2, rows, tokens), LOW), (shard, LOW), (shard, LOW), (shard, LOW),
        ((2, 2 * rows, tokens), LOW), ((slots, 2) + padded, LOW), ((slots, 2) + padded, LOW), (shard, LOW), (shard, LOW),
        ((slots,) + padded, F32), ((slots, 2, width, tokens), LOW), ((slots, 4, units, tokens), LOW),
        ((slots, 4, units, tokens), LOW), ((slots, 2, width, tokens), LOW), (shard, F32), (shard, F32),
        ((slots, 1, tokens), F32), ((7, HOLD, rows, 128), F32),
        ((2, 2, units, width), LOW), ((2, 2, width, units), LOW), ((2, units, width), F32),
        ((2, units, width), LOW), ((2, landing, width), LOW),
        ((slots, SPLIT, pad, piece), LOW), ((1, units), F32), ((16, 256), F32), ((HOLD, 16, 256), F32), ((HOLD, rows, 128), F32), ((HOLD, 8, rows), F32),
        ((HOLD, 8, rows), F32), ((3, 8, rows), F32), ((bits + 1, 16, rows), F32), ((bits, 16, rows), F32),
    ]
    outs = [
        (layer_input.shape, F32), (layer_input.shape, F32), ((width, units), LOW), ((units, width), LOW),
        ((8, rows), F32), ((units // 128, 128), F32),
    ]
    out, grad, wg1, wg2, light, bias = pl.pallas_call(
        functools.partial(layer_kernel, bits),
        name="layer",
        out_shape=[jax.ShapeDtypeStruct(shape, kind) for shape, kind in outs],
        in_specs=[any_] * 8 + [vmem] * 6 + [pl.BlockSpec(memory_space=pltpu.SMEM)],
        out_specs=[any_] * 4 + [vmem] * 2,
        scratch_shapes=[pltpu.VMEM(shape, kind) for shape, kind in scratch]
        + [pltpu.SemaphoreType.DMA((count,)) for count in semaphores(bits)],
        compiler_params=pltpu.CompilerParams(
            collective_id=1, has_side_effects=True, vmem_limit_bytes=VMEM_LIMIT
        ),
    )(
        layer_input, cotangent, weight_in, weight_out, jnp.asarray(small), jnp.asarray(forward),
        jnp.asarray(backward), jnp.asarray(order), *(v.reshape(1, -1) for v in vectors[:5]), bias_in.reshape(-1, 128), live_counts,
    )
    return (
        out, grad, light[3], light[4], wg1.astype(F32), bias.reshape(units), wg2.astype(F32),
        light[2], light[0], light[1],
    )


def solution(mesh):
    return jax.shard_map(
        functools.partial(local, mesh.shape["batch"]),
        mesh=mesh,
        in_specs=(
            P(None, "hidden", "batch"),
            P("hidden"),
            P("hidden"),
            P(None, "hidden"),
            P("hidden"),
            P("hidden", None),
            P("hidden"),
            P("hidden"),
            P("hidden"),
            P(None, "hidden", "batch"),
            P("batch"),
        ),
        out_specs=(
            P(None, "hidden", "batch"),
            P(None, "hidden", "batch"),
            P("hidden"),
            P("hidden"),
            P(None, "hidden"),
            P("hidden"),
            P("hidden", None),
            P("hidden"),
            P("hidden"),
            P("hidden"),
        ),
        check_vma=False,
    )
```

```python
import functools
import math

import jax
import jax.numpy as jnp
import ml_dtypes
import numpy as np
from jax import lax
from jax.experimental import pallas as pl
from jax.experimental.pallas import tpu as pltpu
from jax.sharding import PartitionSpec as P

SPLIT = 4
HOLD = 4
EPS = 1e-06
FINE = 64
LOW = jnp.bfloat16
F32 = jnp.float32
MESH = pl.DeviceIdType.MESH
VMEM_LIMIT = 63 * 2**20


def dot(left, right):
    return jnp.dot(left, right, preferred_element_type=F32)


def dot_rows(left, right):
    return lax.dot_general(left, right, (((1,), (1,)), ((), ())), preferred_element_type=F32)


@functools.cache
def sequence_tables(length, split):
    column = np.arange(length)
    coarse = 2 * np.pi * ((FINE * np.arange(length // FINE)[:, None] * column) % length) / length
    fine = 2 * np.pi * ((np.arange(FINE)[:, None] * column) % length) / length
    factor = 1 / math.sqrt(length)
    whole = np.stack([np.cos(coarse), np.sin(coarse), factor * np.cos(fine), factor * np.sin(fine)])
    return np.ascontiguousarray(
        whole.reshape(4, FINE, split, length // split).transpose(2, 0, 1, 3).astype(np.float32)
    )


@functools.cache
def feature_tables(width, parts):
    index = np.arange(width)
    angle = 2 * np.pi * ((index[:, None] * index) % width) / width
    factor = 1 / math.sqrt(width)
    cos = (np.cos(angle) * factor).astype(np.float32).astype(ml_dtypes.bfloat16)
    sin = (np.sin(angle) * factor).astype(np.float32).astype(ml_dtypes.bfloat16)
    part = width // parts
    pad = part + 16
    forward = np.zeros((parts, parts, part, 2 * part), ml_dtypes.bfloat16)
    backward = np.zeros((parts, pad, width), ml_dtypes.bfloat16)
    order = np.zeros((parts, part, pad), ml_dtypes.bfloat16)
    for h in range(parts):
        chip = slice((h // 2) * 2 * part, (h // 2 + 1) * 2 * part)
        forward[h] = (cos if h % 2 == 0 else -sin)[:, chip].reshape(parts, part, 2 * part)
        first = (h // 2) * part
        backward[h, : part + 1] = (cos, sin)[h % 2][first : first + part + 1]
        for i in range(part):
            order[h, i, i if h in (0, 3) else part - i] = 1
    return forward, backward, order


class Place:
    def __init__(self, bits):
        h = lax.axis_index("hidden")
        b = lax.axis_index("batch")
        self.h, self.b = h, b
        self.c = lax.rem(h, 2)
        self.x = lax.div(h, 2)
        self.hc = h + 1 - 2 * self.c
        self.hx = lax.rem(h + 2, 4)
        self.hd = lax.rem(self.hc + 2, 4)
        self.p = lax.rem(b, 4)
        self.bit = [lax.rem(lax.div(b, 2**k), 2) for k in range(bits)]
        self.py = self.p + 1 - 2 * self.bit[0]
        self.pz = lax.rem(self.p + 2, 4)
        self.pd = lax.rem(self.py + 2, 4)
        self.core = {"hidden": self.hc}
        self.side = {"hidden": self.hx}
        self.cross = {"hidden": self.hd}
        self.flip = [{"batch": b + 2**k - 2 ** (k + 1) * self.bit[k]} for k in range(bits)]
        self.ydev, self.zdev = self.flip[:2]


class Fetch:
    def __init__(self, made, place, free):
        self.made, self.place, self.free = made, place, free

    def wait(self):
        self.made.wait()
        self.free.append(self.place)


class Links:
    def __init__(self, send, recv, near):
        self.send, self.recv, self.near = send, recv, near
        self.used, self.sends, self.fetched = 0, 0, 0
        self.free_sends, self.free_near, self.open = [], [], []

    def describe(self, src, dst, device):
        i = self.used
        self.used += 1
        if not self.free_sends:
            self.free_sends.append(self.sends)
            self.sends += 1
        self.place = self.free_sends.pop()
        return pltpu.make_async_remote_copy(
            src_ref=src,
            dst_ref=dst,
            send_sem=self.send.at[self.place],
            recv_sem=self.recv.at[i],
            device_id=device,
            device_id_type=MESH,
        )

    def copy(self, src, dst, device):
        made = self.describe(src, dst, device)
        made.start()
        self.open.append((made, self.place))
        return made

    def settle(self, some):
        for made in some:
            for entry in self.open:
                if entry[0] is made:
                    made.wait_send()
                    self.free_sends.append(entry[1])
            self.open = [entry for entry in self.open if entry[0] is not made]

    def settle_all(self):
        self.settle([made for made, _ in self.open])

    def fetch(self, src, dst):
        if not self.free_near:
            self.free_near.append(self.fetched)
            self.fetched += 1
        place = self.free_near.pop()
        made = Fetch(pltpu.make_async_copy(src, dst, self.near.at[place]), place, self.free_near)
        made.made.start()
        return made


def semaphores(bits):
    return (47, 143, 34) if bits == 3 else (160, 192, 64)


def greet(devices):
    barrier = pltpu.get_barrier_semaphore()
    for device in devices:
        pl.semaphore_signal(barrier, inc=1, device_id=device, device_id_type=MESH)
    pl.semaphore_wait(barrier, len(devices))


class GatherHidden:
    def __init__(self, me, links, view):
        self.me, self.links, self.view = me, links, view

    def start(self):
        own = self.view(self.me.h)
        self.by_side = self.links.copy(own, own, self.me.side)
        self.by_core = self.links.copy(own, own, self.me.core)

    def forward(self):
        self.by_side.wait_recv()
        far = self.view(self.me.hx)
        self.by_far = self.links.copy(far, far, self.me.core)


class GatherBatch:
    def __init__(self, me, links, view):
        self.me, self.links, self.view = me, links, view

    def start(self):
        ends = ((0, self.me.ydev), (1, self.me.zdev), (1, self.me.ydev), (0, self.me.zdev))
        own = [self.view(self.me.p, 0), self.view(self.me.p, 1)]
        self.y0, self.z1, self.y1, self.z0 = (self.links.copy(own[n], own[n], device) for n, device in ends)

    def forward(self):
        self.y0.wait_recv()
        part = self.view(self.me.py, 0)
        self.on_z = self.links.copy(part, part, self.me.zdev)
        self.z1.wait_recv()
        part = self.view(self.me.pz, 1)
        self.on_y = self.links.copy(part, part, self.me.ydev)

    def arrive(self):
        self.y1.wait_recv()
        self.z0.wait_recv()

    def finish(self):
        self.on_z.wait_recv()
        self.on_y.wait_recv()

    def sent(self):
        return [self.y0, self.y1, self.z0, self.z1, self.on_y, self.on_z]


class Scatter:
    def __init__(self, me, links, rows, sc, rc, sx, rx, acc):
        self.me, self.links, self.rows, self.sent = me, links, rows, []
        self.sc, self.rc, self.sx, self.rx, self.acc = sc, rc, sx, rx, acc

    def run(self, prepare, block, hook, early=False):
        x, c, cut = self.me.x, self.me.c, pl.ds(0, self.rows)
        for n, start in enumerate((2 * (1 - x), 2 * x)):
            away, home = start + 1 - c, start + c

            def send(i, value):
                self.sc[n, i, cut] = value.astype(LOW)

            def keep(i, value):
                value = value + self.rc[n, i, cut].astype(F32)
                if n == 0:
                    self.sx[i] = value.astype(LOW)
                else:
                    self.acc[i, cut] = value

            prepare(0, away)
            block(0, away, send)
            by_core = self.links.copy(self.sc.at[n, :, cut], self.rc.at[n, :, cut], self.me.core)
            self.sent.append(by_core)
            prepare(1, home)
            if n == 0 and early:
                hook()
            by_core.wait_recv()
            block(1, home, keep)
            if n == 0:
                self.by_side = self.links.copy(self.sx, self.rx, self.me.side)
                self.sent.append(self.by_side)
                if not early:
                    hook()

    def wait(self):
        self.by_side.wait_recv()

    def value(self, i):
        return self.acc[i, 0 : self.rows] + self.rx[i].astype(F32)


class Share:
    def __init__(self, me, links, rows, sc, rc, acc):
        self.me, self.links, self.cut = me, links, pl.ds(0, rows)
        self.sc, self.rc, self.acc = sc, rc, acc

    def away(self, block):
        def sink(i, value):
            self.sc[i, self.cut] = value.astype(LOW)

        block(1 - self.me.c, sink)
        self.by_core = self.links.copy(self.sc.at[:, self.cut], self.rc.at[:, self.cut], self.me.core)

    def home(self, block):
        def sink(i, value):
            self.acc[i, self.cut] = value

        block(self.me.c, sink)

    def wait(self):
        self.by_core.wait_recv()

    def value(self, i):
        return self.acc[i, self.cut] + self.rc[i, self.cut].astype(F32)


class Reduce:
    def __init__(self, me, links, order, given, given_landing, total, low, landing, whole):
        self.me, self.links, self.order = me, links, order
        self.given, self.given_landing = given, given_landing
        self.total, self.low, self.landing, self.whole = total, low, landing, whole
        self.blocks = total.shape[1] // whole.shape[2]
        bits, size = len(me.bit), total.shape[0]
        kinds = {"x": self.cross, "y": self.halve, "z": self.quarter}
        self.plan = [(kinds[axis], 0) for axis in order]
        more = extra_halvings(size, bits)
        self.plan += [(self.halve, k) for k in range(3, 3 + more)]
        self.plan += [(self.double, k) for k in range(3 + more, bits)]
        back = [(self.gather_half, k) for k in reversed(range(3, 3 + more))]
        back += [({"y": self.gather_half, "z": self.gather_quarters}[axis], 0) for axis in reversed(order) if axis != "x"]
        self.plan += back
        self.first_back = len(self.plan) - len(back)
        self.doubled = bits > 3 + more
        self.at, self.used, self.spans, self.crossed, self.after = 0, 0, [(0, size)], False, None

    def span(self, first, size):
        return pl.ds(pl.multiple_of(first, 16), size)

    def end(self):
        if self.after is not None:
            self.after()
            self.after = None

    def step(self):
        self.end()
        if self.at == len(self.plan):
            return False
        if self.at == self.first_back:
            mine, wide = self.span(*self.spans[-1]), self.whole.shape[2]
            own = self.low if self.doubled else self.total
            for n in range(self.blocks):
                self.whole[n, mine, :] = own[mine, n * wide : (n + 1) * wide].astype(LOW)
        kind, k = self.plan[self.at]
        self.at += 1
        kind(k)
        return True

    def land(self, size):
        self.used += size
        return pl.ds(self.used - size, size)

    def add(self, made, mine, place):
        made.wait_recv()
        self.add_rows(mine, self.landing, place.start)
        self.links.settle([made])

    def add_rows(self, mine, landing, start):
        def some(at, i, step):
            self.total[pl.ds(at, step), :] += landing[pl.ds(start + i, step), :].astype(F32)

        by_rows(mine.start, mine.size, some)

    def send(self, first, size, device):
        give, place = self.span(first, size), self.land(size)

        def some(at, i, step):
            self.low[pl.ds(at, step), :] = self.total[pl.ds(at, step), :].astype(LOW)

        by_rows(first, size, some)
        return self.links.copy(self.low.at[give], self.landing.at[place], device), place

    def cross(self, _):
        first, size = self.spans[-1]
        mine, place = self.span(first, size), pl.ds(self.given.shape[0] - size, size)
        made = self.links.copy(self.given.at[mine], self.given_landing.at[place], self.me.side)
        self.crossed = True

        def after():
            made.wait_recv()
            self.add_rows(mine, self.given_landing, place.start)
            self.links.settle([made])

        self.after = after

    def halve(self, k):
        first, size = self.spans[-1]
        half, u = size // 2, self.me.bit[k]
        keep, away = first + u * half, first + (1 - u) * half
        mine = self.span(keep, half)
        self.spans.append((keep, half))
        far = None
        if not self.crossed:
            far = self.links.copy(self.given.at[self.span(away, half)], self.given_landing.at[pl.ds(0, half)], self.me.flip[k])
        made, place = self.send(away, half, self.me.flip[k])

        def after():
            if far is not None:
                far.wait_recv()

                def some(at, i, step):
                    rows = pl.ds(at, step)
                    total = self.given[rows, :].astype(F32) + self.given_landing[pl.ds(i, step), :].astype(F32)
                    self.given[rows, :] = total.astype(LOW)

                by_rows(keep, half, some)
                self.links.settle([far])
            self.add(made, mine, place)

        self.after = after

    def column(self, d):
        v = self.me.bit[1] + 2 * self.me.bit[2]
        w = lax.rem(v + d, 4)
        return w, {"batch": self.me.b + 2 * (w - v)}

    def quarter(self, _):
        first, size = self.spans[-1]
        part = size // 4
        keep = first + (self.me.bit[1] + 2 * self.me.bit[2]) * part
        self.spans.append((keep, part))
        made = []
        for d in (2, 1, 3):
            w, device = self.column(d)
            made.append(self.send(first + w * part, part, device))

        def after():
            for one, place in made:
                self.add(one, self.span(keep, part), place)

        self.after = after

    def double(self, k):
        mine = self.span(*self.spans[-1])
        place = self.land(self.spans[-1][1])
        if self.plan[self.at - 2][0] != self.double:
            self.low[mine, :] = self.total[mine, :].astype(LOW)
        made = self.links.copy(self.low.at[mine], self.landing.at[place], self.me.flip[k])

        def after():
            made.wait_recv()
            self.links.settle([made])
            self.low[mine, :] = (self.low[mine, :].astype(F32) + self.landing[place, :].astype(F32)).astype(LOW)

        self.after = after

    def gather(self, devices):
        part = self.whole.at[pl.ds(0, self.blocks), self.span(*self.spans.pop())]
        made = [self.links.copy(part, part, device) for device in devices]

        def after():
            for one in made:
                one.wait_recv()
            self.links.settle(made)

        self.after = after

    def gather_half(self, k):
        self.gather([self.me.flip[k]])

    def gather_quarters(self, _):
        self.gather([self.column(d)[1] for d in (2, 1, 3)])


def extra_halvings(size, bits):
    count, left = 0, size // 8
    while 3 + count < bits and (left // 2) % 16 == 0:
        count, left = count + 1, left // 2
    return count


def landing_rows(size, bits):
    more, left = extra_halvings(size, bits), size // 8
    return 7 * left + sum(left >> (k + 1) for k in range(more)) + (bits - 3 - more) * (left >> more)


def chunk_rows(units):
    third = units // 3
    return (third,) * 3, (third,) * 3


def columns(t, size):
    return pl.ds(pl.multiple_of(t * size, size), size)


def loop(count, body):
    def one(i, carry):
        body(i)
        return carry

    lax.fori_loop(0, count, one, 0)


def by_rows(first, size, body):
    step = min(size, 32)

    def one(i):
        body(pl.multiple_of(first + i * step, 16), pl.multiple_of(i * step, 16), step)

    loop(size // step, one)


ROOT = math.sqrt(2 / math.pi)
CUBE = 0.044715


def gelu_both(v):
    square = v * v
    t = jnp.tanh(v * (ROOT + ROOT * CUBE * square))
    half = 0.5 + 0.5 * t
    slope = half + (0.5 * v) * (1 - t * t) * (ROOT + 3 * ROOT * CUBE * square)
    return v * half, slope


def up(value):
    return jnp.sum(value, 0, keepdims=True)


SCHEDULE = (
    ("give", 0), ("chunk", 1), ("keep", 0), ("chunk", 2), ("back", 0), ("back", 1), ("norm", 0), ("give", 1),
    ("keep", 1), ("chunk", 5), ("chunk", 3), ("chunk", 2), ("chunk", 1), ("near", 0), ("far", 0), ("halves", 0),
    ("chunk", 3), ("chunk", 5), ("norm", 1), ("chunk", 4), ("chunk", 2), ("pack", 0), ("chunk", 5), ("chunk", 2),
    ("near", 1), ("chunk", 0), ("chunk", 3), ("chunk", 5), ("far", 1), ("chunk", 4), ("outs", 1), ("chunk", 0),
    ("chunk", 3), ("small", 0), ("outs", 0), ("sequence", 0), ("order", 0), ("chunk", 2), ("chunk", 4), ("chunk", 1),
    ("ends", 1), ("chunk", 0), ("halves", 1), ("chunk", 5), ("chunk", 4), ("chunk", 1), ("chunk", 3), ("chunk", 0),
    ("chunk", 2), ("chunk", 5), ("round", 0), ("chunk", 1), ("ends", 0), ("chunk", 4), ("sequence", 1), ("order", 1),
    ("chunk", 0), ("grad", 0), ("round", 0), ("chunk", 4), ("chunk", 3), ("grad", 1), ("chunk", 0), ("chunk", 1),
)
ORDERS = ("xyz", "xzy", "yxz", "xyz", "yxz", "yxz")


def layer_kernel(
    bits,
    x_hbm, cot_hbm, w1_hbm, w2_hbm, small_hbm, ht_hbm, gt_hbm, order_hbm,
    g1_ref, s1_ref, bo_ref, g2_ref, s2_ref, bin_ref, live_ref,
    out_hbm, grad_hbm, wg1_hbm, wg2_hbm, light_ref, bias_ref,
    tab, small, ht, gt, order, xg, cs, ct, og, ab, sc, rc, sx, rx, acc, yf, hf, df, zf, u1, gr2, inv1, lanes,
    wr, wt, wg, given, landing, ug, flat, rowv, rows_in, pn, lsend, lrecv, lbias, ltot, lnext, send, recv, near,
):
    slots, _, piece = x_hbm.shape
    parts, rows, tokens = cs.shape[1:]
    width = parts * rows
    units = wg.shape[1]
    pad = gt.shape[0]
    me = Place(bits)
    links = Links(send, recv, near)
    is_cos = me.c == 0
    live = [jnp.where(live_ref[0] > s, 1.0, 0.0).astype(F32) for s in range(slots)]

    def fetch_tokens(src, dst, s):
        return [links.fetch(src.at[s, :, pl.ds(t * tokens, tokens)], dst.at[s, t]) for t in range(parts)]

    x_in = [fetch_tokens(x_hbm, u1, s) for s in range(slots)]
    w1_in, w2_in = links.fetch(w1_hbm, wg.at[0]), links.fetch(w2_hbm, wg.at[1])
    small_in = links.fetch(small_hbm.at[me.p], small)
    cot_in = [fetch_tokens(cot_hbm, gr2, s) for s in range(slots)]
    ht_in = links.fetch(ht_hbm.at[me.h], ht)
    gt_in = links.fetch(gt_hbm.at[me.h], gt)
    order_in = links.fetch(order_hbm.at[me.h], order)
    greet([me.core, me.side, me.cross] + me.flip)

    def input_view(s):
        def view(q, half=None):
            return xg.at[s, q, slice(None) if half is None else pl.ds(half * 2, 2), me.c]

        return view

    spread = [GatherBatch(me, links, input_view(s)) for s in range(slots)]
    over = [[] for _ in range(slots)]

    def hand_over(s, q):
        block = input_view(s)(q)
        over[s].append(links.copy(block, block, me.core))

    for s in range(slots):
        for t in range(parts):
            x_in[s][t].wait()
            xg[s, me.p, t, me.c] = u1[s, t].astype(LOW)
        if s == 0:
            spread[0].start()
        hand_over(s, me.p)

    far = 1 - me.x
    quarter, straight = units // SPLIT, width - 128

    def weight_view(q, half=None):
        at = pl.ds(pl.multiple_of(q * quarter, 16), quarter)
        return wr.at[slice(None) if half is None else pl.ds(half, 1), far, at, pl.ds(0, straight)]

    weights = GatherBatch(me, links, weight_view)
    w1_in.wait()
    w2_in.wait()

    def own_weights(r, carry):
        at = columns(r, 256)
        for n in range(units // 256):
            cut = slice(n * 256, (n + 1) * 256)
            first, second = wg[0, at, cut], wg[1, at, cut]
            wt[0, me.x, at, cut] = first.astype(LOW)
            wr[0, me.x, cut, at] = first.T.astype(LOW)
            wr[1, me.x, at, cut] = second.astype(LOW)
            wt[1, me.x, cut, at] = second.T.astype(LOW)
        return carry

    lax.fori_loop(0, units // 256, own_weights, 0)
    quarter_at = pl.ds(pl.multiple_of(me.p * quarter, 16), quarter)
    mine_w = wr.at[:, me.x, quarter_at, pl.ds(0, straight)]
    by_side = links.copy(mine_w, mine_w, me.side)
    mine_w = wr.at[:, me.x, :, pl.ds(straight, 128)]
    direct = links.copy(mine_w, mine_w, me.side)

    vectors = (g1_ref, s1_ref, bo_ref, g2_ref, s2_ref)
    rowv[...] = jnp.zeros_like(rowv)
    for r in range(units // 128):
        flat[:, r * 128 : (r + 1) * 128] = bin_ref[r : r + 1, :]
    for k, ref in enumerate(vectors):
        rowv[k : k + 1, 0:rows] = ref[...]
    for i in range(parts):
        rowv[5 + i : 6 + i, 0:rows] = flat[:, i * rows : (i + 1) * rows]
    params = [links.copy(rowv, rows_in.at[me.h], device) for device in (me.core, me.side, me.cross)]

    small_in.wait()

    def make_rows(i, carry):
        big_cos, big_sin = small[0, pl.ds(i, 1), :], small[1, pl.ds(i, 1), :]
        by_cos = jnp.where(is_cos, big_cos, big_sin)
        by_sin = jnp.where(is_cos, -big_sin, big_cos)
        at = pl.ds(pl.multiple_of(i * FINE, FINE), FINE)
        for n in range(piece // 256):
            cut = slice(n * 256, (n + 1) * 256)
            tab[at, cut] = (by_cos[:, cut] * small[2, :, cut] + by_sin[:, cut] * small[3, :, cut]).astype(LOW)
        return carry

    lax.fori_loop(0, FINE, make_rows, 0)
    spread[0].forward()
    spread[1].start()
    for s in range(slots):
        for t in range(parts):
            cot_in[s][t].wait()
            cs[s, t] = (gr2[s, t] * live[s]).astype(LOW)
        ct[s, me.h] = cs[s, me.h]
    ht_in.wait()

    sums = [
        Scatter(me, links, rows, sc.at[s], rc.at[s], sx.at[s], rx.at[s], acc.at[s]) for s in range(slots)
    ]

    def prepare(s, j, t):
        at = columns(t, tokens)
        total = None
        for q in range(SPLIT):
            for n in range(parts):
                first = q * piece + n * tokens
                share = dot(xg[s, q, n].reshape(2 * rows, tokens), tab[first : first + tokens, at])
                total = share if total is None else total + share
        ab[j] = total.astype(LOW)

    def transform(s, j, t, sink):
        def one(i):
            own = jnp.where(me.h == i, 1.0, 0.0).astype(F32)
            sink(i, dot(ht[i], ab[j]) + own * u1[s, t])

        loop(parts, one)

    moved = []

    def next_input():
        spread[1].forward()
        by_side.wait_recv()
        weights.start()

    def next_weights():
        weights.forward()

    for s, hook in enumerate((next_input, next_weights)):
        spread[s].arrive()
        hand_over(s, me.py)
        hand_over(s, me.pz)
        spread[s].finish()
        hand_over(s, me.pd)
        for made in over[s]:
            made.wait_recv()
        sums[s].run(functools.partial(prepare, s), functools.partial(transform, s), hook, early=s == 0)
        for to, device in ((me.hc, me.core), (me.hx, me.side), (me.hd, me.cross)):
            moved.append(links.copy(cs.at[s, to], ct.at[s, me.h], device))
        links.settle(over[s] + spread[s].sent())
    for made in params:
        made.wait_recv()
    rows_in[me.h] = rowv[...]
    square = jnp.zeros((128 - rowv.shape[0], rowv.shape[1]), F32)
    for i in range(parts):
        pn[i] = jnp.concatenate([rows_in[i], square], 0).T[0:rows, :]

    def param(k, i):
        return pn[i, :, k : k + 1]

    def folded(value):
        return value[:, :128] + value[:, 128:]

    def lane_sum(k, i, s, value):
        lanes[k, i] = folded(value) if s == 0 else lanes[k, i] + folded(value)

    def row_sums(body):
        sums_of = [[up(value) for value in body(i)] for i in range(parts)]
        return [functools.reduce(jnp.add, values) for values in zip(*sums_of)]

    def each(body):
        for i in range(parts):
            body(i)

    def mean_and_inverse(total, squares):
        mean = total / width
        return mean, lax.rsqrt(squares / width - mean * mean + EPS)

    def part_rows(i):
        return pl.ds(i * rows, rows)

    def norm_first(s):
        whole = sums[s].acc

        def resid(i):
            v = sums[s].value(i)
            whole[i, 0:rows] = v
            return v, v * v

        mean, inverse = mean_and_inverse(*row_sums(resid))
        inv1[s] = inverse

        def one(i):
            u = (whole[i, 0:rows] - mean) * inverse
            u1[s, i] = u
            yf[s, me.c, part_rows(i), :] = (u * param(0, i) + param(1, i)).astype(LOW)

        each(one)

    def forward_in(s, k, unit):
        def one(i):
            at = part_rows(i)
            h, slope = gelu_both(dot(wr[0, unit, at, :], yf[s, k]) + pn[2 * unit + me.c, :, 5 + i : 6 + i])
            hf[s, 2 * k + unit, at, :] = h.astype(LOW)
            df[s, 2 * k + unit, at, :] = slope.astype(LOW)

        each(one)

    def forward_out(s, k, sink):
        def one(i):
            at = part_rows(i)
            sink(i, dot(wt[1, 0, at, :], hf[s, 2 * k]) + dot(wt[1, 1, at, :], hf[s, 2 * k + 1]))

        each(one)

    def norm_second(s, shared):
        whole = shared.acc

        def resid(i):
            v = u1[s, i] * param(0, i) + param(1, i) + shared.value(i) + param(2, i)
            whole[i, 0:rows] = v
            return v, v * v

        mean, inverse = mean_and_inverse(*row_sums(resid))

        def unit(i):
            u = (whole[i, 0:rows] - mean) * inverse
            whole[i, 0:rows] = u
            cs[s, i] = (u * param(3, i) + param(4, i)).astype(LOW)
            g = ct[s, i].astype(F32)
            lane_sum(0, i, s, g * u)
            lane_sum(1, i, s, g)
            q = g * param(3, i)
            return q, q * u

        total, cross = row_sums(unit)
        total, cross = total / width, cross / width

        def one(i):
            q = ct[s, i].astype(F32) * param(3, i)
            grad = inverse * (q - total - whole[i, 0:rows] * cross)
            gr2[s, i] = grad
            lane_sum(2, i, s, grad)
            zf[s, me.c, part_rows(i), :] = grad.astype(LOW)

        each(one)

    def backward_in(s, k, fresh):
        for unit in range(2):

            def one(i):
                at = part_rows(i)
                gp = dot(wr[1, unit, at, :], zf[s, k]) * df[s, 2 * k + unit, at, :].astype(F32)
                place = 5 + unit
                lanes[place, i] = folded(gp) if fresh else lanes[place, i] + folded(gp)
                df[s, 2 * k + unit, at, :] = gp.astype(LOW)

            each(one)

    def backward_out(s, k, sink):
        def one(i):
            at = part_rows(i)
            sink(i, dot(wt[0, 0, at, :], df[s, 2 * k]) + dot(wt[0, 1, at, :], df[s, 2 * k + 1]))

        each(one)

    def weight_grad(which, unit, store):
        def one(r, carry):
            at = columns(r, 256)
            for n in range(units // 256):
                cut = slice(n * 256, (n + 1) * 256)
                total = 0.0
                for s in range(slots):
                    for k in range(2):
                        if which == 0:
                            total = total + dot_rows(hf[s, 2 * k + unit, at, :], zf[s, k, cut, :])
                        else:
                            total = total + dot_rows(yf[s, k, at, :], df[s, 2 * k + unit, cut, :])
                store(which, at, cut, total)
            return carry

        lax.fori_loop(0, units // 256, one, 0)

    def norm_first_back(s, shared):
        whole = shared.acc

        def entry(i):
            grad = gr2[s, i] + shared.value(i)
            whole[i, 0:rows] = grad
            u = u1[s, i]
            lane_sum(3, i, s, grad * u)
            lane_sum(4, i, s, grad)
            q = grad * param(0, i)
            return q, q * u

        total, cross = row_sums(entry)
        total, cross = total / width, cross / width

        def one(i):
            q = whole[i, 0:rows] * param(0, i)
            xg[s, me.h, i, 0] = (inv1[s] * (q - total - u1[s, i] * cross)).astype(LOW)

        each(one)

    def to_core(block):
        return links.copy(block, block, me.core)

    outward = [Share(me, links, rows, sc.at[s, 0], rc.at[s, 0], acc.at[s]) for s in range(slots)]
    inward = [Share(me, links, rows, sc.at[s, 1], rc.at[s, 1], acc.at[s]) for s in range(slots)]

    def enter(s):
        sums[s].wait()
        norm_first(s)
        got = to_core(yf.at[s, me.c])
        forward_in(s, me.c, me.x)
        got.wait_recv()
        forward_in(s, 1 - me.c, me.x)

    def leave(s):
        links.settle(sums[s].sent)
        forward_in(s, 1 - me.c, far)
        forward_in(s, me.c, far)
        outward[s].away(functools.partial(forward_out, s))
        outward[s].home(functools.partial(forward_out, s))

    def far_weights(r, carry):
        at = columns(r, 256)
        for n in range(units // 256):
            cut = slice(n * 256, (n + 1) * 256)
            wt[0, far, cut, at] = wr[0, far, at, cut].astype(F32).T.astype(LOW)
            wt[1, far, cut, at] = wr[1, far, at, cut].astype(F32).T.astype(LOW)
        return carry

    enter(0)
    weights.arrive()
    weights.finish()
    direct.wait_recv()
    lax.fori_loop(0, units // 256, far_weights, 0)
    links.settle([by_side, direct] + weights.sent())
    leave(0)
    enter(1)
    leave(1)
    for made in moved:
        made.wait_recv()
    links.settle(moved)
    seconds, outs = [], {}
    for s in range(slots):
        outward[s].wait()
        norm_second(s, outward[s])
        seconds.append(to_core(zf.at[s, me.c]))

    def mix_view(s):
        return lambda t: xg.at[s, t, :, 0]

    def freq_view(s):
        cuts = (pl.ds(0, pad // 32 * 16), pl.ds(pad // 32 * 16, pad - pad // 32 * 16))

        def view(q, half=None):
            return ug.at[s, q] if half is None else ug.at[s, q, cuts[half]]

        return view

    gathers = [GatherHidden(me, links, mix_view(s)) for s in range(slots)]
    spreads = [GatherBatch(me, links, freq_view(s)) for s in range(slots)]
    heavy, chunks = [], []
    for which, whole in ((0, hf), (1, df)):
        low, used = 0, 0
        for size in chunk_rows(units)[which]:
            at, place = pl.ds(low, size), pl.ds(used, landing_rows(size, bits))
            low, used = low + size, used + landing_rows(size, bits)
            chunks.append((which, at))
            heavy.append(
                Reduce(
                    me, links, ORDERS[len(heavy)], wr.at[0, which, at], given.at[which, at], wg.at[which, at], wt.at[1, which, at],
                    landing.at[which, place], whole.at[0, :, at],
                )
            )

    def features(s, t):
        whole = jnp.concatenate([xg[s, t, i, 0] for i in range(parts)], 0)
        ug[s, me.p, :, columns(t, tokens)] = dot(gt[...], whole).astype(LOW)

    def store_given(which, at, cut, value):
        wr[0, which, at, cut] = value.astype(LOW)

    def store_kept(which, at, cut, value):
        wg[which, at, cut] = value

    for made in seconds:
        made.wait_recv()
    links.settle_all()

    def backward(s):
        backward_in(s, me.c, s == 0)
        backward_in(s, 1 - me.c, False)
        inward[s].away(functools.partial(backward_out, s))
        inward[s].home(functools.partial(backward_out, s))

    def first_back(s):
        inward[s].wait()
        norm_first_back(s, inward[s])
        gathers[s].start()

    def near_features(s):
        features(s, me.h)
        gathers[s].by_core.wait_recv()
        features(s, me.hc)

    def far_features(s):
        gathers[s].forward()
        features(s, me.hx)
        gathers[s].by_far.wait_recv()
        features(s, me.hd)
        spreads[s].start()

    ones = jnp.ones((8, 128), F32)

    def lane_total(k, i):
        return lax.dot_general(
            ones, lanes[k, i], (((1,), (1,)), ((), ())), precision=lax.Precision.HIGHEST, preferred_element_type=F32
        )

    row = lax.broadcasted_iota(jnp.int32, (8, rows), 0)
    light = []

    def start_small_sums():
        for i in range(parts):
            packed = jnp.zeros((8, rows), F32)
            for k in range(5):
                packed = jnp.where(row == k, lane_total(k, i), packed)
            lsend[i] = packed
        for unit in range(2):
            packed = jnp.zeros((8, rows), F32)
            for i in range(parts):
                packed = jnp.where(row == i, lane_total(5 + unit, i), packed)
            lbias[unit] = packed
        for to, device in ((me.hc, me.core), (me.hx, me.side), (me.hd, me.cross)):
            light.append(links.copy(lsend.at[to], lrecv.at[me.h], device))
        light.append(links.copy(lbias.at[far], lbias.at[2], me.side))

    sign = jnp.where((me.h == 0) | (me.h == 3), -1.0, 1.0).astype(F32)
    mine = jnp.where(is_cos, 1.0, sign)
    theirs = jnp.where(is_cos, sign, 1.0)
    stored = []

    def sequence(s):
        spreads[s].arrive()
        spreads[s].finish()
        links.settle([outward[s].by_core])

        def one(t):
            at = columns(t, tokens)
            total = None
            for q in range(SPLIT):
                share = dot(ug[s, q], tab[q * piece : (q + 1) * piece, at])
                total = share if total is None else total + share
            acc[s, t] = total
            sc[s, 0, t] = total.astype(LOW)

        loop(parts, one)
        swaps[s] = links.copy(sc.at[s, 0], rc.at[s, 0], me.core)

    swaps, across = {}, {}

    def ordered(s):
        swaps[s].wait_recv()

        def one(t):
            pair = (mine * acc[s, t] + theirs * rc[s, 0, t].astype(F32)).astype(LOW)
            sx[s, t] = dot(order[...], pair).astype(LOW)

        loop(parts, one)
        made = links.describe(sx.at[s], rx.at[s], me.side)
        across[s] = made

        @pl.when(jnp.logical_not(is_cos))
        def _():
            made.start()

    def store_grad(s):
        def store(part):
            def one(t):
                u1[s, t] = part[s, t].astype(F32) + xg[s, t, me.h, 0].astype(F32)

            loop(parts, one)

        @pl.when(is_cos)
        def _():
            store(sx)

        @pl.when(jnp.logical_not(is_cos))
        def _():
            across[s].wait()
            store(rx)

        for t in range(parts):
            stored.append(links.fetch(u1.at[s, t], grad_hbm.at[s, :, pl.ds(t * tokens, tokens)]))

    def start_outs(s):
        og[s, me.h] = cs[s, me.h]
        outs[s] = [
            links.copy(cs.at[s, to], og.at[s, me.h], device)
            for to, device in ((me.hc, me.core), (me.hx, me.side), (me.hd, me.cross))
        ]

    def end_outs(s):
        for made in outs[s]:
            made.wait_recv()
        for t in range(parts):
            gr2[s, t] = og[s, t].astype(F32) * live[s]
            stored.append(links.fetch(gr2.at[s, t], out_hbm.at[s, :, pl.ds(t * tokens, tokens)]))

    def small_sums():
        for made in light:
            made.wait_recv()
        ltot[0, 0:8] = lsend[me.h] + lrecv[me.hc] + lrecv[me.hx] + lrecv[me.hd]
        ltot[0, 8:16] = lbias[me.x] + lbias[2]
        small_round()

    rounds = []

    def small_round():
        k = len(rounds)
        if k:
            rounds[k - 1].wait_recv()
            ltot[k] = ltot[k - 1] + lnext[k - 1]
        if k < bits:
            rounds.append(links.copy(ltot.at[k], lnext.at[k], me.flip[k]))

    def store_chunk(n):
        which, at = chunks[n]
        dst = (wg2_hbm, wg1_hbm)[which].at[at]
        for m in range(heavy[n].blocks):
            stored.append(links.fetch(heavy[n].whole.at[m], dst.at[:, pl.ds(m * tokens, tokens)]))

    def step(n):
        if not heavy[n].step():
            store_chunk(n)
            return False
        return True

    acts = {
        "back": backward,
        "norm": first_back,
        "near": near_features,
        "far": far_features,
        "halves": lambda s: spreads[s].forward(),
        "sequence": sequence,
        "order": ordered,
        "grad": store_grad,
        "give": lambda which: weight_grad(which, far, store_given),
        "keep": lambda which: weight_grad(which, me.x, store_kept),
        "pack": lambda _: start_small_sums(),
        "small": lambda _: small_sums(),
        "round": lambda _: small_round(),
        "outs": start_outs,
        "ends": end_outs,
        "chunk": lambda n: step(n),
    }
    going = [True] * len(heavy)
    gt_in.wait()
    order_in.wait()
    for kind, n in SCHEDULE:
        did = acts[kind](n)
        if kind == "chunk":
            going[n] = did
    while any(going):
        for n in range(len(heavy)):
            going[n] = going[n] and step(n)
        if len(rounds) < bits:
            small_round()
    while len(rounds) < bits:
        small_round()
    k = bits - 1
    if len(rounds) == bits:
        rounds[k].wait_recv()
        ltot[bits] = ltot[k] + lnext[k]
    light_ref[...] = ltot[bits, 0:8]
    for i in range(parts):
        flat[:, i * rows : (i + 1) * rows] = ltot[bits, 8 + i : 9 + i]
    for r in range(units // 128):
        bias_ref[r : r + 1, :] = flat[:, r * 128 : (r + 1) * 128]
    for made in stored:
        made.wait()
    links.settle_all()


def local(
    n_batch,
    layer_input,
    gain_first,
    shift_first,
    weight_in,
    bias_in,
    weight_out,
    bias_out,
    gain_second,
    shift_second,
    cotangent,
    live_counts,
):
    slots, rows, piece = layer_input.shape
    width = rows * HOLD
    tokens = piece // HOLD
    units = weight_in.shape[1]
    length = piece * SPLIT
    pad = rows + 16
    bits = n_batch.bit_length() - 1
    vectors = (gain_first, shift_first, bias_out, gain_second, shift_second, bias_in)
    small = sequence_tables(length, SPLIT)
    forward, backward, order = feature_tables(width, HOLD)
    any_, vmem = pl.BlockSpec(memory_space=pl.ANY), pl.BlockSpec(memory_space=pltpu.VMEM)
    block = (HOLD, rows, tokens)
    padded = (HOLD, pad, tokens)
    shard = (slots,) + block
    landing = max(sum(landing_rows(size, bits) for size in sizes) for sizes in chunk_rows(units))
    scratch = [
        ((length, piece), LOW), ((4, FINE, piece), F32), (forward.shape[1:], LOW), (backward.shape[1:], LOW),
        (order.shape[1:], LOW), ((slots, SPLIT, HOLD, 2, rows, tokens), LOW), (shard, LOW), (shard, LOW), (shard, LOW),
        ((2, 2 * rows, tokens), LOW), ((slots, 2) + padded, LOW), ((slots, 2) + padded, LOW), (shard, LOW), (shard, LOW),
        ((slots,) + padded, F32), ((slots, 2, width, tokens), LOW), ((slots, 4, units, tokens), LOW),
        ((slots, 4, units, tokens), LOW), ((slots, 2, width, tokens), LOW), (shard, F32), (shard, F32),
        ((slots, 1, tokens), F32), ((7, HOLD, rows, 128), F32),
        ((2, 2, units, width), LOW), ((2, 2, width, units), LOW), ((2, units, width), F32),
        ((2, units, width), LOW), ((2, landing, width), LOW),
        ((slots, SPLIT, pad, piece), LOW), ((1, units), F32), ((16, 256), F32), ((HOLD, 16, 256), F32), ((HOLD, rows, 128), F32), ((HOLD, 8, rows), F32),
        ((HOLD, 8, rows), F32), ((3, 8, rows), F32), ((bits + 1, 16, rows), F32), ((bits, 16, rows), F32),
    ]
    outs = [
        (layer_input.shape, F32), (layer_input.shape, F32), ((width, units), LOW), ((units, width), LOW),
        ((8, rows), F32), ((units // 128, 128), F32),
    ]
    out, grad, wg1, wg2, light, bias = pl.pallas_call(
        functools.partial(layer_kernel, bits),
        name="layer",
        out_shape=[jax.ShapeDtypeStruct(shape, kind) for shape, kind in outs],
        in_specs=[any_] * 8 + [vmem] * 6 + [pl.BlockSpec(memory_space=pltpu.SMEM)],
        out_specs=[any_] * 4 + [vmem] * 2,
        scratch_shapes=[pltpu.VMEM(shape, kind) for shape, kind in scratch]
        + [pltpu.SemaphoreType.DMA((count,)) for count in semaphores(bits)],
        compiler_params=pltpu.CompilerParams(
            collective_id=1, has_side_effects=True, vmem_limit_bytes=VMEM_LIMIT
        ),
    )(
        layer_input, cotangent, weight_in, weight_out, jnp.asarray(small), jnp.asarray(forward),
        jnp.asarray(backward), jnp.asarray(order), *(v.reshape(1, -1) for v in vectors[:5]), bias_in.reshape(-1, 128), live_counts,
    )
    return (
        out, grad, light[3], light[4], wg1.astype(F32), bias.reshape(units), wg2.astype(F32),
        light[2], light[0], light[1],
    )


def solution(mesh):
    return jax.shard_map(
        functools.partial(local, mesh.shape["batch"]),
        mesh=mesh,
        in_specs=(
            P(None, "hidden", "batch"),
            P("hidden"),
            P("hidden"),
            P(None, "hidden"),
            P("hidden"),
            P("hidden", None),
            P("hidden"),
            P("hidden"),
            P("hidden"),
            P(None, "hidden", "batch"),
            P("batch"),
        ),
        out_specs=(
            P(None, "hidden", "batch"),
            P(None, "hidden", "batch"),
            P("hidden"),
            P("hidden"),
            P(None, "hidden"),
            P("hidden"),
            P("hidden", None),
            P("hidden"),
            P("hidden"),
            P("hidden"),
        ),
        check_vma=False,
    )
```
